32 devices in a mesh: dp: 16 (over z, y, x), mp: 2 (over core).
Axes of the slice: x: 2, y: 2, z: 4, core: 2. Of those that a mesh axis runs over, the one named last changes fastest.
Arguments:
- small_images: bfloat16 [64, 196, 768], P('dp', None, 'mp'), may hold values from -6 to 6
- large_images: bfloat16 [64, 576, 768], P('dp', None, 'mp'), may hold values from -6 to 6
- token_gain: float32 [768], P('mp'), may hold values from 0.5 to 1.5
- token_shift: float32 [768], P('mp'), may hold values from -1.75 to 1.75
- small_expand: bfloat16 [196, 384], replicated, may hold values from -0.4375 to 0.4375
- small_expand_bias: float32 [384], replicated, may hold values from -1.75 to 1.75
- small_project: bfloat16 [384, 196], replicated, may hold values from -0.3125 to 0.3125
- small_project_bias: float32 [196], replicated, may hold values from -1.75 to 1.75
- large_expand: bfloat16 [576, 384], replicated, may hold values from -0.25 to 0.25
- large_expand_bias: float32 [384], replicated, may hold values from -1.75 to 1.75
- large_project: bfloat16 [384, 576], replicated, may hold values from -0.3125 to 0.3125
- large_project_bias: float32 [576], replicated, may hold values from -1.75 to 1.75
- channel_gain: float32 [768], replicated, may hold values from 0.5 to 1.5
- channel_shift: float32 [768], replicated, may hold values from -1.75 to 1.75
- channel_expand: bfloat16 [768, 3072], replicated, may hold values from -0.21875 to 0.21875
- channel_expand_bias: float32 [3072], replicated, may hold values from -1.75 to 1.75
- channel_project: bfloat16 [3072, 768], replicated, may hold values from -0.109375 to 0.109375
- channel_project_bias: float32 [768], replicated, may hold values from -1.75 to 1.75
- small_cotangent: bfloat16 [64, 196, 768], P('dp', 'mp'), may hold values from -6 to 6
- large_cotangent: bfloat16 [64, 576, 768], P('dp', 'mp'), may hold values from -6 to 6
Outputs:
- small_output: bfloat16 [64, 196, 768], P('dp', 'mp')
- large_output: bfloat16 [64, 576, 768], P('dp', 'mp')
- small_input_grad: bfloat16 [64, 196, 768], P('dp', None, 'mp')
- large_input_grad: bfloat16 [64, 576, 768], P('dp', None, 'mp')
- grad_token_gain: float32 [768], replicated
- grad_token_shift: float32 [768], replicated
- grad_small_expand: float32 [196, 384], replicated
- grad_small_expand_bias: float32 [384], replicated
- grad_small_project: float32 [384, 196], replicated
- grad_small_project_bias: float32 [196], replicated
- grad_large_expand: float32 [576, 384], replicated
- grad_large_expand_bias: float32 [384], replicated
- grad_large_project: float32 [384, 576], replicated
- grad_large_project_bias: float32 [576], replicated
- grad_channel_gain: float32 [768], replicated
- grad_channel_shift: float32 [768], replicated
- grad_channel_expand: float32 [768, 3072], P(('dp', 'mp'))
- grad_channel_expand_bias: float32 [3072], replicated
- grad_channel_project: float32 [3072, 768], P(('dp', 'mp'))
- grad_channel_project_bias: float32 [768], replicated
The draws below stay inside these ranges and needn't reach their ends.
All inputs are finite; a program needn't handle non-finite values.
Results may differ from the reference program's by a relative error of at most 0.008.
Values may be sent and summed in bfloat16 or wider, within the bound.
No kernel may reach another device: no remote copies, remote signals or barrier semaphores. Data moves between devices by JAX's collectives and lax.ppermute only.
A program may use at most 256 MiB of HBM per device.

```python
import jax
import jax.numpy as jnp
from jax import lax

D = 768
DS = 384
DC = 3072
SA = 196
SB = 576
A_DEV = 4
B_DEV = 4
NA = 64
NB = 64


def spiked(drawn, key, source, target, blocks, factor):
    def block_of(position):
        return (jnp.arange(drawn.shape[position]) // (drawn.shape[position] // blocks)).reshape((-1,) + (1,) * (drawn.ndim - 1 - position))

    first = jax.random.permutation(key, blocks)[block_of(target)]
    far = (block_of(target) + blocks // 2) % blocks
    return jnp.where((block_of(source) == first) | (block_of(source) == far), factor * drawn, drawn)


def block_levels(own_key, extent, split, least, top_value):
    level, own = 1.0, jax.random.fold_in(own_key, 6)
    for dim, parts in split:
        draws = jnp.exp(jax.random.uniform(jax.random.fold_in(own, dim), (parts,), jnp.float32, least / len(split), top_value / len(split)))
        level = level * jnp.repeat(draws, extent[dim] // parts).reshape([-1 if axis == dim else 1 for axis in range(len(extent))])
    return level


def centred(own_key, dims, scale, limit, shards=(), kind=jnp.bfloat16):
    level = block_levels(own_key, dims, shards, -0.22, 0.18) if shards else 1.0
    drawn = jax.random.normal(own_key, dims, jnp.float32) * scale * level
    return jnp.minimum(jnp.maximum(drawn, -limit), limit).astype(kind)


def gaussian_with(own_key, dims, width, limit, shards, heavy, kind=jnp.bfloat16):
    drawn = width * jax.random.normal(own_key, dims, jnp.float32)
    if shards:
        drawn = drawn * block_levels(own_key, dims, shards, -0.22, 0.18)
    return jnp.clip(spiked(drawn, jax.random.fold_in(own_key, 3), *heavy), -limit, limit).astype(kind)


def setup_inputs(seed: int = 0) -> dict:
    keys = jax.random.split(jax.random.key(seed), 21)
    return {
        "small_images": centred(keys[0], (NA, SA, D), 1.0, 6.0, ((0, 16), (2, 2))),
        "large_images": centred(keys[1], (NB, SB, D), 1.0, 6.0, ((0, 16), (2, 2))),
        "token_gain": jnp.clip(1.0 + 0.1 * jax.random.normal(keys[2], (D,), jnp.float32), 0.5, 1.5),
        "token_shift": centred(keys[3], (D,), 0.3, 1.75, ((0, 2),), jnp.float32),
        "small_expand": centred(keys[4], (SA, DS), SA ** -0.5, 0.4375),
        "small_expand_bias": centred(keys[5], (DS,), 0.3, 1.75, (), jnp.float32),
        "small_project": centred(keys[6], (DS, SA), DS ** -0.5, 0.3125),
        "small_project_bias": centred(keys[7], (SA,), 0.3, 1.75, (), jnp.float32),
        "large_expand": centred(keys[8], (SB, DS), SB ** -0.5, 0.25),
        "large_expand_bias": centred(keys[9], (DS,), 0.3, 1.75, (), jnp.float32),
        "large_project": centred(keys[10], (DS, SB), DS ** -0.5, 0.3125),
        "large_project_bias": centred(keys[11], (SB,), 0.3, 1.75, (), jnp.float32),
        "channel_gain": jnp.clip(1.0 + 0.1 * jax.random.normal(keys[12], (D,), jnp.float32), 0.5, 1.5),
        "channel_shift": centred(keys[13], (D,), 0.3, 1.75, (), jnp.float32),
        "channel_expand": centred(keys[14], (D, DC), D ** -0.5, 0.21875),
        "channel_expand_bias": centred(keys[15], (DC,), 0.3, 1.75, (), jnp.float32),
        "channel_project": centred(keys[16], (DC, D), DC ** -0.5, 0.109375),
        "channel_project_bias": centred(keys[17], (D,), 0.3, 1.75, (), jnp.float32),
        "small_cotangent": gaussian_with(keys[18], (NA, SA, D), 1.0, 6.0, ((0, 16), (1, 2)), (0, 2, 16, 2.0)),
        "large_cotangent": centred(keys[19], (NB, SB, D), 1.0, 6.0, ((0, 16), (1, 2))),
    }


@jax.custom_vjp
def low(v):
    return lax.optimization_barrier(v.astype(jnp.bfloat16)).astype(jnp.float32)

@jax.custom_vjp
def low_back(v):
    return v

def low_keep(v):
    return (low(v), None)

def low_pass(kept, grad):
    return (grad,)

def back_keep(v):
    return (v, None)

def back_low(kept, grad):
    return (low(grad),)
low.defvjp(low_keep, low_pass)
low_back.defvjp(back_keep, back_low)
HIGH = lax.Precision.HIGHEST
EPS = 1e-06

def gelu_exact(values):
    return jax.nn.gelu(values, approximate=False)

def layer_norm(values, gain, shift):
    mean = lax.optimization_barrier(jnp.mean(values, -1, keepdims=True))
    spread = lax.optimization_barrier(jnp.mean(values * values, -1, keepdims=True)) - mean * mean
    return (values - mean) * lax.rsqrt(spread + EPS) * gain + shift

def block_forward(shared, token, images):
    norm_gain, norm_shift, chan_gain, chan_shift, chan_expand, chan_expand_bias, chan_project, chan_project_bias = shared
    expand, expand_bias, project, project_bias = token
    normed = low(layer_norm(images, norm_gain, norm_shift))
    before = low_back(jnp.einsum('nsc,sk->nkc', normed, expand, precision=HIGH) + expand_bias[None, :, None])
    active = low(gelu_exact(before))
    mixed = jnp.einsum('nkc,ks->nsc', active, project, precision=HIGH) + project_bias[None, :, None]
    middle = low_back(low(images + mixed))
    normed_two = low(layer_norm(middle, chan_gain, chan_shift))
    hidden = low_back(jnp.einsum('nsd,df->nsf', normed_two, chan_expand, precision=HIGH) + chan_expand_bias)
    active_two = low(gelu_exact(hidden))
    return middle + jnp.einsum('nsf,fd->nsd', active_two, chan_project, precision=HIGH) + chan_project_bias

def run_group(shared, token, images, cotangent, block):
    count = images.shape[0] // block
    blocks = images.reshape(count, block, images.shape[1], images.shape[2]).astype(jnp.float32)
    cot_blocks = cotangent.reshape(count, block, images.shape[1], images.shape[2]).astype(jnp.float32)
    start = (jax.tree.map(jnp.zeros_like, shared), jax.tree.map(jnp.zeros_like, token))

    def step(carry, pair):
        image_block, cot_block = pair
        result, pullback = jax.vjp(block_forward, shared, token, image_block)
        grad_shared, grad_token, grad_images = pullback(cot_block)
        carry = (jax.tree.map(jnp.add, carry[0], grad_shared), jax.tree.map(jnp.add, carry[1], grad_token))
        return (carry, (result.astype(jnp.bfloat16), grad_images.astype(jnp.bfloat16)))
    totals, (results, grads) = lax.scan(step, start, (blocks, cot_blocks))
    return (results.reshape(images.shape), grads.reshape(images.shape), totals[0], totals[1])

def reference(small_images, large_images, token_gain, token_shift, small_expand, small_expand_bias, small_project, small_project_bias, large_expand, large_expand_bias, large_project, large_project_bias, channel_gain, channel_shift, channel_expand, channel_expand_bias, channel_project, channel_project_bias, small_cotangent, large_cotangent):
    shared = tuple((value.astype(jnp.float32) for value in (token_gain, token_shift, channel_gain, channel_shift, channel_expand, channel_expand_bias, channel_project, channel_project_bias)))
    small_token = tuple((value.astype(jnp.float32) for value in (small_expand, small_expand_bias, small_project, small_project_bias)))
    large_token = tuple((value.astype(jnp.float32) for value in (large_expand, large_expand_bias, large_project, large_project_bias)))
    small_out, small_grad, small_shared, small_tok = run_group(shared, small_token, small_images, small_cotangent, A_DEV)
    large_out, large_grad, large_shared, large_tok = run_group(shared, large_token, large_images, large_cotangent, B_DEV)
    totals = jax.tree.map(jnp.add, small_shared, large_shared)
    return (small_out, large_out, small_grad, large_grad, totals[0], totals[1], small_tok[0], small_tok[1], small_tok[2], small_tok[3], large_tok[0], large_tok[1], large_tok[2], large_tok[3], totals[2], totals[3], totals[4], totals[5], totals[6], totals[7])
```

```python
import functools

import jax
import jax.numpy as jnp
from jax import lax
from jax.experimental import pallas as pl
from jax.experimental.pallas import tpu as pltpu
from jax.sharding import PartitionSpec as P

BF = jnp.bfloat16
F32 = jnp.float32
EPS = 1e-06
SQRT_HALF = 0.7071067811865476
INV_SQRT_2PI = 0.3989422804014327
HALF_LOG2E = 0.7213475204444817
NN = ((1,), (0,))
NT = ((1,), (1,))
TN = ((0,), (0,))
MB = 1 << 20
PLANES = 4
ORDER = (0, 3, 1, 2)
VEC = 16


def dot(left, right, dims):
    return lax.dot_general(left, right, (dims, ((), ())), preferred_element_type=F32)


def gelu_pair(values):
    cdf = 0.5 * lax.erf(values * SQRT_HALF) + 0.5
    pdf = jnp.exp2((values * values) * (-HALF_LOG2E)) * INV_SQRT_2PI
    return values * cdf, cdf + values * pdf


def norm(values):
    width = values.shape[-1]
    mean = jnp.sum(values, -1, keepdims=True) * (1.0 / width)
    square = jnp.sum(values * values, -1, keepdims=True) * (1.0 / width)
    scale = lax.rsqrt(square - mean * mean + EPS)
    return (values - mean) * scale, scale


def round_up(value, to):
    return (value + to - 1) // to * to


def params(limit, **extra):
    return pltpu.CompilerParams(vmem_limit_bytes=limit * MB, **extra)


def whole(shape):
    return pl.BlockSpec(shape, lambda *_: (0,) * len(shape))


def load_images(sc, own, other, dest):
    rows, part = own.shape[1], own.shape[2]
    mine = pl.multiple_of(sc[0] * part, 128)
    theirs = pl.multiple_of((1 - sc[0]) * part, 128)
    if dest.shape[0] != rows:
        dest[...] = jnp.zeros_like(dest)
    dest[0:rows, pl.ds(mine, part)] = own[0].astype(F32)
    dest[0:rows, pl.ds(theirs, part)] = other[0].astype(F32)


def load_token_params(sc, own, other, dest):
    part = own.shape[1]
    dest[:, pl.ds(pl.multiple_of(sc[0] * part, 128), part)] = own[...]
    dest[:, pl.ds(pl.multiple_of((1 - sc[0]) * part, 128), part)] = other[...]


def front_kernel(
    sc, xs, xs_in, xl, xl_in, ys, ys_in, yl, yl_in, tok, tok_in,
    es, bes, pjs, bps, el, bel, pjl, bpl, gain2, shift2,
    x1s, n2s, as_, ds_, yrs, x1l, n2l, al, dl, yrl, gy,
    x_s, x_l, tk, y_s,
):
    load_images(sc, xs, xs_in, x_s)
    load_images(sc, xl, xl_in, x_l)
    load_token_params(sc, tok, tok_in, tk)
    first = sc[0] == 0
    half = ys.shape[1]
    mine, theirs = ys[0].astype(F32), ys_in[0].astype(F32)
    y_s[...] = jnp.zeros_like(y_s)
    y_s[0:half, :] = jnp.where(first, mine, theirs)
    y_s[half : 2 * half, :] = jnp.where(first, theirs, mine)
    yrs[0] = y_s[...].astype(BF)
    half = yl.shape[1]
    yrl[0, pl.ds(pl.multiple_of(sc[0] * half, 16), half), :] = yl[0]
    yrl[0, pl.ds(pl.multiple_of((1 - sc[0]) * half, 16), half), :] = yl_in[0]
    sums = jnp.sum(mine, 0, keepdims=True) + jnp.sum(theirs, 0, keepdims=True)
    sums = sums + jnp.sum(yl[0].astype(F32), 0, keepdims=True)
    sums = sums + jnp.sum(yl_in[0].astype(F32), 0, keepdims=True)

    @pl.when(pl.program_id(0) == 0)
    def _():
        gy[...] = sums

    @pl.when(pl.program_id(0) != 0)
    def _():
        gy[...] += sums

    gain, shift = tk[0:1, :], tk[1:2, :]

    def group(x_ref, e, be, pj, bp, x1, n2, a_ref, d_ref):
        x = x_ref[...]
        hat, _ = norm(x)
        normed = (hat * gain + shift).astype(BF)
        active, slope = gelu_pair(dot(e[...], normed, TN) + be[...])
        active = active.astype(BF)
        a_ref[0] = active
        d_ref[0] = slope
        middle = (x_ref[...] + (dot(pj[...], active, TN) + bp[...])).astype(BF)
        x1[0] = middle
        hat2, _ = norm(middle.astype(F32))
        n2[0] = (hat2 * gain2[...] + shift2[...]).astype(BF)

    group(x_s, es, bes, pjs, bps, x1s, n2s, as_, ds_)
    group(x_l, el, bel, pjl, bpl, x1l, n2l, al, dl)


def own_image(rows, width, count):
    return pl.BlockSpec((1, rows, width), lambda i, sc: (sc[0] * count + i, 0, 0))


def per_image(rows, width):
    return pl.BlockSpec((1, rows, width), lambda i, sc: (i, 0, 0))


def front(sc, xs, xs_in, xl, xl_in, ys, ys_in, yl, yl_in, tok, tok_in, token_s, token_l, gain2, shift2):
    count, small, part = xs_in.shape
    large = xl_in.shape[1]
    width = 2 * part
    hidden = token_s[0].shape[1]
    pad_s = token_s[0].shape[0]
    pad_l = token_l[0].shape[0]
    hs, hl = ys.shape[1], yl.shape[1]
    outs = []
    for rows in (pad_s, pad_l):
        outs += [
            ((count, rows, width), BF),
            ((count, rows, width), BF),
            ((count, hidden, width), BF),
            ((count, hidden, width), F32),
            ((count, rows, width), BF),
        ]
    return pl.pallas_call(
        front_kernel,
        grid_spec=pltpu.PrefetchScalarGridSpec(
            num_scalar_prefetch=1,
            grid=(count,),
            in_specs=[
                own_image(small, part, count), per_image(small, part),
                own_image(large, part, count), per_image(large, part),
                own_image(hs, width, count), per_image(hs, width),
                own_image(hl, width, count), per_image(hl, width),
                whole(tok.shape), whole(tok.shape),
            ]
            + [whole(w.shape) for w in token_s + token_l]
            + [whole((1, width))] * 2,
            out_specs=[per_image(*shape[1:]) for shape, _ in outs] + [whole((1, width))],
            scratch_shapes=[
                pltpu.VMEM((pad_s, width), F32),
                pltpu.VMEM((pad_l, width), F32),
                pltpu.VMEM((2, width), F32),
                pltpu.VMEM((pad_s, width), F32),
            ],
        ),
        out_shape=[jax.ShapeDtypeStruct(*o) for o in outs] + [jax.ShapeDtypeStruct((1, width), F32)],
        compiler_params=params(56),
        name="front",
    )(sc, xs, xs_in, xl, xl_in, ys, ys_in, yl, yl_in, tok, tok_in, *token_s, *token_l, gain2, shift2)


def channel_kernel(is_first, is_last, *refs):
    refs = list(refs)
    sc = refs.pop(0)
    n2s, n2l, ys, yl, w1, b1, w2 = [refs.pop(0) for _ in range(7)]
    if not is_first:
        out_in, dn_in = refs.pop(0), refs.pop(0)
    if is_last:
        x1s, x1l, gain2, b2 = [refs.pop(0) for _ in range(4)]
    send, keep, gb1 = [refs.pop(0) for _ in range(3)]
    if is_last:
        out_rows, dx1, g2 = [refs.pop(0) for _ in range(3)]
    else:
        out_acc, dn_acc = refs.pop(0), refs.pop(0)
    n2, y, acts, grads, out, dn, sems = refs
    rows, width = n2.shape
    small = n2s.shape[0]
    hidden = w1.shape[1]
    if not is_first:
        loads = [
            pltpu.make_async_copy(out_in, out, sems.at[0]),
            pltpu.make_async_copy(dn_in, dn, sems.at[1]),
        ]
        for copy in loads:
            copy.start()
    n2[0:small, :] = n2s[...]
    n2[small:rows, :] = n2l[...]
    y[0:small, :] = ys[...]
    y[small:rows, :] = yl[...]
    tile = rows // 2
    bias_grad = jnp.zeros((1, hidden), F32)
    for step in range(2):
        at = pl.ds(step * tile, tile)
        active, slope = gelu_pair(dot(n2[at, :], w1[...], NN) + b1[...])
        grad = dot(y[at, :], w2[...], NT) * slope
        bias_grad = bias_grad + jnp.sum(grad, 0, keepdims=True)
        acts[at, :] = active.astype(BF)
        grads[at, :] = grad.astype(BF)
    gb1[...] = bias_grad
    if not is_first:
        for copy in loads:
            copy.wait()
    for step in range(2):
        at = pl.ds(step * tile, tile)
        mixed = dot(acts[at, :], w2[...], NN)
        back = dot(grads[at, :], w1[...], NT)
        if is_first:
            out[at, :] = mixed
            dn[at, :] = back
        else:
            out[at, :] += mixed
            dn[at, :] += back
    if is_last:
        gain_sum = jnp.zeros((1, width), F32)
        shift_sum = jnp.zeros((1, width), F32)
        for low, high, ref in ((0, small, x1s), (small, rows, x1l)):
            middle = ref[...].astype(F32)
            out_rows[low:high, :] = (middle + out[low:high, :] + b2[...]).astype(BF)
            hat, scale = norm(middle)
            back = dn[low:high, :]
            gain_sum = gain_sum + jnp.sum(back * hat, 0, keepdims=True)
            shift_sum = shift_sum + jnp.sum(back, 0, keepdims=True)
            scaled = back * gain2[...]
            mean = jnp.sum(scaled, -1, keepdims=True) * (1.0 / width)
            along = jnp.sum(scaled * hat, -1, keepdims=True) * (1.0 / width)
            dx1[low:high, :] = (
                y[low:high, :].astype(F32) + scale * (scaled - mean - hat * along)
            ).astype(BF)
        g2[0:1, :] = gain_sum
        g2[1:2, :] = shift_sum
    else:
        stores = [
            pltpu.make_async_copy(out, out_acc, sems.at[0]),
            pltpu.make_async_copy(dn, dn_acc, sems.at[1]),
        ]
        for copy in stores:
            copy.start()
    first = sc[0] == 0
    quarter = width // 32
    expand = dot(n2[...], grads[...], TN).reshape(PLANES, 4, 2, quarter, hidden)
    for c in range(4):
        low = expand[:, c, 0].reshape(PLANES * quarter, hidden)
        high = expand[:, c, 1].reshape(PLANES * quarter, hidden)
        keep[c, 0 : PLANES * quarter, :] = jnp.where(first, low, high).astype(BF)
        send[c, 0 : PLANES * quarter, :] = jnp.where(first, high, low).astype(BF)
    project = dot(acts[...], y[...], TN).reshape(4, 2, hidden // 8, width)
    for c in range(4):
        low, high = project[c, 0], project[c, 1]
        keep[c, PLANES * quarter :, :] = jnp.where(first, low, high).astype(BF)
        send[c, PLANES * quarter :, :] = jnp.where(first, high, low).astype(BF)
    if not is_last:
        for copy in stores:
            copy.wait()


def channel(sc, plane, is_first, is_last, rows_in, w1, b1, w2, carried, ending):
    n2s, n2l, ys, yl = rows_in
    small, width = n2s.shape
    rows = small + n2l.shape[0]
    hidden = w1.shape[1] // PLANES
    any_spec = pl.BlockSpec(memory_space=pl.ANY)
    in_specs = [whole(a.shape) for a in rows_in] + [
        pl.BlockSpec((width, hidden), lambda i, sc: (0, plane)),
        pl.BlockSpec((1, hidden), lambda i, sc: (0, plane)),
        pl.BlockSpec((hidden, width), lambda i, sc: (plane, 0)),
    ]
    in_specs += [any_spec for _ in carried] + [whole(a.shape) for a in ending]
    block = (4, width // 8 + hidden // 8, width)
    outs = [(block, BF), (block, BF), ((1, hidden), F32)]
    out_specs = [whole(s) for s, _ in outs]
    if is_last:
        extra = [((rows, width), BF), ((rows, width), BF), ((2, width), F32)]
        out_specs += [whole(s) for s, _ in extra]
    else:
        extra = [((rows, width), F32)] * 2
        out_specs += [any_spec] * 2
    flops = 6 * 2 * rows * width * hidden
    return pl.pallas_call(
        functools.partial(channel_kernel, is_first, is_last),
        grid_spec=pltpu.PrefetchScalarGridSpec(
            num_scalar_prefetch=1,
            grid=(1,),
            in_specs=in_specs,
            out_specs=out_specs,
            scratch_shapes=[
                pltpu.VMEM((rows, width), BF),
                pltpu.VMEM((rows, width), BF),
                pltpu.VMEM((rows, hidden), BF),
                pltpu.VMEM((rows, hidden), BF),
                pltpu.VMEM((rows, width), F32),
                pltpu.VMEM((rows, width), F32),
                pltpu.SemaphoreType.DMA((2,)),
            ],
        ),
        out_shape=[jax.ShapeDtypeStruct(*o) for o in outs + extra],
        compiler_params=params(60),
        cost_estimate=pl.CostEstimate(flops=flops, bytes_accessed=20 * MB, transcendentals=2 * rows * hidden),
        name="channel",
    )(sc, *rows_in, w1, b1, w2, *carried, *ending)


def back_kernel(
    sc, dxs, dxl, xs, xs_in, xl, xl_in, tok, tok_in,
    as_, ds_, al, dl, es, pjs, el, pjl, g2, gy, b1a, b1b, b1c, b1d,
    gis_keep, gis_send, gil_keep, gil_send, w_keep, w_send, vec,
    x_s, x_l, tk, gps, ges, gpl, gel, gi_s, gi_l,
):
    step = pl.program_id(0)
    load_images(sc, xs, xs_in, x_s)
    load_images(sc, xl, xl_in, x_l)
    load_token_params(sc, tok, tok_in, tk)
    gain, shift = tk[0:1, :], tk[1:2, :]

    @pl.when(step == 0)
    def _():
        vec[...] = jnp.zeros_like(vec)
        for ref in (gps, ges, gpl, gel):
            ref[...] = jnp.zeros_like(ref)

    def group(x_ref, dx, a, d, e, pj, gp, ge, be_at, bp_row, gi, keep, send):
        rows, width = x_ref.shape
        hidden = a.shape[1]
        dx = dx[0]
        hat, scale = norm(x_ref[...])
        normed = (hat * gain + shift).astype(BF)
        gp[0:rows, :] += dot(dx, a[0], NT)
        before = (dot(pj[...], dx, NN) * d[0]).astype(BF)
        ge[0:rows, :] += dot(normed, before, NT)
        ones = jnp.ones((8, width), BF)
        vec[bp_row : bp_row + 1, 0:rows] += dot(ones, dx, NT)[0:1, :]
        vec[9:10, be_at : be_at + hidden] += dot(ones, before, NT)[0:1, :]
        grad = dot(e[...], before, NN)
        vec[0:1, :] += jnp.sum(grad * hat, 0, keepdims=True)
        vec[1:2, :] += jnp.sum(grad, 0, keepdims=True)
        scaled = grad * gain
        mean = jnp.sum(scaled, -1, keepdims=True) * (1.0 / width)
        along = jnp.sum(scaled * hat, -1, keepdims=True) * (1.0 / width)
        gi[...] = dx.astype(F32) + scale * (scaled - mean - hat * along)
        part = width // 2
        count = keep.shape[1]
        keep[0] = gi[0:count, pl.ds(pl.multiple_of(sc[0] * part, 128), part)].astype(BF)
        send[0] = gi[0:count, pl.ds(pl.multiple_of((1 - sc[0]) * part, 128), part)].astype(BF)

    hidden = as_.shape[1]
    group(x_s, dxs, as_, ds_, es, pjs, gps, ges, 0, 10, gi_s, gis_keep, gis_send)
    group(x_l, dxl, al, dl, el, pjl, gpl, gel, hidden, 11, gi_l, gil_keep, gil_send)

    @pl.when(step == pl.num_programs(0) - 1)
    def _():
        vec[2:4, :] = g2[...]
        vec[4:5, :] = gy[...]
        for i, ref in enumerate((b1a, b1b, b1c, b1d)):
            vec[5 + i : 6 + i, :] = ref[...]
        size = w_keep.shape[2]
        half_s, half_l = gps.shape[0] // 2, gpl.shape[0] // 2
        for side, ref in ((sc[0], w_keep), (1 - sc[0], w_send)):
            for t, (small, large) in enumerate(((gps, gpl), (ges, gel))):
                at = pl.multiple_of(side * half_s, 8)
                ref[0, t] = small[pl.ds(at, size), :].astype(BF)
                for c in range(1, 4):
                    have = min(size, half_l - (c - 1) * size)
                    at = pl.multiple_of(side * half_l + (c - 1) * size, 8)
                    ref[c, t, 0:have, :] = large[pl.ds(at, have), :].astype(BF)
                    if have < size:
                        ref[c, t, have:, :] = jnp.zeros((size - have, hidden), BF)


def back(sc, dxs, dxl, xs, xs_in, xl, xl_in, tok, tok_in, saved, weights, vectors):
    count, small, part = xs_in.shape
    large = xl_in.shape[1]
    width = 2 * part
    pad_s, pad_l = dxs.shape[1], dxl.shape[1]
    hidden = saved[0].shape[1]
    size = piece_rows(pad_s, pad_l)
    outs = [
        ((count, small, part), BF),
        ((count, small, part), BF),
        ((count, large, part), BF),
        ((count, large, part), BF),
        ((4, 2, size, hidden), BF),
        ((4, 2, size, hidden), BF),
        ((VEC, width), F32),
    ]
    return pl.pallas_call(
        back_kernel,
        grid_spec=pltpu.PrefetchScalarGridSpec(
            num_scalar_prefetch=1,
            grid=(count,),
            in_specs=[
                per_image(pad_s, width), per_image(pad_l, width),
                own_image(small, part, count), per_image(small, part),
                own_image(large, part, count), per_image(large, part),
                whole(tok.shape), whole(tok.shape),
            ]
            + [per_image(hidden, width)] * 4
            + [whole(a.shape) for a in weights]
            + [whole(a.shape) for a in vectors],
            out_specs=[per_image(*s[1:]) for s, _ in outs[:4]] + [whole(s) for s, _ in outs[4:]],
            scratch_shapes=[
                pltpu.VMEM((pad_s, width), F32),
                pltpu.VMEM((pad_l, width), F32),
                pltpu.VMEM((2, width), F32),
                pltpu.VMEM((2 * size, hidden), F32),
                pltpu.VMEM((2 * size, hidden), F32),
                pltpu.VMEM((pad_l, hidden), F32),
                pltpu.VMEM((pad_l, hidden), F32),
                pltpu.VMEM((pad_s, width), F32),
                pltpu.VMEM((pad_l, width), F32),
            ],
        ),
        out_shape=[jax.ShapeDtypeStruct(*o) for o in outs],
        compiler_params=params(56),
        name="back",
    )(sc, dxs, dxl, xs, xs_in, xl, xl_in, tok, tok_in, *saved, *weights, *vectors)


def piece_rows(pad_s, pad_l):
    return max(round_up(pad_s // 2, 16), round_up(-(-(pad_l // 2) // 3), 16))


def total4(parts):
    a, b, c, d = [p.astype(F32) for p in parts]
    return (a + b) + (c + d)


def pair_kernel(count, sc, *refs):
    keeps, recvs, outs = refs[:4], refs[4:8], refs[8:12]
    for a, b, o in zip(keeps, recvs, outs):
        o[...] = (a[0].astype(F32) + b[0].astype(F32)).astype(BF)
    for k in range(count):
        refs[12 + k][...] = refs[12 + count + k][...]


def pair_sum(sc, keep, recv):
    block = keep.shape[1:]
    zeros = (0,) * len(block)
    specs = [
        pl.BlockSpec((1,) + block, lambda i, sc, k=k: (sc[1] ^ k,) + zeros) for k in range(4)
    ]
    return pl.pallas_call(
        functools.partial(pair_kernel, 0),
        grid_spec=pltpu.PrefetchScalarGridSpec(
            num_scalar_prefetch=1,
            grid=(1,),
            in_specs=specs * 2,
            out_specs=[whole(block)] * 4,
        ),
        out_shape=[jax.ShapeDtypeStruct(block, BF)] * 4,
        compiler_params=params(32),
        name="pair_sum",
    )(sc, *([keep] * 4), *([recv] * 4))


def quad_kernel(sc, own, r1, r2, r3, d0, d1, d2, d3, rest, hold):
    rows = own.shape[0] // 2
    hold[...] = total4([r[0:rows, :] for r in (own, r1, r2, r3)]).reshape(hold.shape)
    rest[...] = total4([r[rows:, :] for r in (own, r1, r2, r3)]).astype(BF)
    for k, ref in enumerate((d0, d1, d2, d3)):
        ref[...] = hold[sc[2] ^ k].astype(BF)


def quad_sum(sc, own, received):
    rows, width = own.shape
    piece = (rows // 2 // PLANES, width)
    return pl.pallas_call(
        quad_kernel,
        grid_spec=pltpu.PrefetchScalarGridSpec(
            num_scalar_prefetch=1,
            grid=(1,),
            in_specs=[whole(own.shape)] * 4,
            out_specs=[whole(piece)] * 4 + [whole((rows // 2, width))],
            scratch_shapes=[pltpu.VMEM((PLANES,) + piece, F32)],
        ),
        out_shape=[jax.ShapeDtypeStruct(piece, BF)] * 4 + [jax.ShapeDtypeStruct((rows // 2, width), BF)],
        compiler_params=params(32),
        name="quad_sum",
    )(sc, own, *received)


def last_kernel(sc, *refs):
    expand_out, project_out = refs[-2:]
    width = refs[0].shape[1]
    for plane in range(PLANES):
        expand_out[:, plane * width : (plane + 1) * width] = total4(
            [r[...] for r in refs[4 * plane : 4 * plane + 4]]
        )
        parts = refs[16 + 4 * plane : 20 + 4 * plane]

        @pl.when(sc[2] == plane)
        def _():
            project_out[...] = total4([r[...] for r in parts])


def last_sum(sc, expands, projects):
    flat = [a for plane in range(PLANES) for a in expands[plane]]
    flat += [a for plane in range(PLANES) for a in projects[plane]]
    rows, width = flat[0].shape
    outs = [(rows, PLANES * width), flat[-1].shape]
    return pl.pallas_call(
        last_kernel,
        grid_spec=pltpu.PrefetchScalarGridSpec(
            num_scalar_prefetch=1,
            grid=(1,),
            in_specs=[whole(a.shape) for a in flat],
            out_specs=[whole(s) for s in outs],
        ),
        out_shape=[jax.ShapeDtypeStruct(s, F32) for s in outs],
        compiler_params=params(32),
        name="last_sum",
    )(sc, *flat)


def token_sum_kernel(*refs):
    w, v = refs[-2:]
    w[...] = total4([r[...] for r in refs[0:4]]).astype(BF)
    v[...] = total4([r[...] for r in refs[4:8]])


def token_sum(ws, vs):
    return pl.pallas_call(
        token_sum_kernel,
        out_shape=[jax.ShapeDtypeStruct(ws[0].shape, BF), jax.ShapeDtypeStruct(vs[0].shape, F32)],
        compiler_params=params(32),
        name="token_sum",
    )(*ws, *vs)


def unpack_kernel(sc, *refs):
    mine, theirs = refs[0:4], refs[4:8]
    vec = refs[8]
    ges, gps, gel, gpl = refs[9:13]
    vectors = refs[13:23]
    hold, flip_s, flip_l = refs[23:]
    for k in range(4):
        hold[sc[0], sc[1] ^ k] = mine[k][...]
        hold[1 - sc[0], sc[1] ^ k] = theirs[k][...]
    size = mine[0].shape[1]
    small, large = ges.shape[0], gel.shape[0]
    for side in range(2):
        low = side * size
        have = min(size, small - low)
        ges[low : low + have, :] = hold[side, 0, 1].astype(F32)[0:have, :]
        flip_s[low : low + size, :] = hold[side, 0, 0].astype(F32)
        for c in range(1, 4):
            low = side * (large // 2) + (c - 1) * size
            have = min(size, large // 2 - (c - 1) * size)
            gel[low : low + have, :] = hold[side, c, 1].astype(F32)[0:have, :]
            flip_l[low : low + have, :] = hold[side, c, 0].astype(F32)[0:have, :]
    gps[...] = flip_s[...].T[:, 0:small]
    gpl[...] = flip_l[...].T[:, 0:large]
    hidden = ges.shape[1]
    picks = [(0, 0), (1, 0), (9, 0), (10, 0), (9, hidden), (11, 0), (2, 0), (3, 0), None, (4, 0)]
    for ref, pick in zip(vectors, picks):
        if pick is None:
            width = vec.shape[1]
            for i in range(ref.shape[1] // width):
                ref[0:1, i * width : (i + 1) * width] = vec[5 + i : 6 + i, :]
        else:
            row, at = pick
            ref[...] = vec[row : row + 1, at : at + ref.shape[1]]


def unpack(sc, mine, theirs, vec, small, large, hidden, channel_hidden):
    width = vec.shape[1]
    size = mine[0].shape[1]
    outs = [(small, hidden), (hidden, small), (large, hidden), (hidden, large)]
    outs += [(1, n) for n in (width, width, hidden, small, hidden, large, width, width, channel_hidden, width)]
    return pl.pallas_call(
        unpack_kernel,
        grid_spec=pltpu.PrefetchScalarGridSpec(
            num_scalar_prefetch=1,
            grid=(1,),
            in_specs=[whole(a.shape) for a in mine + theirs] + [whole(vec.shape)],
            out_specs=[whole(s) for s in outs],
            scratch_shapes=[
                pltpu.VMEM((2, 4) + mine[0].shape, BF),
                pltpu.VMEM((round_up(2 * size, 128), hidden), F32),
                pltpu.VMEM((round_up(large, 128), hidden), F32),
            ],
        ),
        out_shape=[jax.ShapeDtypeStruct(s, F32) for s in outs],
        compiler_params=params(32),
        name="unpack",
    )(sc, *mine, *theirs, vec)


def swap(values):
    return lax.ppermute(values, "mp", [(0, 1), (1, 0)])


def across(values, mask, pairs):
    return lax.ppermute(values, "dp", [(i, i ^ mask) for i in pairs])


def per_device(
    chips,
    small_images,
    large_images,
    token_gain,
    token_shift,
    small_expand,
    small_expand_bias,
    small_project,
    small_project_bias,
    large_expand,
    large_expand_bias,
    large_project,
    large_project_bias,
    channel_gain,
    channel_shift,
    channel_expand,
    channel_expand_bias,
    channel_project,
    channel_project_bias,
    small_cotangent,
    large_cotangent,
):
    core = lax.axis_index("mp")
    chip = lax.axis_index("dp")
    sc = jnp.stack([core, chip % 4, (chip // 4) % PLANES]).astype(jnp.int32)
    count = small_images.shape[0] // 2
    small, large = small_images.shape[1], large_images.shape[1]
    width = channel_expand.shape[0]
    hidden = small_expand.shape[1]
    pad_s, pad_l = round_up(small, 16), round_up(large, 16)

    def theirs(values):
        return lax.dynamic_slice_in_dim(values, (1 - core) * count, count, 0)

    xs_in, xl_in = swap(theirs(small_images)), swap(theirs(large_images))
    tok = jnp.stack([token_gain, token_shift])
    tok_in = swap(tok)
    ys_in, yl_in = swap(theirs(small_cotangent)), swap(theirs(large_cotangent))

    def token_weights(expand, expand_bias, project, project_bias, pad):
        extra = pad - expand.shape[0]
        return [
            jnp.pad(expand, ((0, extra), (0, 0))),
            expand_bias[:, None],
            jnp.pad(project, ((0, 0), (0, extra))),
            jnp.pad(project_bias, (0, extra))[:, None],
        ]

    token_s = token_weights(small_expand, small_expand_bias, small_project, small_project_bias, pad_s)
    token_l = token_weights(large_expand, large_expand_bias, large_project, large_project_bias, pad_l)
    gain2, shift2 = channel_gain[None], channel_shift[None]
    (x1s, n2s, as_, ds_, yrs, x1l, n2l, al, dl, yrl, gy) = front(
        sc, small_images, xs_in, large_images, xl_in, small_cotangent, ys_in, large_cotangent, yl_in,
        tok, tok_in, token_s, token_l, gain2, shift2,
    )

    def rows(values):
        return values.reshape(-1, width)

    rows_in = [rows(n2s), rows(n2l), rows(yrs), rows(yrl)]
    carried = []
    sends, keeps, b1_grads = {}, {}, {}
    for i, plane in enumerate(ORDER):
        is_first, is_last = i == 0, i == PLANES - 1
        ending = [rows(x1s), rows(x1l), gain2, channel_project_bias[None]] if is_last else []
        sends[plane], keeps[plane], b1_grads[plane], *carried = channel(
            sc, plane, is_first, is_last, rows_in,
            channel_expand, channel_expand_bias[None], channel_project, carried, ending,
        )
    out_rows, dx1, g2 = carried
    cut = count * pad_s
    dxs = dx1[:cut].reshape(count, pad_s, width)
    dxl = dx1[cut:].reshape(count, pad_l, width)
    gis_keep, gis_send, gil_keep, gil_send, w_keep, w_send, vec = back(
        sc, dxs, dxl, small_images, xs_in, large_images, xl_in, tok, tok_in,
        [as_, ds_, al, dl],
        [token_s[0], token_s[2], token_l[0], token_l[2]],
        [g2, gy] + [b1_grads[plane] for plane in range(PLANES)],
    )

    def whole_images(keep, received):
        keep_first = jnp.concatenate([keep, received], 0)
        keep_last = jnp.concatenate([received, keep], 0)
        return jnp.where(core == 0, keep_first, keep_last)

    def halves(values):
        half = values.shape[1] // 2
        parts = values.reshape(count, 2, half, width)
        mine = lax.dynamic_index_in_dim(parts, core, 1, False)
        other = lax.dynamic_index_in_dim(parts, 1 - core, 1, False)
        return whole_images(mine, swap(other))

    small_output = halves(out_rows[:cut].reshape(count, pad_s, width)[:, :small])
    large_output = halves(out_rows[cut:].reshape(count, pad_l, width)[:, :large])
    small_input_grad = whole_images(gis_keep, swap(gis_send))
    large_input_grad = whole_images(gil_keep, swap(gil_send))

    if chips == 4 * PLANES:
        everyone = range(chips)
        expands, projects = {}, {}
        for plane in ORDER:
            own, *others = pair_sum(sc, keeps[plane], swap(sends[plane]))
            received = [across(o, k + 1, everyone) for k, o in enumerate(others)]
            d0, d1, d2, d3, rest = quad_sum(sc, own, received)
            expands[plane] = [d0] + [across(d, 4 * k, everyone) for k, d in ((1, d1), (2, d2), (3, d3))]
            projects[plane] = [rest] + [
                across(rest, 4 * k, [4 * (plane ^ k) + c for c in range(4)]) for k in (1, 2, 3)
            ]
        expand_part, project_part = last_sum(sc, expands, projects)
        own, *others = pair_sum(sc, w_keep, swap(w_send))
        vec = vec + swap(vec)
        w, v = token_sum(
            [own] + [across(o, k + 1, everyone) for k, o in enumerate(others)],
            [vec] + [across(vec, k, everyone) for k in (1, 2, 3)],
        )
        w, v = token_sum(
            [w] + [across(w, 4 * k, everyone) for k in (1, 2, 3)],
            [v] + [across(v, 4 * k, everyone) for k in (1, 2, 3)],
        )
        mine = [w] + [across(w, k, everyone) for k in (1, 2, 3)]
    else:
        def both(keep, send):
            return jnp.where(core == 0, jnp.stack([keep, send]), jnp.stack([send, keep])).astype(F32)

        expand_full, project_full = [], []
        for plane in range(PLANES):
            parts = both(keeps[plane], sends[plane])
            cut_rows = width // 8
            e = parts[:, :, :cut_rows].reshape(2, 4, PLANES, width // 32, -1)
            expand_full.append(e.transpose(2, 1, 0, 3, 4).reshape(width, -1))
            project_full.append(parts[:, :, cut_rows:].transpose(1, 0, 2, 3).reshape(-1, width))
        expand_part = lax.psum_scatter(
            jnp.concatenate(expand_full, 1), ("dp", "mp"), scatter_dimension=0, tiled=True
        )
        project_part = lax.psum_scatter(
            jnp.concatenate(project_full, 0), ("dp", "mp"), scatter_dimension=0, tiled=True
        )
        token, v = lax.psum((both(w_keep, w_send), vec), ("dp", "mp"))
        token = lax.dynamic_index_in_dim(token, core, 0, False).astype(BF)
        mine = [lax.dynamic_index_in_dim(token, sc[1] ^ k, 0, False) for k in range(4)]
    unpacked = unpack(
        sc, mine, [swap(w) for w in mine], v, small, large, hidden, channel_expand.shape[1]
    )
    ges, gps, gel, gpl = unpacked[:4]
    (gtg, gts, gbes, gbps, gbel, gbpl, gcg, gcs, gb1, gb2) = [a.reshape(-1) for a in unpacked[4:]]
    return (
        small_output, large_output, small_input_grad, large_input_grad,
        gtg, gts, ges, gbes, gps, gbps, gel, gbel, gpl, gbpl,
        gcg, gcs, expand_part, gb1, project_part, gb2,
    )


def solution(mesh):
    replicated = P()
    by_channel = P("dp", None, "mp")
    by_patch = P("dp", "mp", None)
    by_row = P(("dp", "mp"), None)
    return jax.shard_map(
        functools.partial(per_device, mesh.shape["dp"]),
        mesh=mesh,
        in_specs=(by_channel, by_channel, P("mp"), P("mp")) + (replicated,) * 14 + (by_patch, by_patch),
        out_specs=(by_patch, by_patch, by_channel, by_channel)
        + (replicated,) * 12
        + (by_row, replicated, by_row, replicated),
        check_vma=False,
    )
```

```python
import functools

import jax
import jax.numpy as jnp
from jax import lax
from jax.experimental import pallas as pl
from jax.experimental.pallas import tpu as pltpu
from jax.sharding import PartitionSpec as P

BF = jnp.bfloat16
F32 = jnp.float32
EPS = 1e-06
SQRT_HALF = 0.7071067811865476
INV_SQRT_2PI = 0.3989422804014327
HALF_LOG2E = 0.7213475204444817
NN = ((1,), (0,))
NT = ((1,), (1,))
TN = ((0,), (0,))
MB = 1 << 20
PLANES = 4
ORDER = (0, 3, 1, 2)
VEC = 16


def dot(left, right, dims):
    return lax.dot_general(left, right, (dims, ((), ())), preferred_element_type=F32)


def gelu_pair(values):
    cdf = 0.5 * lax.erf(values * SQRT_HALF) + 0.5
    pdf = jnp.exp2((values * values) * (-HALF_LOG2E)) * INV_SQRT_2PI
    return values * cdf, cdf + values * pdf


def norm(values):
    width = values.shape[-1]
    mean = jnp.sum(values, -1, keepdims=True) * (1.0 / width)
    square = jnp.sum(values * values, -1, keepdims=True) * (1.0 / width)
    scale = lax.rsqrt(square - mean * mean + EPS)
    return (values - mean) * scale, scale


def round_up(value, to):
    return (value + to - 1) // to * to


def call(kernel, sc, deps, inputs, outs, name, limit, scratch=(), aliases=None, cost=None):
    anywhere, vmem = pl.BlockSpec(memory_space=pl.ANY), pl.BlockSpec(memory_space=pltpu.VMEM)
    first = 1 + len(deps)
    return pl.pallas_call(
        functools.partial(kernel, len(deps)),
        in_specs=[pl.BlockSpec(memory_space=pltpu.SMEM)]
        + [vmem] * len(deps)
        + [vmem if not isinstance(a, Far) else anywhere for a in inputs],
        out_specs=[anywhere if len(o) == 3 else vmem for o in outs],
        out_shape=[pltpu.HBM(*o[:2]) if len(o) == 3 else pltpu.VMEM(*o) for o in outs],
        scratch_shapes=scratch,
        input_output_aliases={first + a: b for a, b in (aliases or {}).items()},
        compiler_params=pltpu.CompilerParams(vmem_limit_bytes=limit * MB),
        cost_estimate=cost,
        name=name,
    )(sc, *deps, *[a.array if isinstance(a, Far) else a for a in inputs])


class Far:
    def __init__(self, array):
        self.array = pltpu.with_memory_space_constraint(array, pltpu.HBM)


def start_all(pairs, sems, first=0):
    copies = [pltpu.make_async_copy(a, b, sems.at[first + i]) for i, (a, b) in enumerate(pairs)]
    for copy in copies:
        copy.start()
    return copies


def wait_all(copies):
    for copy in copies:
        copy.wait()


def quarter_of(plane, size, w1, w2):
    here = slice(plane * size, (plane + 1) * size)
    return w1.at[:, here], w2.at[here, :]


def load_image(sc, own, other, dest):
    rows, part = own.shape
    dest[0:rows, pl.ds(pl.multiple_of(sc[0] * part, 128), part)] = own[...].astype(F32)
    dest[0:rows, pl.ds(pl.multiple_of((1 - sc[0]) * part, 128), part)] = other[...].astype(F32)
    if dest.shape[0] != rows:
        dest[rows:, :] = jnp.zeros((dest.shape[0] - rows, dest.shape[1]), F32)


def load_token_params(sc, tok, dest):
    for row in range(2):
        own, other = tok[2 * row : 2 * row + 2]
        part = own.shape[0]
        dest[row : row + 1, pl.ds(pl.multiple_of(sc[0] * part, 128), part)] = own[...][None]
        dest[row : row + 1, pl.ds(pl.multiple_of((1 - sc[0]) * part, 128), part)] = other[...][None]


def fill(dest, source):
    dest[...] = jnp.zeros_like(dest)
    dest[0 : source.shape[0], :] = source[...]


def fill_column(dest, source):
    size = source.shape[0]
    if dest.shape[0] != size:
        dest[...] = jnp.zeros_like(dest)
    dest[0:size, :] = jnp.broadcast_to(source[...][None], (8, size)).T[:, 0:1]


def front_kernel(
    n_deps, sc, xs, xs_in, xl_far, xl_in, gain_own, gain_in, shift_own, shift_in,
    es, bes, pjs, bps, el, bel, pjl, bpl, gain2, shift2, w1, w2,
    n2, w1v, w2v, x1_far, as_far, ds_far, al_far, dl_far,
    xl, xs_f, xs_in_f, x_s, x_l, tk, es_p, pjs_p, bes_c, bps_c, bel_c, bpl_c, x1, as_, ds_, al, dl, sems,
):
    count = xl.shape[0]
    loads = start_all([(xl_far.at[pl.ds(sc[0] * count, count)], xl)], sems, 2 + 6 * count)
    hidden = w1v.shape[1]
    copies = start_all(zip(quarter_of(ORDER[0], hidden, w1, w2), (w1v, w2v)), sems)
    xs_f[...] = xs[...].astype(F32)
    xs_in_f[...] = xs_in[...].astype(F32)
    load_token_params(sc, (gain_own, gain_in, shift_own, shift_in), tk)
    fill(es_p, es)
    fill(pjs_p, pjs)
    fill_column(bes_c, bes)
    fill_column(bps_c, bps)
    fill_column(bel_c, bel)
    fill_column(bpl_c, bpl)
    gain, shift = tk[0:1, :], tk[1:2, :]
    after_gain, after_shift = gain2[...][None], shift2[...][None]

    def group(x_ref, e, be, pj, bp, index, at, a_ref, d_ref):
        rows = x_ref.shape[0]
        hat, _ = norm(x_ref[...])
        normed = (hat * gain + shift).astype(BF)
        active, slope = gelu_pair(dot(e[...], normed, TN) + be[...])
        active = active.astype(BF)
        a_ref[index] = active
        d_ref[index] = slope.astype(d_ref.dtype)
        middle = (x_ref[...] + (dot(pj[...], active, NN) + bp[...])).astype(BF)
        x1[at : at + rows, :] = middle
        hat2, _ = norm(middle.astype(F32))
        n2[at : at + rows, :] = (hat2 * after_gain + after_shift).astype(BF)

    pad_s, pad_l = x_s.shape[1], x_l.shape[1]
    wait_all(loads)
    for i in range(count):
        image = sc[0] * count + i
        load_image(sc, xs_f.at[:, image], xs_in_f.at[:, image], x_s.at[i])
        load_image(sc, xl.at[i], xl_in.at[image], x_l.at[i])
        group(x_s.at[i], es_p, bes_c, pjs_p, bps_c, i, i * pad_s, as_, ds_)
        group(x_l.at[i], el, bel_c, pjl, bpl_c, i, count * pad_s + i * pad_l, al, dl)
        pairs = [(a.at[i], b.at[i]) for a, b in ((as_, as_far), (ds_, ds_far), (al, al_far), (dl, dl_far))]
        for rows in (
            slice(i * pad_s, (i + 1) * pad_s),
            slice(count * pad_s + i * pad_l, count * pad_s + (i + 1) * pad_l),
        ):
            pairs.append((x1.at[rows], x1_far.at[rows]))
        copies += start_all(pairs, sems, len(copies))
    wait_all(copies)


def front(sc, xs, xs_in, xl, xl_in, tok, token_s, token_l, gain2, shift2, w1, w2):
    small, images, part = xs.shape
    count, large, width = images // 2, xl.shape[1], 2 * part
    hidden = token_s[0].shape[1]
    pad_s, pad_l = round_up(small, 16), round_up(large, 16)
    rows = count * (pad_s + pad_l)
    state = (count, hidden, width)
    quarter = w1.shape[1] // PLANES
    return call(
        front_kernel, sc, [],
        [xs, xs_in, Far(xl), xl_in, *tok, *token_s, *token_l, gain2, shift2, Far(w1), Far(w2)],
        [((rows, width), BF), ((width, quarter), BF), ((quarter, width), BF), ((rows, width), BF, None)]
        + [(state, BF, None)] * 4,
        "front", 22,
        [
            pltpu.VMEM((count, large, part), BF),
            *[pltpu.VMEM(xs.shape, F32)] * 2,
            pltpu.VMEM((count, pad_s, width), F32),
            pltpu.VMEM((count, pad_l, width), F32),
            pltpu.VMEM((2, width), F32),
            pltpu.VMEM((pad_s, hidden), BF),
            pltpu.VMEM((pad_s, hidden), BF),
            pltpu.VMEM((hidden, 1), F32),
            pltpu.VMEM((pad_s, 1), F32),
            pltpu.VMEM((hidden, 1), F32),
            pltpu.VMEM((pad_l, 1), F32),
            pltpu.VMEM((rows, width), BF),
            *[pltpu.VMEM(state, BF)] * 4,
            pltpu.SemaphoreType.DMA((3 + 6 * count,)),
        ],
    )


def rows_kernel(n_deps, sc, *refs):
    ys, ys_in, yl_far, yl_in, y, gy, yl, ys_f, ys_in_f, hold, sems = refs[n_deps:]
    first = sc[0] == 0
    half, images, width = ys.shape
    loads = start_all([(yl_far.at[pl.ds(sc[0] * yl.shape[0], yl.shape[0])], yl)], sems)
    ys_f[...] = ys[...].astype(F32)
    ys_in_f[...] = ys_in[...].astype(F32)
    count = images // 2
    pad_s, half_l = hold.shape[0], yl.shape[1]
    sums = jnp.zeros((1, width), F32)
    hold[2 * half :, :] = jnp.zeros((pad_s - 2 * half, width), F32)
    wait_all(loads)
    for i in range(count):
        image = sc[0] * count + i
        mine, theirs = ys_f[:, image, :], ys_in_f[:, image, :]
        sums = sums + jnp.sum(mine, 0, keepdims=True) + jnp.sum(theirs, 0, keepdims=True)
        hold[0:half, :] = jnp.where(first, mine, theirs)
        hold[half : 2 * half, :] = jnp.where(first, theirs, mine)
        y[i * pad_s : (i + 1) * pad_s, :] = hold[...].astype(BF)
        base = count * pad_s + i * 2 * half_l
        for side, part in ((sc[0], yl[i]), (1 - sc[0], yl_in[image])):
            sums = sums + jnp.sum(part.astype(F32), 0, keepdims=True)
            y[pl.ds(pl.multiple_of(base + side * half_l, 16), half_l), :] = part
    gy[...] = sums


def cotangent_rows(sc, deps, ys, ys_in, yl, yl_in):
    hs, images, width = ys.shape
    count, hl = images // 2, yl.shape[1]
    pad_s = round_up(2 * hs, 16)
    return call(
        rows_kernel, sc, deps, [ys, ys_in, Far(yl), yl_in],
        [((count * (pad_s + 2 * hl), width), BF), ((1, width), F32)],
        "rows", 12, [pltpu.VMEM((count, hl, width), BF), *[pltpu.VMEM(ys.shape, F32)] * 2, pltpu.VMEM((pad_s, width), F32), pltpu.SemaphoreType.DMA((1,))],
    )


def channel_kernel(plane, following, is_first, n_deps, sc, *refs):
    is_last = following is None
    refs = list(refs[n_deps:])
    n2, y, w1, b1, w2 = [refs.pop(0) for _ in range(5)]
    if not is_first:
        del refs[:2]
    if is_last:
        x1_far, gain2, b2 = [refs.pop(0) for _ in range(3)]
    else:
        w1_far, w2_far = refs.pop(0), refs.pop(0)
    if is_last:
        acts, grads, gb1, out, dn = [refs.pop(0) for _ in range(5)]
    else:
        send, keep, gb1, out, dn = [refs.pop(0) for _ in range(5)]
    if is_last:
        outs_keep, outs_send, outl_full, outl_send, dx1, g2 = [refs.pop(0) for _ in range(6)]
    else:
        w1_next, w2_next = refs.pop(0), refs.pop(0)
    if not is_last:
        acts, grads = refs.pop(0), refs.pop(0)
    sems = refs.pop(0)
    rows, width = n2.shape
    hidden = acts.shape[1]
    tile = rows // 2
    cols = slice(plane * hidden, (plane + 1) * hidden)
    if is_last:
        outl_keep, x1 = refs
        copies = start_all([(x1_far, x1)], sems)
    else:
        copies = start_all(zip(quarter_of(following, hidden, w1_far, w2_far), (w1_next, w2_next)), sems)
    bias_grad = jnp.zeros((1, hidden), F32)
    for step in range(2):
        here = pl.ds(step * tile, tile)
        active, slope = gelu_pair(dot(n2[here, :], w1[...], NN) + b1[0:1, cols])
        grad = dot(y[here, :], w2[...], NT) * slope
        bias_grad = bias_grad + jnp.sum(grad, 0, keepdims=True)
        acts[here, :] = active.astype(BF)
        grads[here, :] = grad.astype(BF)
    gb1[...] = bias_grad
    for step in range(2):
        here = pl.ds(step * tile, tile)
        mixed = dot(acts[here, :], w2[...], NN)
        back = dot(grads[here, :], w1[...], NT)
        if is_first:
            out[here, :] = mixed
            dn[here, :] = back
        else:
            out[here, :] += mixed
            dn[here, :] += back
    first = sc[0] == 0
    if is_last:
        wait_all(copies)
        copies = []
        count, half_s = outs_keep.shape[:2]
        half_l = outl_keep.shape[1]
        pad_s = round_up(2 * half_s, 16)
        gain = gain2[...][None]
        gain_sum = jnp.zeros((1, width), F32)
        shift_sum = jnp.zeros((1, width), F32)
        for low in range(0, rows, tile):
            here = slice(low, low + tile)
            middle = x1[here, :].astype(F32)
            out[here, :] = middle + out[here, :] + b2[...][None]
            hat, scale = norm(middle)
            back = dn[here, :]
            gain_sum = gain_sum + jnp.sum(back * hat, 0, keepdims=True)
            shift_sum = shift_sum + jnp.sum(back, 0, keepdims=True)
            scaled = back * gain
            mean = jnp.sum(scaled, -1, keepdims=True) * (1.0 / width)
            along = jnp.sum(scaled * hat, -1, keepdims=True) * (1.0 / width)
            dx1[here, :] = (
                y[here, :].astype(F32) + scale * (scaled - mean - hat * along)
            ).astype(BF)
        g2[0:1, :] = gain_sum
        g2[1:2, :] = shift_sum
        base = 0
        for size, padded, to_keep, to_send, full in (
            (half_s, pad_s, outs_keep, outs_send, None),
            (half_l, 2 * half_l, outl_keep, outl_send, outl_full),
        ):
            for i in range(count):
                low = out[base : base + size, :]
                high = out[base + size : base + 2 * size, :]
                to_keep[i] = jnp.where(first, low, high).astype(BF)
                to_send[i] = jnp.where(first, high, low).astype(BF)
                base += padded
            if full is not None:
                copies = start_all([(to_keep, full.at[pl.ds(sc[0] * count, count)])], sems)
    else:
        weight_grads(sc, n2, y, acts, grads, send, keep)
    wait_all(copies)


def weight_grads(sc, n2, y, acts, grads, send, keep):
    width, hidden = n2.shape[1], acts.shape[1]
    first = sc[0] == 0
    quarter = width // 32
    cut = PLANES * quarter
    expand = dot(n2[...], grads[...], TN).reshape(PLANES, 4, 2, quarter, hidden)
    for c in range(4):
        low = expand[:, c, 0].reshape(cut, hidden)
        high = expand[:, c, 1].reshape(cut, hidden)
        keep[c, 0:cut, :] = jnp.where(first, low, high).astype(BF)
        send[c, 0:cut, :] = jnp.where(first, high, low).astype(BF)
    project = dot(acts[...], y[...], TN).reshape(4, 2, hidden // 8, width)
    for c in range(4):
        low, high = project[c, 0], project[c, 1]
        keep[c, cut:, :] = jnp.where(first, low, high).astype(BF)
        send[c, cut:, :] = jnp.where(first, high, low).astype(BF)


def weights_kernel(n_deps, sc, *refs):
    weight_grads(sc, *refs[n_deps:])


def channel_weights(sc, deps, n2, y, acts, grads):
    width, hidden = n2.shape[1], acts.shape[1]
    block = (4, width // 8 + hidden // 8, width)
    return call(
        weights_kernel, sc, deps, [n2, y, acts, grads], [(block, BF)] * 2, "weights", 12,
        cost=pl.CostEstimate(
            flops=4 * n2.shape[0] * width * hidden, bytes_accessed=MB, transcendentals=0
        ),
    )


def channel(sc, deps, plane, following, rows_in, w1, b1, w2, carried, ending, halves):
    is_first, is_last = not carried, following is None
    rows, width = rows_in[0].shape
    hidden = w1.shape[1]
    block = (4, width // 8 + hidden // 8, width)
    outs = [((rows, hidden) if is_last else block, BF)] * 2
    outs += [((1, hidden), F32), ((rows, width), F32), ((rows, width), F32)]
    scratch = [pltpu.SemaphoreType.DMA((2,))]
    if not is_last:
        outs += [(w1.shape, BF), (w2.shape, BF)]
        scratch = [pltpu.VMEM((rows, hidden), BF)] * 2 + scratch
    else:
        count, half_s, half_l = halves
        outs += [((count, half_s, width), BF)] * 2
        outs += [((2 * count, half_l, width), BF, None), ((count, half_l, width), BF)]
        scratch.append(pltpu.VMEM((count, half_l, width), BF))
        outs += [((rows, width), BF), ((2, width), F32)]
        scratch.append(pltpu.VMEM((rows, width), BF))
    return call(
        functools.partial(channel_kernel, plane, following, is_first), sc, deps,
        [*rows_in, w1, b1, w2, *carried, *ending], outs, "channel", 14 if is_last else 17, scratch,
        None if is_first else {5: 3, 6: 4},
        pl.CostEstimate(
            flops=(8 if is_last else 12) * rows * width * hidden, bytes_accessed=4 * MB, transcendentals=2 * rows * hidden
        ),
    )


def back_kernel(n_deps, sc, *refs):
    (
        dx1, xs_far, xs_in_far, xl_far, xl_in_far, gain_own, gain_in, shift_own, shift_in, as_far, ds_far, al_far, dl_far,
        es, pjs, el, pjl, g2, gy, b1a, b1b, b1c, b1d,
        gis_keep, gis_send, gil, gil_send, w_keep, w_send,
        vec, x_s, x_l, tk, es_p, pjs_p, gps, ges, gpl, gel, gi_s, gi_l, gil_keep,
        xs_f, xs_in_f, xs, xs_in, xl, xl_in, as_, ds_, al, dl, sems,
    ) = refs[n_deps:]
    count = as_.shape[0]
    loads = []
    small_loads = start_all([(xs_far, xs), (xs_in_far, xs_in)], sems)
    for i in range(count):
        pairs = [
            (far.at[sc[0] * count + i], ref.at[i])
            for far, ref in ((xl_far, xl), (xl_in_far, xl_in))
        ]
        pairs += [(far.at[i], ref.at[i]) for far, ref in ((ds_far, ds_), (as_far, as_), (dl_far, dl), (al_far, al))]
        loads.append(start_all(pairs, sems, 2 + 6 * i))
    load_token_params(sc, (gain_own, gain_in, shift_own, shift_in), tk)
    fill(es_p, es)
    fill(pjs_p, pjs)
    vec[...] = jnp.zeros_like(vec)
    gain, shift = tk[0:1, :], tk[1:2, :]

    def group(x_ref, index, at, a, d, e, pj, gp, ge, be_at, bp_row, gi, keep, send):
        rows, width = x_ref.shape
        hidden = a.shape[1]
        dx = dx1[at : at + rows, :]
        hat, scale = norm(x_ref[...])
        normed = (hat * gain + shift).astype(BF)
        before = (dot(pj[...], dx, TN) * d[index].astype(F32)).astype(BF)
        grad = dot(e[...], before, NN)
        project_grad = dot(dx, a[index], NT)
        expand_grad = dot(normed, before, NT)
        if index == 0:
            gp[0:rows, :] = project_grad
            ge[0:rows, :] = expand_grad
        else:
            gp[0:rows, :] += project_grad
            ge[0:rows, :] += expand_grad
        ones = jnp.ones((8, width), BF)
        vec[bp_row : bp_row + 1, 0:rows] += dot(ones, dx, NT)[0:1, :]
        vec[9:10, be_at : be_at + hidden] += dot(ones, before, NT)[0:1, :]
        vec[0:1, :] += jnp.sum(grad * hat, 0, keepdims=True)
        vec[1:2, :] += jnp.sum(grad, 0, keepdims=True)
        scaled = grad * gain
        mean = jnp.sum(scaled, -1, keepdims=True) * (1.0 / width)
        along = jnp.sum(scaled * hat, -1, keepdims=True) * (1.0 / width)
        gi[...] = dx.astype(F32) + scale * (scaled - mean - hat * along)
        part = width // 2
        size = keep.shape[1]
        keep[index] = gi[0:size, pl.ds(pl.multiple_of(sc[0] * part, 128), part)].astype(BF)
        send[index] = gi[0:size, pl.ds(pl.multiple_of((1 - sc[0]) * part, 128), part)].astype(BF)

    hidden = as_.shape[1]
    pad_s, pad_l = x_s.shape[1], x_l.shape[1]
    wait_all(small_loads)
    xs_f[...] = xs[...].astype(F32)
    xs_in_f[...] = xs_in[...].astype(F32)
    for i in range(count):
        wait_all(loads[i])
        image = sc[0] * count + i
        load_image(sc, xs_f.at[:, image], xs_in_f.at[:, image], x_s.at[i])
        load_image(sc, xl.at[i], xl_in.at[i], x_l.at[i])
        group(x_s.at[i], i, i * pad_s, as_, ds_, es_p, pjs_p, gps, ges, 0, 10, gi_s, gis_keep, gis_send)
        group(
            x_l.at[i], i, count * pad_s + i * pad_l, al, dl, el, pjl, gpl, gel, hidden, 11,
            gi_l, gil_keep, gil_send,
        )
    copies = start_all([(gil_keep, gil.at[pl.ds(sc[0] * count, count)])], sems)
    vec[2:4, :] = g2[...]
    vec[4:5, :] = gy[...]
    for i, ref in enumerate((b1a, b1b, b1c, b1d)):
        vec[5 + i : 6 + i, :] = ref[...]
    size = w_keep.shape[2]
    half_s, half_l = gps.shape[0] // 2, gpl.shape[0] // 2
    for ref in (gps, ges):
        ref[pad_s:, :] = jnp.zeros((ref.shape[0] - pad_s, hidden), F32)
    for side, ref in ((sc[0], w_keep), (1 - sc[0], w_send)):
        for t, (small, large) in enumerate(((gps, gpl), (ges, gel))):
            at = pl.multiple_of(side * half_s, 8)
            ref[0, t] = small[pl.ds(at, size), :].astype(BF)
            for c in range(1, 4):
                have = min(size, half_l - (c - 1) * size)
                at = pl.multiple_of(side * half_l + (c - 1) * size, 8)
                ref[c, t, 0:have, :] = large[pl.ds(at, have), :].astype(BF)
                if have < size:
                    ref[c, t, have:, :] = jnp.zeros((size - have, hidden), BF)
        at = pl.multiple_of(side * hidden, 128)
        ref[3, 0, have : have + VEC, :] = vec[:, pl.ds(at, hidden)].astype(BF)
    wait_all(copies)


def piece_rows(pad_s, pad_l):
    return max(round_up(pad_s // 2, 16), round_up(-(-(pad_l // 2 + VEC) // 3), 16))


def back(sc, deps, dx1, xs, xs_in, xl, xl_in, tok, saved, weights, vectors):
    small, images, part = xs.shape
    count, large, width = images // 2, xl.shape[1], 2 * part
    pad_s, pad_l = round_up(small, 16), round_up(large, 16)
    hidden = saved[0].shape[1]
    size = piece_rows(pad_s, pad_l)
    return call(
        back_kernel, sc, deps,
        [dx1, Far(xs), Far(xs_in), Far(xl), Far(xl_in), *tok, *[Far(a) for a in saved], *weights, *vectors],
        [
            ((count, small, part), BF),
            ((count, small, part), BF),
            ((images, large, part), BF, None),
            ((count, large, part), BF),
            ((4, 2, size, hidden), BF),
            ((4, 2, size, hidden), BF),
        ],
        "back", 27,
        [
            pltpu.VMEM((VEC, width), F32),
            pltpu.VMEM((count, pad_s, width), F32),
            pltpu.VMEM((count, pad_l, width), F32),
            pltpu.VMEM((2, width), F32),
            pltpu.VMEM((pad_s, hidden), BF),
            pltpu.VMEM((pad_s, hidden), BF),
            pltpu.VMEM((2 * size, hidden), F32),
            pltpu.VMEM((2 * size, hidden), F32),
            pltpu.VMEM((pad_l, hidden), F32),
            pltpu.VMEM((pad_l, hidden), F32),
            pltpu.VMEM((pad_s, width), F32),
            pltpu.VMEM((pad_l, width), F32),
            pltpu.VMEM((count, large, part), BF),
            *[pltpu.VMEM(xs.shape, F32)] * 2,
            *[pltpu.VMEM(xs.shape, BF)] * 2,
            *[pltpu.VMEM((count, large, part), BF)] * 2,
            *[pltpu.VMEM((count, hidden, width), BF)] * 4,
            pltpu.SemaphoreType.DMA((2 + 6 * count,)),
        ],
    )


def total4(parts):
    a, b, c, d = [p.astype(F32) for p in parts]
    return (a + b) + (c + d)


def pair_kernel(n_deps, sc, *refs):
    keep, recv = refs[n_deps : n_deps + 2]
    for k, ref in enumerate(refs[-4:]):
        ref[...] = (keep[sc[1] ^ k].astype(F32) + recv[sc[1] ^ k].astype(F32)).astype(BF)


def pair_sum(sc, deps, keep, recv, passenger=None):
    outs = [(keep.shape[1:], BF)] * 4
    if passenger is None:
        return call(pair_kernel, sc, deps, [keep, recv], outs, "pair_sum", 4)
    passed, *sums = call(
        pair_kernel, sc, deps, [keep, recv, passenger], [(passenger.shape, BF)] + outs, "pair_sum", 4,
        aliases={2: 0},
    )
    return sums, passed


def sides_kernel(n_deps, sc, *refs):
    keep, recv, *outs = refs[n_deps:]
    half = keep.shape[2] // 2
    x, y = sc[1] % 2, sc[1] // 2
    for side in range(2):
        cols = slice(side * half, (side + 1) * half)
        for stays, ref in ((True, outs[2 * side]), (False, outs[2 * side + 1])):
            for k in range(2):
                if side == 0:
                    chip = 2 * (y ^ k) + (x if stays else 1 - x)
                else:
                    chip = 2 * (y if stays else 1 - y) + (x ^ k)
                total = keep[chip, :, cols].astype(F32) + recv[chip, :, cols].astype(F32)
                ref[k] = total.astype(BF)


def sides_sum(sc, deps, keep, recv):
    chips, rows, width = keep.shape
    return call(
        sides_kernel, sc, deps, [keep, recv], [((2, rows, width // 2), BF)] * 4, "sides_sum", 4
    )


def second_kernel(n_deps, sc, *refs):
    refs = refs[n_deps:]
    for side in range(2):
        keep, recv = refs[2 * side : 2 * side + 2]
        for k in range(2):
            refs[4 + 2 * side + k][...] = (keep[k].astype(F32) + recv[k].astype(F32)).astype(BF)


def second_sum(sc, deps, parts):
    return call(second_kernel, sc, deps, parts, [(parts[0].shape[1:], BF)] * 4, "second_sum", 4)


def quad_kernel(n_deps, sc, *refs):
    refs = refs[n_deps:]
    keep, send, hold, rest = refs[8:]
    rows = refs[0].shape[0] // 2
    quarter = rows // PLANES
    half = rest.shape[2] // 2
    for i in range(2):
        part = refs[4 * i : 4 * i + 4]
        if part[0].shape[1] == half:
            sums = [part[j][...].astype(F32) + part[j + 1][...].astype(F32) for j in (0, 2)]
            total = jnp.concatenate(sums, 1)
        else:
            total = total4([r[...] for r in part])
        hold[i] = total[0:rows].reshape(hold.shape[1:])
        rest[i] = total[rows:]
    high, low = sc[2] // 2, sc[2] % 2
    for side, ref in ((high, keep), (1 - high, send)):
        for k in range(2):
            pair = [hold[i, 2 * side + (low ^ k)] for i in range(2)]
            ref[2 * k * quarter : 2 * (k + 1) * quarter, :] = jnp.concatenate(pair, 0).astype(BF)
        ref[rows:, :] = rest[side].astype(BF)


def quad_sum(sc, deps, first, second):
    rows, width = first[0].shape
    quarter = rows // 2 // PLANES
    return call(
        quad_kernel, sc, deps, first + second, [((rows, width), BF)] * 2, "quad_sum", 6,
        [pltpu.VMEM((2, PLANES, quarter, width), F32), pltpu.VMEM((2, rows // 2, width), F32)],
    )


def planes_kernel(n_deps, sc, *refs):
    a, b = refs[n_deps : n_deps + 2]
    keep, send = refs[-2:]
    rows = a.shape[0]
    cut = rows // 4
    total = a[...].astype(F32) + b[...].astype(F32)
    keep[0:cut, :] = total[0:cut].astype(BF)
    send[0:cut, :] = total[cut : 2 * cut].astype(BF)
    rest = total[2 * cut :].astype(BF)
    keep[cut:, :] = rest
    send[cut:, :] = rest


def planes_sum(sc, deps, keep, recv, passengers=()):
    rows, width = keep.shape
    passed = [(a.shape, a.dtype) for a in passengers]
    *passed, keep, send = call(
        planes_kernel, sc, deps, [keep, recv, *passengers], passed + [((3 * rows // 4, width), BF)] * 2,
        "planes_sum", 4, aliases={2 + i: i for i in range(len(passed))},
    )
    return keep, send, passed


def last_kernel(groups, n_deps, sc, *refs):
    refs = refs[n_deps:]
    expand_out, project_out, expand, project, sems = refs[-5:]
    width = expand.shape[1] // PLANES
    quarter = expand.shape[0]
    for g, planes in enumerate(groups):
        total = refs[2 * g][...].astype(F32) + refs[2 * g + 1][...].astype(F32)
        for i, plane in enumerate(planes):
            expand[:, plane * width : (plane + 1) * width] = total[i * quarter : (i + 1) * quarter]

        @pl.when((sc[2] == planes[0]) | (sc[2] == planes[1]))
        def _():
            project[...] = total[2 * quarter :]

    wait_all(start_all([(expand, expand_out), (project, project_out)], sems))


def last_sum(sc, groups, pieces):
    flat = [a for group in groups for a in pieces[group]]
    rows, width = flat[0].shape
    shapes = [(rows // 6, PLANES * width), (2 * rows // 3, width)]
    return call(
        functools.partial(last_kernel, groups), sc, [], flat, [(s, F32, None) for s in shapes], "last_sum", 4,
        [pltpu.VMEM(s, F32) for s in shapes] + [pltpu.SemaphoreType.DMA((2,))],
    )


def token_sum_kernel(n_deps, sc, *refs):
    refs[-1][...] = total4([r[...] for r in refs[n_deps : n_deps + 4]]).astype(BF)


def token_sum(sc, deps, parts):
    return call(token_sum_kernel, sc, deps, parts, [(parts[0].shape, BF)], "token_sum", 4)[0]


def unpack_kernel(n_deps, sc, *refs):
    refs = refs[n_deps:]
    mine, theirs = refs[0:4], refs[4:8]
    ges, gps, gel, gpl = refs[8:12]
    vectors = refs[12:22]
    hold, vec = refs[22:]
    for k in range(4):
        hold[sc[0], sc[1] ^ k] = mine[k][...]
        hold[1 - sc[0], sc[1] ^ k] = theirs[k][...]
    size, hidden = mine[0].shape[1:]
    small, large = ges.shape[0], gel.shape[0]
    for side in range(2):
        low = side * size
        have = min(size, small - low)
        for t, ref in enumerate((gps, ges)):
            ref[low : low + have, :] = hold[side, 0, t].astype(F32)[0:have, :]
        for c in range(1, 4):
            low = side * (large // 2) + (c - 1) * size
            have = min(size, large // 2 - (c - 1) * size)
            for t, ref in enumerate((gpl, gel)):
                ref[low : low + have, :] = hold[side, c, t].astype(F32)[0:have, :]
        vec[:, side * hidden : (side + 1) * hidden] = hold[side, 3, 0].astype(F32)[have : have + VEC, :]
    width = vec.shape[1]
    picks = [(0, 0), (1, 0), (9, 0), (10, 0), (9, hidden), (11, 0), (2, 0), (3, 0), None, (4, 0)]
    for ref, pick in zip(vectors, picks):
        if pick is None:
            for i in range(ref.shape[0] // width):
                ref[i * width : (i + 1) * width] = vec[5 + i, :]
        else:
            row, at = pick
            ref[...] = vec[row, at : at + ref.shape[0]]


def unpack(sc, deps, mine, theirs, small, large, width, channel_hidden):
    hidden = mine[0].shape[2]
    outs = [(small, hidden)] * 2 + [(large, hidden)] * 2
    outs += [(n,) for n in (width, width, hidden, small, hidden, large, width, width, channel_hidden, width)]
    return pl.pallas_call(
        functools.partial(unpack_kernel, len(deps)),
        in_specs=[pl.BlockSpec(memory_space=pltpu.SMEM)]
        + [pl.BlockSpec(memory_space=pltpu.VMEM)] * (len(deps) + 8),
        out_shape=[jax.ShapeDtypeStruct(s, F32) for s in outs],
        scratch_shapes=[pltpu.VMEM((2, 4) + mine[0].shape, BF), pltpu.VMEM((VEC, width), F32)],
        compiler_params=pltpu.CompilerParams(vmem_limit_bytes=12 * MB),
        name="unpack",
    )(sc, *deps, *mine, *theirs)


def place_kernel(n_deps, sc, *refs):
    refs = refs[n_deps:]
    small, large = refs[0:4], refs[6:8]
    tick, far_small, far_large, near, sems = refs[8], refs[9:11], refs[11:13], refs[13:15], refs[15]
    count = large[0].shape[0]
    pairs = [(a, b.at[pl.ds((1 - sc[0]) * count, count)]) for a, b in zip(large, far_large)]
    copies = start_all(pairs, sems)
    for i in range(2):
        mine, theirs = small[2 * i : 2 * i + 2]
        for j in range(2 * count):
            own = sc[0] == j // count
            k = j % count
            near[i][:, j, :] = jnp.where(own, mine[k].astype(F32), theirs[k].astype(F32)).astype(BF)
    copies += start_all(zip(near, far_small), sems, 2)
    tick[...] = jnp.zeros_like(tick)
    wait_all(copies)


def place(sc, deps, small, filled, received):
    shapes = [(a.shape[1], 2 * a.shape[0], a.shape[2]) for a in small[0::2]]
    return call(
        place_kernel, sc, deps, small + [Far(a) for a in filled] + received,
        [((8, 128), F32)] + [(shape, BF, None) for shape in shapes] + [(a.shape, BF, None) for a in filled],
        "place", 6,
        [pltpu.VMEM(shape, BF) for shape in shapes] + [pltpu.SemaphoreType.DMA((4,))],
        {4: 3, 5: 4},
    )


def swap(values):
    return lax.ppermute(values, "mp", [(0, 1), (1, 0)])


def across(values, mask, pairs):
    return lax.ppermute(values, "dp", [(i, i ^ mask) for i in pairs])


def per_device(
    chips,
    small_images,
    large_images,
    token_gain,
    token_shift,
    small_expand,
    small_expand_bias,
    small_project,
    small_project_bias,
    large_expand,
    large_expand_bias,
    large_project,
    large_project_bias,
    channel_gain,
    channel_shift,
    channel_expand,
    channel_expand_bias,
    channel_project,
    channel_project_bias,
    small_cotangent,
    large_cotangent,
):
    core = lax.axis_index("mp")
    chip = lax.axis_index("dp")
    sc = jnp.stack([core, chip % 4, (chip // 4) % PLANES]).astype(jnp.int32)
    small_images, small_cotangent = small_images.transpose(1, 0, 2), small_cotangent.transpose(1, 0, 2)
    small, images, part = small_images.shape
    large = large_images.shape[1]
    count = images // 2
    width = channel_expand.shape[0]
    everyone = range(chips)
    tuned = chips == 4 * PLANES

    xs_in, xl_in = swap(small_images), swap(large_images)
    tok = [token_gain, swap(token_gain), token_shift, swap(token_shift)]
    ys_in, yl_in = swap(small_cotangent), swap(large_cotangent)
    token_s = [small_expand, small_expand_bias, small_project.T, small_project_bias]
    token_l = [large_expand, large_expand_bias, large_project.T, large_project_bias]
    n2, w1, w2, x1, as_, ds_, al, dl = front(
        sc, small_images, xs_in, large_images, xl_in, tok, token_s, token_l,
        channel_gain, channel_shift, channel_expand, channel_project,
    )
    y, gy = cotangent_rows(sc, [n2], small_cotangent, ys_in, large_cotangent, yl_in)
    carried = []
    sends, keeps, b1_grads, halved, pieces = {}, {}, {}, {}, {}
    groups = (ORDER[:2], ORDER[2:])

    def halve(plane, deps, passenger=None):
        sums = pair_sum(sc, deps, keeps[plane], swap(sends[plane]), None if passenger is None else sends[passenger])
        if passenger is not None:
            sums, sends[passenger] = sums
        own, *others = sums
        halved[plane] = [own] + [across(o, k + 1, everyone) for k, o in enumerate(others)]

    def quarter(group, deps, later):
        keep, send = quad_sum(sc, deps, halved[group[0]], halved[group[1]])
        pieces[group] = [keep, across(send, 8, everyone)]

        def finish(deps, passengers=()):
            keep, send, passed = planes_sum(sc, deps, *pieces[group], passengers)
            pieces[group] = [keep, across(send, 4, everyone)]
            return passed

        return finish

    n_last = PLANES - 1
    for i, plane in enumerate(ORDER):
        is_last = i == n_last
        following = None if is_last else ORDER[i + 1]
        if is_last:
            ending = [Far(x1), channel_gain, channel_project_bias]
        else:
            ending = [Far(channel_expand), Far(channel_project)]
        deps = []
        if tuned and i >= 2:
            arrived = halved[ORDER[i - 3]][1:] if i >= 3 else []
            halve(ORDER[i - 2], [b1_grads[ORDER[i - 1]]] + arrived, ORDER[2] if is_last else None)
            deps = halved[ORDER[i - 2]][:1]
        first_out, second_out, b1_grads[plane], *carried = channel(
            sc, deps, plane, following, [n2, y], w1, channel_expand_bias[None], w2,
            carried, ending, (count, small // 2, large // 2),
        )
        if not is_last:
            sends[plane], keeps[plane] = first_out, second_out
            *carried, w1, w2 = carried
    acts, grads = first_out, second_out
    _, _, outs_keep, outs_send, outl_full, outl_send, dx1, g2 = carried
    deps = []
    if tuned:
        finish = quarter(groups[0], [b1_grads[ORDER[3]]], None)
        halve(ORDER[2], [b1_grads[ORDER[3]]] + halved[ORDER[1]][1:])
        deps = [pieces[groups[0]][0], halved[ORDER[2]][0]]
    gis_keep, gis_send, gil, gil_send, w_keep, w_send = back(
        sc, deps, dx1, small_images, xs_in, large_images, xl_in, tok,
        [as_, ds_, al, dl],
        [small_expand, small_project.T, large_expand, large_project.T],
        [g2, gy] + [b1_grads[plane] for plane in range(PLANES)],
    )
    deps = [w_keep]
    if tuned:
        w_send, gis_send, gil_send = finish([w_keep] + halved[ORDER[2]][1:], [w_send, gis_send, gil_send])
        deps += [pieces[groups[0]][0]]
    sends[ORDER[3]], keeps[ORDER[3]] = channel_weights(sc, deps, n2, y, acts, grads)

    def deliver(deps):
        return place(
            sc, deps, [outs_keep, swap(outs_send), gis_keep, swap(gis_send)], [outl_full, gil],
            [swap(outl_send), swap(gil_send)],
        )

    if tuned:
        last = ORDER[3]
        (own, *others), sends[last] = pair_sum(
            sc, [keeps[last], pieces[groups[0]][1]], w_keep, swap(w_send), sends[last]
        )
        parts = [own] + [across(o, k + 1, everyone) for k, o in enumerate(others)]
        keep_a, send_a, keep_b, send_b = sides_sum(sc, [own], keeps[last], swap(sends[last]))
        w = token_sum(sc, [keep_a], parts)
        parts = [w] + [across(w, 4 * k, everyone) for k in (1, 2, 3)]
        keep_a, send_a, keep_b, send_b = second_sum(
            sc, [w], [keep_a, across(send_a, 1, everyone), keep_b, across(send_b, 2, everyone)]
        )
        halved[last] = [keep_a, across(send_a, 2, everyone), keep_b, across(send_b, 1, everyone)]
        finish = quarter(groups[1], [w], None)
        tick, small_output, small_input_grad, large_output, large_input_grad = deliver([pieces[groups[1]][0]])
        w = token_sum(sc, [tick], parts)
        mine = [w] + [across(w, k, everyone) for k in (1, 2, 3)]
        finish([w])
        expand_part, project_part = last_sum(sc, groups, pieces)
    else:
        _, small_output, small_input_grad, large_output, large_input_grad = deliver([])

        def both(keep, send):
            return jnp.where(core == 0, jnp.stack([keep, send]), jnp.stack([send, keep])).astype(F32)

        expand_full, project_full = [], []
        for plane in range(PLANES):
            parts = both(keeps[plane], sends[plane])
            cut = width // 8
            e = parts[:, :, :cut].reshape(2, 4, PLANES, width // 32, -1)
            expand_full.append(e.transpose(2, 1, 0, 3, 4).reshape(width, -1))
            project_full.append(parts[:, :, cut:].transpose(1, 0, 2, 3).reshape(-1, width))
        expand_part = lax.psum_scatter(
            jnp.concatenate(expand_full, 1), ("dp", "mp"), scatter_dimension=0, tiled=True
        )
        project_part = lax.psum_scatter(
            jnp.concatenate(project_full, 0), ("dp", "mp"), scatter_dimension=0, tiled=True
        )
        token = lax.psum(both(w_keep, w_send), ("dp", "mp"))
        token = lax.dynamic_index_in_dim(token, core, 0, False).astype(BF)
        mine = [lax.dynamic_index_in_dim(token, sc[1] ^ k, 0, False) for k in range(4)]
    unpacked = unpack(
        sc, [], mine, [swap(w) for w in mine], small, large, width, channel_expand.shape[1]
    )
    (ges, gps_t, gel, gpl_t, gtg, gts, gbes, gbps, gbel, gbpl, gcg, gcs, gb1, gb2) = unpacked
    small_output, small_input_grad = small_output.transpose(1, 0, 2), small_input_grad.transpose(1, 0, 2)
    return (
        small_output, large_output, small_input_grad, large_input_grad,
        gtg, gts, ges, gbes, gps_t.T, gbps, gel, gbel, gpl_t.T, gbpl,
        gcg, gcs, expand_part, gb1, project_part, gb2,
    )


def solution(mesh):
    replicated = P()
    by_channel = P("dp", None, "mp")
    by_patch = P("dp", "mp", None)
    by_row = P(("dp", "mp"), None)
    return jax.shard_map(
        functools.partial(per_device, mesh.shape["dp"]),
        mesh=mesh,
        in_specs=(by_channel, by_channel, P("mp"), P("mp")) + (replicated,) * 14 + (by_patch, by_patch),
        out_specs=(by_patch, by_patch, by_channel, by_channel)
        + (replicated,) * 12
        + (by_row, replicated, by_row, replicated),
        check_vma=False,
    )
```

```python
import functools

import jax
import jax.numpy as jnp
from jax import lax
from jax.experimental import pallas as pl
from jax.experimental.pallas import tpu as pltpu
from jax.sharding import PartitionSpec as P

BF = jnp.bfloat16
F32 = jnp.float32
EPS = 1e-06
SQRT_HALF = 0.7071067811865476
INV_SQRT_2PI = 0.3989422804014327
HALF_LOG2E = 0.7213475204444817
NN = ((1,), (0,))
NT = ((1,), (1,))
TN = ((0,), (0,))
MB = 1 << 20
GFLOP = 10**9
PLANES = 4
ORDER = (0, 3, 1, 2)
VEC = 16


def dot(left, right, dims):
    return lax.dot_general(left, right, (dims, ((), ())), preferred_element_type=F32)


def gelu_pair(values):
    cdf = 0.5 * lax.erf(values * SQRT_HALF) + 0.5
    pdf = jnp.exp2((values * values) * (-HALF_LOG2E)) * INV_SQRT_2PI
    return values * cdf, cdf + values * pdf


def norm(values):
    width = values.shape[-1]
    mean = jnp.sum(values, -1, keepdims=True) * (1.0 / width)
    square = jnp.sum(values * values, -1, keepdims=True) * (1.0 / width)
    scale = lax.rsqrt(square - mean * mean + EPS)
    return (values - mean) * scale, scale


def round_up(value, to):
    return (value + to - 1) // to * to


def call(kernel, sc, deps, inputs, outs, name, limit, scratch=(), aliases=None, cost=0):
    anywhere, vmem = pl.BlockSpec(memory_space=pl.ANY), pl.BlockSpec(memory_space=pltpu.VMEM)
    first = 1 + len(deps)
    return pl.pallas_call(
        functools.partial(kernel, len(deps)),
        in_specs=[pl.BlockSpec(memory_space=pltpu.SMEM)]
        + [vmem] * len(deps)
        + [vmem if not isinstance(a, Far) else anywhere for a in inputs],
        out_specs=[anywhere if len(o) == 3 else vmem for o in outs],
        out_shape=[pltpu.HBM(*o[:2]) if len(o) == 3 else pltpu.VMEM(*o) for o in outs],
        scratch_shapes=scratch,
        input_output_aliases={first + a: b for a, b in (aliases or {}).items()},
        compiler_params=pltpu.CompilerParams(vmem_limit_bytes=limit * MB),
        cost_estimate=pl.CostEstimate(flops=cost, bytes_accessed=0, transcendentals=0),
        name=name,
    )(sc, *deps, *[a.array if isinstance(a, Far) else a for a in inputs])


class Far:
    def __init__(self, array):
        self.array = pltpu.with_memory_space_constraint(array, pltpu.HBM)


def start_all(pairs, sems, first=0):
    copies = [pltpu.make_async_copy(a, b, sems.at[first + i]) for i, (a, b) in enumerate(pairs)]
    for copy in copies:
        copy.start()
    return copies


def wait_all(copies):
    for copy in copies:
        copy.wait()


def quarter_of(plane, size, w1, w2):
    here = slice(plane * size, (plane + 1) * size)
    return w1.at[:, here], w2.at[here, :]


def load_image(sc, own, other, dest):
    rows, part = own.shape
    dest[0:rows, pl.ds(pl.multiple_of(sc[0] * part, 128), part)] = own[...].astype(F32)
    dest[0:rows, pl.ds(pl.multiple_of((1 - sc[0]) * part, 128), part)] = other[...].astype(F32)
    if dest.shape[0] != rows:
        dest[rows:, :] = jnp.zeros((dest.shape[0] - rows, dest.shape[1]), F32)


def load_token_params(sc, tok, dest):
    for row in range(2):
        own, other = tok[2 * row : 2 * row + 2]
        part = own.shape[0]
        dest[row : row + 1, pl.ds(pl.multiple_of(sc[0] * part, 128), part)] = own[...][None]
        dest[row : row + 1, pl.ds(pl.multiple_of((1 - sc[0]) * part, 128), part)] = other[...][None]


def fill(dest, source):
    rows = source.shape[0]
    dest[0:rows, :] = source[...]
    if dest.shape[0] != rows:
        dest[rows:, :] = jnp.zeros((dest.shape[0] - rows, dest.shape[1]), dest.dtype)


def fill_column(dest, source):
    size = source.shape[0]
    if dest.shape[0] != size:
        dest[...] = jnp.zeros_like(dest)
    dest[0:size, :] = jnp.broadcast_to(source[...][None], (8, size)).T[:, 0:1]


def prepare_kernel(
    n_deps, sc, xs_far, xl_far, yl_far, w1, w2, el_far, pjl_far, es_far, pjs_far, bes_far, bps_far, bel_far, bpl_far,
    xs, xl, y, w1v, w2v, el, pjl, es_p, pjs_p, bes_c, bps_c, bel_c, bpl_c,
    es, pjs, bes, bps, bel, bpl, sems,
):
    count, half = xl.shape[0], yl_far.shape[1]
    own = pl.ds(sc[0] * count, count)
    pairs = [(es_far, es), (pjs_far, pjs), (bes_far, bes), (bps_far, bps), (bel_far, bel), (bpl_far, bpl)]
    pairs += [(xs_far, xs), (xl_far.at[own], xl), (el_far, el), (pjl_far, pjl)]
    pairs += zip(quarter_of(ORDER[0], w1v.shape[1], w1, w2), (w1v, w2v))
    base = y.shape[0] - 2 * half * count
    for i in range(count):
        at = pl.multiple_of(base + 2 * half * i + sc[0] * half, 16)
        pairs.append((yl_far.at[sc[0] * count + i], y.at[pl.ds(at, half)]))
    copies = start_all(pairs, sems)
    wait_all(copies[:6])
    fill(es_p, es)
    fill(pjs_p, pjs)
    fill_column(bes_c, bes)
    fill_column(bps_c, bps)
    fill_column(bel_c, bel)
    fill_column(bpl_c, bpl)
    wait_all(copies[6:])


def prepare(sc, xs, xl, ys, yl, token_s, token_l, w1, w2):
    small, images, part = xs.shape
    count, large, width = images // 2, xl.shape[1], 2 * part
    es, bes, pjs, bps = token_s
    el, bel, pjl, bpl = token_l
    hidden = es.shape[1]
    pad_s, pad_l = round_up(small, 16), round_up(large, 16)
    quarter = w1.shape[1] // PLANES
    far = [xs, xl, yl, w1, w2, el, pjl, es, pjs, bes, bps, bel, bpl]
    return call(
        prepare_kernel, sc, [], [Far(a) for a in far],
        [
            (xs.shape, BF),
            ((count, large, part), BF),
            ((count * (pad_s + pad_l), width), BF),
            ((width, quarter), BF),
            ((quarter, width), BF),
            (el.shape, BF),
            (pjl.shape, BF),
            ((pad_s, hidden), BF),
            ((pad_s, hidden), BF),
            *[((rows, 1), F32) for rows in (hidden, pad_s, hidden, pad_l)],
        ],
        "prepare", 6, cost=3 * GFLOP, scratch=
        [pltpu.VMEM(es.shape, BF), pltpu.VMEM(pjs.shape, BF)]
        + [pltpu.VMEM(a.shape, F32) for a in (bes, bps, bel, bpl)]
        + [pltpu.SemaphoreType.DMA((12 + count,))],
    )


def front_kernel(
    n_deps, sc, xs, xs_in, xl, xl_in, gain_own, gain_in, shift_own, shift_in,
    el, pjl, es, pjs, bes, bps, bel, bpl, gain2, shift2,
    n2, x1_far, as_far, ds_far, al_far, dl_far,
    xs_f, xs_in_f, x_s, x_l, tk, x1, as_, ds_, al, dl, sems,
):
    count = xl.shape[0]
    xs_f[...] = xs[...].astype(F32)
    xs_in_f[...] = xs_in[...].astype(F32)
    load_token_params(sc, (gain_own, gain_in, shift_own, shift_in), tk)
    gain, shift = tk[0:1, :], tk[1:2, :]
    after_gain, after_shift = gain2[...][None], shift2[...][None]
    copies = []

    def group(x_ref, e, be, pj, bp, index, at, a_ref, d_ref, a_far, d_far):
        rows = x_ref.shape[0]
        hat, _ = norm(x_ref[...])
        normed = (hat * gain + shift).astype(BF)
        active, slope = gelu_pair(dot(e[...], normed, TN) + be[...])
        active = active.astype(BF)
        a_ref[index] = active
        d_ref[index] = slope
        copies.extend(
            start_all([(a_ref.at[index], a_far.at[index]), (d_ref.at[index], d_far.at[index])], sems, len(copies))
        )
        middle = (x_ref[...] + (dot(pj[...], active, NN) + bp[...])).astype(BF)
        here = slice(at, at + rows)
        x1[here, :] = middle
        copies.extend(start_all([(x1.at[here], x1_far.at[here])], sems, len(copies)))
        hat2, _ = norm(middle.astype(F32))
        n2[here, :] = (hat2 * after_gain + after_shift).astype(BF)

    pad_s, pad_l = x_s.shape[1], x_l.shape[1]
    for i in range(count):
        image = sc[0] * count + i
        load_image(sc, xl.at[i], xl_in.at[image], x_l.at[i])
        load_image(sc, xs_f.at[:, image], xs_in_f.at[:, image], x_s.at[i])
        group(x_l.at[i], el, bel, pjl, bpl, i, count * pad_s + i * pad_l, al, dl, al_far, dl_far)
        group(x_s.at[i], es, bes, pjs, bps, i, i * pad_s, as_, ds_, as_far, ds_far)
    wait_all(copies)


def front(sc, xs, xs_in, xl, xl_in, tok, weights, gain2, shift2):
    images, part = xs.shape[1:]
    count, width = images // 2, 2 * part
    pad_l, hidden = weights[0].shape
    pad_s = weights[2].shape[0]
    rows = count * (pad_s + pad_l)
    state = (count, hidden, width)
    return call(
        front_kernel, sc, [], [xs, xs_in, xl, xl_in, *tok, *weights, gain2, shift2],
        [((rows, width), BF), ((rows, width), BF, None)] + [(state, BF, None), (state, F32, None)] * 2,
        "front", 22, cost=8 * GFLOP, scratch=
        [
            *[pltpu.VMEM(xs.shape, F32)] * 2,
            pltpu.VMEM((count, pad_s, width), F32),
            pltpu.VMEM((count, pad_l, width), F32),
            pltpu.VMEM((2, width), F32),
            pltpu.VMEM((rows, width), BF),
            *[pltpu.VMEM(state, BF), pltpu.VMEM(state, F32)] * 2,
            pltpu.SemaphoreType.DMA((6 * count,)),
        ],
    )


def rows_kernel(n_deps, sc, *refs):
    ys, ys_in, yl_in, _, y, ys_f, ys_in_f, hold, sems = refs[n_deps:]
    first = sc[0] == 0
    half, images, width = ys.shape
    count = images // 2
    pad_s, half_l = hold.shape[0], yl_in.shape[1]
    pairs = []
    for i in range(count):
        at = pl.multiple_of(count * pad_s + 2 * half_l * i + (1 - sc[0]) * half_l, 16)
        pairs.append((yl_in.at[sc[0] * count + i], y.at[pl.ds(at, half_l)]))
    copies = start_all(pairs, sems)
    ys_f[...] = ys[...].astype(F32)
    ys_in_f[...] = ys_in[...].astype(F32)
    hold[2 * half :, :] = jnp.zeros((pad_s - 2 * half, width), F32)
    for i in range(count):
        image = sc[0] * count + i
        mine, theirs = ys_f[:, image, :], ys_in_f[:, image, :]
        hold[0:half, :] = jnp.where(first, mine, theirs)
        hold[half : 2 * half, :] = jnp.where(first, theirs, mine)
        y[i * pad_s : (i + 1) * pad_s, :] = hold[...].astype(BF)
    wait_all(copies)


def cotangent_rows(sc, deps, ys, ys_in, yl_in, y):
    hs, images, width = ys.shape
    count = images // 2
    pad_s = round_up(2 * hs, 16)
    return call(
        rows_kernel, sc, deps, [ys, ys_in, yl_in, y], [(y.shape, BF)], "rows", 8, cost=3 * GFLOP, scratch=
        [*[pltpu.VMEM(ys.shape, F32)] * 2, pltpu.VMEM((pad_s, width), F32), pltpu.SemaphoreType.DMA((count,))],
        aliases={3: 0},
    )[0]


def channel_kernel(following, is_first, n_deps, sc, *refs):
    is_last = following is None
    refs = list(refs[n_deps:])
    n2, y, w1, b1, w2 = [refs.pop(0) for _ in range(5)]
    if not is_first:
        del refs[:1]
    if is_last:
        x1_far, gain2 = refs.pop(0), refs.pop(0)
    else:
        w1_far, w2_far = refs.pop(0), refs.pop(0)
    send, keep, gb1, dn, acts = [refs.pop(0) for _ in range(5)]
    if is_last:
        dx1, g2 = refs.pop(0), refs.pop(0)
    else:
        w1_next, w2_next = refs.pop(0), refs.pop(0)
    if is_first:
        gy = refs.pop(0)
        gy[...] = dot(jnp.ones((8, y.shape[0]), BF), y[...], NN)[0:1, :]
    grads, sems = refs.pop(0), refs.pop(0)
    rows, width = n2.shape
    hidden = acts.shape[1]
    tile = rows // 2
    if is_last:
        x1 = refs.pop(0)
        copies = start_all([(x1_far, x1)], sems)
    else:
        copies = start_all(zip(quarter_of(following, hidden, w1_far, w2_far), (w1_next, w2_next)), sems)
    bias_grad = jnp.zeros((1, hidden), F32)
    for step in range(2):
        here = pl.ds(step * tile, tile)
        active, slope = gelu_pair(dot(n2[here, :], w1[...], NN) + b1[...])
        grad = dot(y[here, :], w2[...], NT) * slope
        bias_grad = bias_grad + jnp.sum(grad, 0, keepdims=True)
        acts[here, :] = active.astype(BF)
        grads[here, :] = grad.astype(BF)
    gb1[...] = bias_grad
    for step in range(2):
        here = pl.ds(step * tile, tile)
        back = dot(grads[here, :], w1[...], NT)
        if is_first:
            dn[here, :] = back
        else:
            dn[here, :] += back
    if is_last:
        wait_all(copies)
        copies = []
        gain = gain2[...][None]
        gain_sum = jnp.zeros((1, width), F32)
        shift_sum = jnp.zeros((1, width), F32)
        for low in range(0, rows, tile):
            here = slice(low, low + tile)
            hat, scale = norm(x1[here, :].astype(F32))
            back = dn[here, :]
            gain_sum = gain_sum + jnp.sum(back * hat, 0, keepdims=True)
            shift_sum = shift_sum + jnp.sum(back, 0, keepdims=True)
            scaled = back * gain
            mean = jnp.sum(scaled, -1, keepdims=True) * (1.0 / width)
            along = jnp.sum(scaled * hat, -1, keepdims=True) * (1.0 / width)
            dx1[here, :] = (
                y[here, :].astype(F32) + scale * (scaled - mean - hat * along)
            ).astype(BF)
        g2[0:1, :] = gain_sum
        g2[1:2, :] = shift_sum
    weight_grads(sc, n2, y, acts, grads, send, keep)
    wait_all(copies)


def weight_grads(sc, n2, y, acts, grads, send, keep):
    width, hidden = n2.shape[1], acts.shape[1]
    first = sc[0] == 0
    quarter = width // 32
    cut = PLANES * quarter
    expand = dot(n2[...], grads[...], TN).reshape(PLANES, 4, 2, quarter, hidden)
    for c in range(4):
        low = expand[:, c, 0].reshape(cut, hidden)
        high = expand[:, c, 1].reshape(cut, hidden)
        keep[c, 0:cut, :] = jnp.where(first, low, high).astype(BF)
        send[c, 0:cut, :] = jnp.where(first, high, low).astype(BF)
    project = dot(acts[...], y[...], TN).reshape(4, 2, hidden // 8, width)
    for c in range(4):
        low, high = project[c, 0], project[c, 1]
        keep[c, cut:, :] = jnp.where(first, low, high).astype(BF)
        send[c, cut:, :] = jnp.where(first, high, low).astype(BF)


def channel(sc, deps, plane, following, rows_in, w1, b1, w2, carried, ending):
    is_first, is_last = not carried, following is None
    rows, width = rows_in[0].shape
    hidden = w1.shape[1]
    block = (4, width // 8 + hidden // 8, width)
    outs = [(block, BF)] * 2 + [((1, hidden), F32), ((rows, width), F32), ((rows, hidden), BF)]
    scratch = [pltpu.VMEM((rows, hidden), BF), pltpu.SemaphoreType.DMA((2,))]
    if is_last:
        outs += [((rows, width), BF), ((2, width), F32)]
        scratch.append(pltpu.VMEM((rows, width), BF))
    else:
        outs += [(w1.shape, BF), (w2.shape, BF)]
    if is_first:
        outs.append(((1, width), F32))
    here = lax.slice_in_dim(b1, plane * hidden, (plane + 1) * hidden)
    return call(
        functools.partial(channel_kernel, following, is_first), sc, deps,
        [*rows_in, w1, here[None], w2, *carried, *ending], outs, "channel", 18 if is_last else 16, scratch,
        None if is_first else {5: 3},
        13 * GFLOP,
    )


def output_kernel(first, n_in, image, pad_s, n_deps, sc, *refs):
    acts, w2s, (x1_far, b2) = refs[n_deps : n_deps + 4], refs[n_deps + 4 : n_deps + 8], refs[n_deps + 8 : n_deps + 10]
    send, tick, *rest = refs[n_deps + n_in :]
    x1, hold, sems = rest[-3:]
    size = x1.shape[0]
    copies = start_all([(x1_far.at[first : first + size], x1)], sems)
    here = slice(first, first + size)
    parts = [dot(a[here, :], w[...], NN) for a, w in zip(acts, w2s)]
    total = (parts[0] + parts[1]) + (parts[2] + parts[3])
    wait_all(copies)
    hold[...] = x1[...].astype(F32) + total + b2[...][None]
    mine = sc[0] == 0
    tick[...] = jnp.zeros_like(tick)
    if image is None:
        keep = rest[0]
        count, half = keep.shape[:2]
        for i in range(count):
            low = hold[i * pad_s : i * pad_s + half, :]
            high = hold[i * pad_s + half : i * pad_s + 2 * half, :]
            keep[i] = jnp.where(mine, low, high).astype(BF)
            send[i, 0:half, :] = jnp.where(mine, high, low).astype(BF)
    else:
        full, keep = rest[0], rest[1]
        half = keep.shape[0]
        low, high = hold[0:half, :], hold[half : 2 * half, :]
        keep[...] = jnp.where(mine, low, high).astype(BF)
        copies = start_all([(keep, full.at[sc[0] * send.shape[0] + image])], sems)
        send[image, send.shape[1] - half :, :] = jnp.where(mine, high, low).astype(BF)
        wait_all(copies)


def output(sc, deps, acts, w2s, x1, b2, image, halves, send, full):
    count, half_s, half_l = halves
    width = w2s[0].shape[1]
    pad_s = round_up(2 * half_s, 16)
    first = 0 if image is None else count * pad_s + 2 * half_l * image
    size = count * pad_s if image is None else 2 * half_l
    inputs = [*acts, *w2s, Far(x1), b2]
    outs = [((count, round_up(half_s, 16) + half_l, width), BF), ((8, 128), F32)]
    aliases = {}
    if send is not None:
        aliases[len(inputs)] = 0
        inputs.append(send)
    scratch = []
    if image is None:
        outs.append(((count, half_s, width), BF))
    else:
        outs.append(((2 * count, half_l, width), BF, None))
        if full is not None:
            aliases[len(inputs)] = 2
            inputs.append(Far(full))
        scratch.append(pltpu.VMEM((half_l, width), BF))
    scratch += [pltpu.VMEM((size, width), BF), pltpu.VMEM((size, width), F32), pltpu.SemaphoreType.DMA((1,))]
    return call(
        functools.partial(output_kernel, first, len(inputs), image, pad_s), sc, deps, inputs, outs,
        "output", 14, scratch, aliases,
    )


def back_kernel(n_deps, sc, *refs):
    (
        dx1, xs_far, xs_in_far, xl_far, xl_in_far, gain_own, gain_in, shift_own, shift_in, as_far, ds_far, al_far, dl_far,
        es, pjs, el, pjl, g2, gy, b1a, b1b, b1c, b1d,
        gis_keep, gi_send, gil, w_keep, w_send,
        vec, x_s, x_l, tk, es_p, pjs_p, gps, ges, gpl, gel, gi_s, gi_l, gil_keep,
        xs_f, xs_in_f, xs, xs_in, xl, xl_in, as_, ds_, al, dl, sems,
    ) = refs[n_deps:]
    count = as_.shape[0]
    loads = []
    small_loads = start_all([(xs_far, xs), (xs_in_far, xs_in)], sems)
    for i in range(count):
        pairs = [
            (far.at[sc[0] * count + i], ref.at[i])
            for far, ref in ((xl_far, xl), (xl_in_far, xl_in))
        ]
        pairs += [(far.at[i], ref.at[i]) for far, ref in ((ds_far, ds_), (as_far, as_), (dl_far, dl), (al_far, al))]
        loads.append(start_all(pairs, sems, 2 + 6 * i))
    load_token_params(sc, (gain_own, gain_in, shift_own, shift_in), tk)
    fill(es_p, es)
    fill(pjs_p, pjs)
    vec[...] = jnp.zeros_like(vec)
    gain, shift = tk[0:1, :], tk[1:2, :]

    def group(x_ref, index, at, a, d, e, pj, gp, ge, be_at, bp_row, gi, keep, send_at):
        rows, width = x_ref.shape
        hidden = a.shape[1]
        dx = dx1[at : at + rows, :]
        hat, scale = norm(x_ref[...])
        normed = (hat * gain + shift).astype(BF)
        before = (dot(pj[...], dx, TN) * d[index]).astype(BF)
        grad = dot(e[...], before, NN)
        project_grad = dot(dx, a[index], NT)
        expand_grad = dot(normed, before, NT)
        if index == 0:
            gp[0:rows, :] = project_grad
            ge[0:rows, :] = expand_grad
        else:
            gp[0:rows, :] += project_grad
            ge[0:rows, :] += expand_grad
        ones = jnp.ones((8, width), BF)
        vec[bp_row : bp_row + 1, 0:rows] += dot(ones, dx, NT)[0:1, :]
        vec[9:10, be_at : be_at + hidden] += dot(ones, before, NT)[0:1, :]
        vec[0:1, :] += jnp.sum(grad * hat, 0, keepdims=True)
        vec[1:2, :] += jnp.sum(grad, 0, keepdims=True)
        scaled = grad * gain
        mean = jnp.sum(scaled, -1, keepdims=True) * (1.0 / width)
        along = jnp.sum(scaled * hat, -1, keepdims=True) * (1.0 / width)
        gi[...] = dx.astype(F32) + scale * (scaled - mean - hat * along)
        part = width // 2
        size = keep.shape[1]
        keep[index] = gi[0:size, pl.ds(pl.multiple_of(sc[0] * part, 128), part)].astype(BF)
        theirs = gi[0:size, pl.ds(pl.multiple_of((1 - sc[0]) * part, 128), part)]
        gi_send[index, send_at : send_at + size, :] = theirs.astype(BF)

    hidden = as_.shape[1]
    pad_s, pad_l = x_s.shape[1], x_l.shape[1]
    wait_all(small_loads)
    xs_f[...] = xs[...].astype(F32)
    xs_in_f[...] = xs_in[...].astype(F32)
    for i in range(count):
        wait_all(loads[i])
        image = sc[0] * count + i
        load_image(sc, xs_f.at[:, image], xs_in_f.at[:, image], x_s.at[i])
        load_image(sc, xl.at[i], xl_in.at[i], x_l.at[i])
        group(x_s.at[i], i, i * pad_s, as_, ds_, es_p, pjs_p, gps, ges, 0, 10, gi_s, gis_keep, 0)
        group(
            x_l.at[i], i, count * pad_s + i * pad_l, al, dl, el, pjl, gpl, gel, hidden, 11,
            gi_l, gil_keep, pad_s,
        )
    copies = start_all([(gil_keep, gil.at[pl.ds(sc[0] * count, count)])], sems)
    vec[2:4, :] = g2[...]
    vec[4:5, :] = gy[...]
    for i, ref in enumerate((b1a, b1b, b1c, b1d)):
        vec[5 + i : 6 + i, :] = ref[...]
    size = w_keep.shape[2]
    half_s, half_l = gps.shape[0] // 2, gpl.shape[0] // 2
    for ref in (gps, ges):
        ref[pad_s:, :] = jnp.zeros((ref.shape[0] - pad_s, hidden), F32)
    for side, ref in ((sc[0], w_keep), (1 - sc[0], w_send)):
        for t, (small, large) in enumerate(((gps, gpl), (ges, gel))):
            at = pl.multiple_of(side * half_s, 8)
            ref[0, t] = small[pl.ds(at, size), :].astype(BF)
            for c in range(1, 4):
                have = min(size, half_l - (c - 1) * size)
                at = pl.multiple_of(side * half_l + (c - 1) * size, 8)
                ref[c, t, 0:have, :] = large[pl.ds(at, have), :].astype(BF)
                if have < size:
                    ref[c, t, have:, :] = jnp.zeros((size - have, hidden), BF)
        at = pl.multiple_of(side * hidden, 128)
        ref[3, 0, have : have + VEC, :] = vec[:, pl.ds(at, hidden)].astype(BF)
    wait_all(copies)


def piece_rows(pad_s, pad_l):
    return max(round_up(pad_s // 2, 16), round_up(-(-(pad_l // 2 + VEC) // 3), 16))


def back(sc, deps, dx1, xs, xs_in, xl, xl_in, tok, saved, weights, vectors):
    small, images, part = xs.shape
    count, large, width = images // 2, xl.shape[1], 2 * part
    pad_s, pad_l = round_up(small, 16), round_up(large, 16)
    hidden = saved[0].shape[1]
    size = piece_rows(pad_s, pad_l)
    return call(
        back_kernel, sc, deps,
        [dx1, Far(xs), Far(xs_in), Far(xl), Far(xl_in), *tok, *[Far(a) for a in saved], *weights, *vectors],
        [
            ((count, small, part), BF),
            ((count, pad_s + large, part), BF),
            ((images, large, part), BF, None),
            ((4, 2, size, hidden), BF),
            ((4, 2, size, hidden), BF),
        ],
        "back", 30, cost=12 * GFLOP, scratch=
        [
            pltpu.VMEM((VEC, width), F32),
            pltpu.VMEM((count, pad_s, width), F32),
            pltpu.VMEM((count, pad_l, width), F32),
            pltpu.VMEM((2, width), F32),
            pltpu.VMEM((pad_s, hidden), BF),
            pltpu.VMEM((pad_s, hidden), BF),
            pltpu.VMEM((2 * size, hidden), F32),
            pltpu.VMEM((2 * size, hidden), F32),
            pltpu.VMEM((pad_l, hidden), F32),
            pltpu.VMEM((pad_l, hidden), F32),
            pltpu.VMEM((pad_s, width), F32),
            pltpu.VMEM((pad_l, width), F32),
            pltpu.VMEM((count, large, part), BF),
            *[pltpu.VMEM(xs.shape, F32)] * 2,
            *[pltpu.VMEM(xs.shape, BF)] * 2,
            *[pltpu.VMEM((count, large, part), BF)] * 2,
            *[pltpu.VMEM((count, hidden, width), BF), pltpu.VMEM((count, hidden, width), F32)] * 2,
            pltpu.SemaphoreType.DMA((2 + 6 * count,)),
        ],
    )


def total4(parts):
    a, b, c, d = [p.astype(F32) for p in parts]
    return (a + b) + (c + d)


def pair_kernel(n_deps, sc, *refs):
    keep, recv = refs[n_deps : n_deps + 2]
    for k, ref in enumerate(refs[-4:]):
        ref[...] = (keep[sc[1] ^ k].astype(F32) + recv[sc[1] ^ k].astype(F32)).astype(BF)


def pair_sum(sc, deps, keep, recv, passenger=None):
    outs = [(keep.shape[1:], BF)] * 4
    if passenger is None:
        return call(pair_kernel, sc, deps, [keep, recv], outs, "pair_sum", 4)
    passed, *sums = call(
        pair_kernel, sc, deps, [keep, recv, passenger], [(passenger.shape, BF)] + outs, "pair_sum", 4,
        aliases={2: 0},
    )
    return sums, passed


def sides_kernel(n_deps, sc, *refs):
    parts, outs = refs[n_deps : n_deps + 4], refs[-4:]
    rows = parts[0].shape[1]
    half = parts[0].shape[2] // 2
    x, y = sc[1] % 2, sc[1] // 2
    for side in range(2):
        cols = slice(side * half, (side + 1) * half)
        for stays, ref in ((True, outs[2 * side]), (False, outs[2 * side + 1])):
            for k in range(2):
                if side == 0:
                    chip = 2 * (y ^ k) + (x if stays else 1 - x)
                else:
                    chip = 2 * (y if stays else 1 - y) + (x ^ k)
                for i in range(2):
                    keep, recv = parts[2 * i : 2 * i + 2]
                    total = keep[chip, :, cols].astype(F32) + recv[chip, :, cols].astype(F32)
                    ref[k, i * rows : (i + 1) * rows, :] = total.astype(BF)


def sides_sum(sc, deps, parts):
    chips, rows, width = parts[0].shape
    return call(sides_kernel, sc, deps, parts, [((2, 2 * rows, width // 2), BF)] * 4, "sides_sum", 6)


def second_kernel(n_deps, sc, *refs):
    refs = refs[n_deps:]
    for side in range(2):
        keep, recv = refs[2 * side : 2 * side + 2]
        for k in range(2):
            refs[4 + 2 * side + k][...] = (keep[k].astype(F32) + recv[k].astype(F32)).astype(BF)


def second_sum(sc, deps, parts):
    return call(second_kernel, sc, deps, parts, [(parts[0].shape[1:], BF)] * 4, "second_sum", 4)


def quad_kernel(n_parts, n_deps, sc, *refs):
    parts, (keep, send, hold, rest) = refs[n_deps : n_deps + n_parts], refs[-4:]
    rows = keep.shape[0] // 2
    quarter = rows // PLANES
    for i in range(2):
        if len(parts) == 4:
            here = slice(2 * rows * i, 2 * rows * (i + 1))
            sums = [parts[j][here, :].astype(F32) + parts[j + 1][here, :].astype(F32) for j in (0, 2)]
            total = jnp.concatenate(sums, 1)
        else:
            total = total4([r[...] for r in parts[4 * i : 4 * i + 4]])
        hold[i] = total[0:rows].reshape(hold.shape[1:])
        rest[i] = total[rows:]
    high, low = sc[2] // 2, sc[2] % 2
    for side, ref in ((high, keep), (1 - high, send)):
        for k in range(2):
            pair = [hold[i, 2 * side + (low ^ k)] for i in range(2)]
            ref[2 * k * quarter : 2 * (k + 1) * quarter, :] = jnp.concatenate(pair, 0).astype(BF)
        ref[rows:, :] = rest[side].astype(BF)


def quad_sum(sc, deps, parts, passengers=()):
    rows, width = parts[0].shape
    if len(parts) == 4:
        rows, width = rows // 2, 2 * width
    quarter = rows // 2 // PLANES
    passed = [(a.shape, a.dtype) for a in passengers]
    *passed, keep, send = call(
        functools.partial(quad_kernel, len(parts)), sc, deps, [*parts, *passengers],
        passed + [((rows, width), BF)] * 2, "quad_sum", 6,
        [pltpu.VMEM((2, PLANES, quarter, width), F32), pltpu.VMEM((2, rows // 2, width), F32)],
        {len(parts) + i: i for i in range(len(passed))},
    )
    return keep, send, passed


def planes_kernel(n_deps, sc, *refs):
    a, b = refs[n_deps : n_deps + 2]
    keep, send = refs[-2:]
    rows = a.shape[0]
    cut = rows // 4
    total = a[...].astype(F32) + b[...].astype(F32)
    keep[0:cut, :] = total[0:cut].astype(BF)
    send[0:cut, :] = total[cut : 2 * cut].astype(BF)
    rest = total[2 * cut :].astype(BF)
    keep[cut:, :] = rest
    send[cut:, :] = rest


def planes_sum(sc, deps, keep, recv, passengers=()):
    rows, width = keep.shape
    passed = [(a.shape, a.dtype) for a in passengers]
    *passed, keep, send = call(
        planes_kernel, sc, deps, [keep, recv, *passengers], passed + [((3 * rows // 4, width), BF)] * 2,
        "planes_sum", 4, aliases={2 + i: i for i in range(len(passed))},
    )
    return keep, send, passed


def last_kernel(groups, n_deps, sc, *refs):
    refs = refs[n_deps:]
    expand_out, project_out, expand, project, sems = refs[-5:]
    width = expand.shape[1] // PLANES
    quarter = expand.shape[0]
    for g, planes in enumerate(groups):
        total = refs[2 * g][...].astype(F32) + refs[2 * g + 1][...].astype(F32)
        for i, plane in enumerate(planes):
            expand[:, plane * width : (plane + 1) * width] = total[i * quarter : (i + 1) * quarter]

        @pl.when((sc[2] == planes[0]) | (sc[2] == planes[1]))
        def _():
            project[...] = total[2 * quarter :]

    wait_all(start_all([(expand, expand_out), (project, project_out)], sems))


def last_sum(sc, groups, pieces):
    flat = [a for group in groups for a in pieces[group]]
    rows, width = flat[0].shape
    shapes = [(rows // 6, PLANES * width), (2 * rows // 3, width)]
    return call(
        functools.partial(last_kernel, groups), sc, [], flat, [(s, F32, None) for s in shapes], "last_sum", 4,
        [pltpu.VMEM(s, F32) for s in shapes] + [pltpu.SemaphoreType.DMA((2,))],
    )


def piece_at(rows):
    size = round_up(-(-rows // 2), 16)
    return rows - size, size


def split_kernel(n_deps, sc, *refs):
    parts, outs, hold = refs[n_deps : n_deps + 4], refs[-5:-1], refs[-1]
    hold[...] = total4([r[...] for r in parts])
    second, size = piece_at(hold.shape[1])
    for k, ref in enumerate(outs):
        piece = sc[2] ^ k
        at = pl.multiple_of((piece % 2) * second, 16)
        ref[...] = hold[piece // 2, pl.ds(at, size), :].astype(BF)


def token_split(sc, deps, parts, passenger):
    size = piece_at(parts[0].shape[1])[1]
    return call(
        split_kernel, sc, deps, [*parts, passenger],
        [(passenger.shape, passenger.dtype)] + [((size, parts[0].shape[2]), BF)] * 4, "token_split", 4,
        [pltpu.VMEM(parts[0].shape, F32)], {4: 0},
    )


def token_sum_kernel(n_deps, sc, *refs):
    refs[-1][...] = total4([r[...] for r in refs[n_deps : n_deps + 4]]).astype(BF)


def token_sum(sc, deps, parts, passenger):
    outs = [(passenger.shape, passenger.dtype), (parts[0].shape, BF)]
    return call(token_sum_kernel, sc, deps, [*parts, passenger], outs, "token_sum", 4, aliases={4: 0})


def join_kernel(n_deps, sc, *refs):
    parts, w, hold = refs[n_deps : n_deps + 4], refs[-2], refs[-1]
    for k, ref in enumerate(parts):
        hold[sc[2] ^ k] = ref[...]
    second, size = piece_at(w.shape[1])
    for piece in range(PLANES):
        at = (piece % 2) * second
        w[piece // 2, at : at + size, :] = hold[piece]


def token_join(sc, deps, parts, rows):
    size, hidden = parts[0].shape
    return call(
        join_kernel, sc, deps, parts, [((2, rows, hidden), BF)], "token_join", 4,
        [pltpu.VMEM((PLANES, size, hidden), BF)],
    )[0]


def unpack_kernel(n_deps, sc, *refs):
    refs = refs[n_deps:]
    mine, theirs = refs[0:4], refs[4:8]
    ges, gps, gel, gpl = refs[8:12]
    vectors = refs[12:22]
    hold, vec = refs[22:]
    for k in range(4):
        hold[sc[0], sc[1] ^ k] = mine[k][...]
        hold[1 - sc[0], sc[1] ^ k] = theirs[k][...]
    size, hidden = mine[0].shape[1:]
    small, large = ges.shape[0], gel.shape[0]
    for side in range(2):
        low = side * size
        have = min(size, small - low)
        for t, ref in enumerate((gps, ges)):
            ref[low : low + have, :] = hold[side, 0, t].astype(F32)[0:have, :]
        for c in range(1, 4):
            low = side * (large // 2) + (c - 1) * size
            have = min(size, large // 2 - (c - 1) * size)
            for t, ref in enumerate((gpl, gel)):
                ref[low : low + have, :] = hold[side, c, t].astype(F32)[0:have, :]
        vec[:, side * hidden : (side + 1) * hidden] = hold[side, 3, 0].astype(F32)[have : have + VEC, :]
    width = vec.shape[1]
    picks = [(0, 0), (1, 0), (9, 0), (10, 0), (9, hidden), (11, 0), (2, 0), (3, 0), None, (4, 0)]
    for ref, pick in zip(vectors, picks):
        if pick is None:
            for i in range(ref.shape[0] // width):
                ref[i * width : (i + 1) * width] = vec[5 + i, :]
        else:
            row, at = pick
            ref[...] = vec[row, at : at + ref.shape[0]]


def unpack(sc, deps, mine, theirs, small, large, width, channel_hidden):
    hidden = mine[0].shape[2]
    outs = [(small, hidden)] * 2 + [(large, hidden)] * 2
    outs += [(n,) for n in (width, width, hidden, small, hidden, large, width, width, channel_hidden, width)]
    return pl.pallas_call(
        functools.partial(unpack_kernel, len(deps)),
        in_specs=[pl.BlockSpec(memory_space=pltpu.SMEM)]
        + [pl.BlockSpec(memory_space=pltpu.VMEM)] * (len(deps) + 8),
        out_shape=[jax.ShapeDtypeStruct(s, F32) for s in outs],
        scratch_shapes=[pltpu.VMEM((2, 4) + mine[0].shape, BF), pltpu.VMEM((VEC, width), F32)],
        compiler_params=pltpu.CompilerParams(vmem_limit_bytes=12 * MB),
        cost_estimate=pl.CostEstimate(flops=0, bytes_accessed=0, transcendentals=0),
        name="unpack",
    )(sc, *deps, *mine, *theirs)


def place_kernel(n_deps, sc, *refs):
    refs = refs[n_deps:]
    keeps, received = refs[0:2], refs[2:4]
    tick, far_small, far_large, near, sems = refs[6], refs[7:9], refs[9:11], refs[11:13], refs[13]
    count = keeps[0].shape[0]
    pairs = []
    for theirs, far in zip(received, far_large):
        at = theirs.shape[1] - far.shape[1]
        for i in range(count):
            pairs.append((theirs.at[i, at:, :], far.at[(1 - sc[0]) * count + i]))
    copies = start_all(pairs, sems)
    for mine, theirs, ref in zip(keeps, received, near):
        size = mine.shape[1]
        for j in range(2 * count):
            k = j % count
            other = theirs[k, 0:size, :].astype(F32)
            ref[:, j, :] = jnp.where(sc[0] == j // count, mine[k].astype(F32), other).astype(BF)
    copies += start_all(zip(near, far_small), sems, len(copies))
    tick[...] = jnp.zeros_like(tick)
    wait_all(copies)


def place(sc, deps, keeps, received, filled):
    shapes = [(a.shape[1], 2 * a.shape[0], a.shape[2]) for a in keeps]
    count = keeps[0].shape[0]
    return call(
        place_kernel, sc, deps, keeps + received + [Far(a) for a in filled],
        [((8, 128), F32)] + [(shape, BF, None) for shape in shapes] + [(a.shape, BF, None) for a in filled],
        "place", 6,
        [pltpu.VMEM(shape, BF) for shape in shapes] + [pltpu.SemaphoreType.DMA((2 * count + 2,))],
        {4: 3, 5: 4},
    )


def swap(values):
    return lax.ppermute(values, "mp", [(0, 1), (1, 0)])


def across(values, mask, pairs):
    return lax.ppermute(values, "dp", [(i, i ^ mask) for i in pairs])


def per_device(
    chips,
    small_images,
    large_images,
    token_gain,
    token_shift,
    small_expand,
    small_expand_bias,
    small_project,
    small_project_bias,
    large_expand,
    large_expand_bias,
    large_project,
    large_project_bias,
    channel_gain,
    channel_shift,
    channel_expand,
    channel_expand_bias,
    channel_project,
    channel_project_bias,
    small_cotangent,
    large_cotangent,
):
    core = lax.axis_index("mp")
    chip = lax.axis_index("dp")
    sc = jnp.stack([core, chip % 4, (chip // 4) % PLANES]).astype(jnp.int32)
    small_images, small_cotangent = small_images.transpose(1, 0, 2), small_cotangent.transpose(1, 0, 2)
    small, images, part = small_images.shape
    large = large_images.shape[1]
    count = images // 2
    width = channel_expand.shape[0]
    everyone = range(chips)
    tuned = chips == 4 * PLANES

    xs_in, xl_in = swap(small_images), swap(large_images)
    tok = [token_gain, swap(token_gain), token_shift, swap(token_shift)]
    ys_in, yl_in = swap(small_cotangent), swap(large_cotangent)
    token_s = [small_expand, small_expand_bias, small_project.T, small_project_bias]
    token_l = [large_expand, large_expand_bias, large_project.T, large_project_bias]
    xs, xl, y, w1, w2, *weights = prepare(
        sc, small_images, large_images, small_cotangent, large_cotangent, token_s, token_l,
        channel_expand, channel_project,
    )
    n2, x1, as_, ds_, al, dl = front(sc, xs, xs_in, xl, xl_in, tok, weights, channel_gain, channel_shift)
    y = cotangent_rows(sc, [n2], small_cotangent, ys_in, yl_in, y)
    carried = []
    sends, keeps, b1_grads, halved, pieces = {}, {}, {}, {}, {}
    groups = (ORDER[:2], ORDER[2:])

    def halve(plane, deps, passenger=None):
        sums = pair_sum(sc, deps, keeps[plane], swap(sends[plane]), None if passenger is None else sends[passenger])
        if passenger is not None:
            sums, sends[passenger] = sums
        own, *others = sums
        halved[plane] = [own] + [across(o, k + 1, everyone) for k, o in enumerate(others)]

    def quarter(group, deps, passenger=None):
        parts = halved[group] if group in halved else halved[group[0]] + halved[group[1]]
        if passenger is None:
            keep, send, _ = quad_sum(sc, deps, parts)
        else:
            keep, send, (sends[passenger],) = quad_sum(sc, deps, parts, [sends[passenger]])
        pieces[group] = [keep, across(send, 8, everyone)]

        def finish(deps, passengers=()):
            keep, send, passed = planes_sum(sc, deps, *pieces[group], passengers)
            pieces[group] = [keep, send]
            return passed

        return finish

    n_last = PLANES - 1
    acts, w2s = [], []
    halves = (count, small // 2, large // 2)

    def rows_out(deps, image, send, full):
        return output(sc, deps, acts, w2s, x1, channel_project_bias, image, halves, send, full)

    for i, plane in enumerate(ORDER):
        is_last = i == n_last
        following = None if is_last else ORDER[i + 1]
        if is_last:
            ending = [Far(x1), channel_gain]
        else:
            ending = [Far(channel_expand), Far(channel_project)]
        deps = []
        if tuned and i >= 2:
            arrived = halved[ORDER[i - 3]][1:] if i >= 3 else []
            halve(ORDER[i - 2], [b1_grads[ORDER[i - 1]]] + arrived, ORDER[2] if is_last else None)
            deps = halved[ORDER[i - 2]][:1]
        w2s.append(w2)
        sends[plane], keeps[plane], b1_grads[plane], dn, active, *carried = channel(
            sc, deps, plane, following, [n2, y], w1, channel_expand_bias, w2, carried, ending
        )
        acts.append(active)
        if i == 0:
            *carried, gy = carried
        if not is_last:
            w1, w2 = carried
            carried = [dn]
    dx1, g2 = carried
    deps = []
    if tuned:
        finish = quarter(groups[0], [b1_grads[ORDER[3]]], ORDER[3])
        keep_a, send_a, keep_b, send_b = sides_sum(
            sc, [pieces[groups[0]][0]],
            [a for plane in groups[1] for a in (keeps[plane], swap(sends[plane]))],
        )
        recv_a, recv_b = across(send_a, 1, everyone), across(send_b, 2, everyone)
        deps = [keep_a]
    gis_keep, gi_send, gil, w_keep, w_send = back(
        sc, deps, dx1, small_images, xs_in, large_images, xl_in, tok,
        [as_, ds_, al, dl],
        [small_expand, small_project.T, large_expand, large_project.T],
        [g2, gy] + [b1_grads[plane] for plane in range(PLANES)],
    )

    if tuned:
        w_send, gi_send = finish([w_keep, recv_a, recv_b], [w_send, gi_send])
        gi_in = swap(gi_send)
        keep_a, send_a, keep_b, send_b = second_sum(
            sc, [pieces[groups[0]][0]], [keep_a, recv_a, keep_b, recv_b]
        )
        halved[groups[1]] = [keep_a, across(send_a, 2, everyone), keep_b, across(send_b, 1, everyone)]
        own, *others = pair_sum(sc, [keep_a, gi_in], w_keep, swap(w_send))
        parts = [own] + [across(o, k + 1, everyone) for k, o in enumerate(others)]
        out_send, tick, outl_full = rows_out([own], 0, None, None)
        finish = quarter(groups[1], [tick])
        out_send, tick, outs_keep = rows_out([pieces[groups[1]][0]], None, out_send, None)
        send, own, *others = token_split(sc, [tick], parts, pieces[groups[0]][1])
        pieces[groups[0]][1] = across(send, 4, everyone)
        parts = [own] + [across(o, 4 * (k + 1), everyone) for k, o in enumerate(others)]
        out_send, tick, outl_full = rows_out([own], 1, out_send, outl_full)
        out_send, w = token_sum(sc, [tick, pieces[groups[0]][1], pieces[groups[1]][1]], parts, out_send)
        out_in = swap(out_send)
        parts = [w] + [across(w, 4 * k, everyone) for k in (1, 2, 3)]
        finish([w])
        pieces[groups[1]][1] = across(pieces[groups[1]][1], 4, everyone)
        tick, small_output, small_input_grad, large_output, large_input_grad = place(
            sc, [pieces[groups[1]][0]], [outs_keep, gis_keep], [out_in, gi_in], [outl_full, gil]
        )
        w = token_join(sc, [tick], parts, w_keep.shape[2])
        mine = [w] + [across(w, k, everyone) for k in (1, 2, 3)]
        extra = []
        expand_part, project_part = last_sum(sc, groups, pieces)
    else:
        out_send, _, outl_full = rows_out([], 0, None, None)
        out_send, _, outl_full = rows_out([], 1, out_send, outl_full)
        out_send, _, outs_keep = rows_out([], None, out_send, None)
        _, small_output, small_input_grad, large_output, large_input_grad = place(
            sc, [], [outs_keep, gis_keep], [swap(out_send), swap(gi_send)], [outl_full, gil]
        )
        extra = []

        def both(keep, send):
            return jnp.where(core == 0, jnp.stack([keep, send]), jnp.stack([send, keep])).astype(F32)

        expand_full, project_full = [], []
        for plane in range(PLANES):
            parts = both(keeps[plane], sends[plane])
            cut = width // 8
            e = parts[:, :, :cut].reshape(2, 4, PLANES, width // 32, -1)
            expand_full.append(e.transpose(2, 1, 0, 3, 4).reshape(width, -1))
            project_full.append(parts[:, :, cut:].transpose(1, 0, 2, 3).reshape(-1, width))
        expand_part = lax.psum_scatter(
            jnp.concatenate(expand_full, 1), ("dp", "mp"), scatter_dimension=0, tiled=True
        )
        project_part = lax.psum_scatter(
            jnp.concatenate(project_full, 0), ("dp", "mp"), scatter_dimension=0, tiled=True
        )
        token = lax.psum(both(w_keep, w_send), ("dp", "mp"))
        token = lax.dynamic_index_in_dim(token, core, 0, False).astype(BF)
        mine = [lax.dynamic_index_in_dim(token, sc[1] ^ k, 0, False) for k in range(4)]
    unpacked = unpack(
        sc, extra, mine, [swap(w) for w in mine], small, large, width, channel_expand.shape[1]
    )
    (ges, gps_t, gel, gpl_t, gtg, gts, gbes, gbps, gbel, gbpl, gcg, gcs, gb1, gb2) = unpacked
    small_output, small_input_grad = small_output.transpose(1, 0, 2), small_input_grad.transpose(1, 0, 2)
    return (
        small_output, large_output, small_input_grad, large_input_grad,
        gtg, gts, ges, gbes, gps_t.T, gbps, gel, gbel, gpl_t.T, gbpl,
        gcg, gcs, expand_part, gb1, project_part, gb2,
    )


def solution(mesh):
    replicated = P()
    by_channel = P("dp", None, "mp")
    by_patch = P("dp", "mp", None)
    by_row = P(("dp", "mp"), None)
    return jax.shard_map(
        functools.partial(per_device, mesh.shape["dp"]),
        mesh=mesh,
        in_specs=(by_channel, by_channel, P("mp"), P("mp")) + (replicated,) * 14 + (by_patch, by_patch),
        out_specs=(by_patch, by_patch, by_channel, by_channel)
        + (replicated,) * 12
        + (by_row, replicated, by_row, replicated),
        check_vma=False,
    )
```

```python
import functools

import jax
import jax.numpy as jnp
from jax import lax
from jax.experimental import pallas as pl
from jax.experimental.pallas import tpu as pltpu
from jax.sharding import PartitionSpec as P

BF = jnp.bfloat16
F32 = jnp.float32
EPS = 1e-06
SQRT_HALF = 0.7071067811865476
INV_SQRT_2PI = 0.3989422804014327
HALF_LOG2E = 0.7213475204444817
NN = ((1,), (0,))
NT = ((1,), (1,))
TN = ((0,), (0,))
MB = 1 << 20
GFLOP = 10**9
PLANES = 4
ORDER = (0, 3, 1, 2)
VEC = 16


def dot(left, right, dims):
    return lax.dot_general(left, right, (dims, ((), ())), preferred_element_type=F32)


def gelu_pair(values):
    cdf = 0.5 * lax.erf(values * SQRT_HALF) + 0.5
    pdf = jnp.exp2((values * values) * (-HALF_LOG2E)) * INV_SQRT_2PI
    return values * cdf, cdf + values * pdf


def norm(values):
    width = values.shape[-1]
    mean = jnp.sum(values, -1, keepdims=True) * (1.0 / width)
    square = jnp.sum(values * values, -1, keepdims=True) * (1.0 / width)
    scale = lax.rsqrt(square - mean * mean + EPS)
    return (values - mean) * scale, scale


def round_up(value, to):
    return (value + to - 1) // to * to


def call(kernel, sc, deps, inputs, outs, name, limit, scratch=(), aliases=None, cost=0):
    anywhere, vmem = pl.BlockSpec(memory_space=pl.ANY), pl.BlockSpec(memory_space=pltpu.VMEM)
    first = 1 + len(deps)
    return pl.pallas_call(
        functools.partial(kernel, len(deps)),
        in_specs=[pl.BlockSpec(memory_space=pltpu.SMEM)]
        + [vmem] * len(deps)
        + [vmem if not isinstance(a, Far) else anywhere for a in inputs],
        out_specs=[anywhere if len(o) == 3 else vmem for o in outs],
        out_shape=[pltpu.HBM(*o[:2]) if len(o) == 3 else pltpu.VMEM(*o) for o in outs],
        scratch_shapes=scratch,
        input_output_aliases={first + a: b for a, b in (aliases or {}).items()},
        compiler_params=pltpu.CompilerParams(vmem_limit_bytes=limit * MB),
        cost_estimate=pl.CostEstimate(flops=cost, bytes_accessed=0, transcendentals=0),
        name=name,
    )(sc, *deps, *[a.array if isinstance(a, Far) else a for a in inputs])


class Far:
    def __init__(self, array):
        self.array = pltpu.with_memory_space_constraint(array, pltpu.HBM)


def start_all(pairs, sems, first=0):
    copies = [pltpu.make_async_copy(a, b, sems.at[first + i]) for i, (a, b) in enumerate(pairs)]
    for copy in copies:
        copy.start()
    return copies


def wait_all(copies):
    for copy in copies:
        copy.wait()


def quarter_of(plane, size, w1, w2):
    here = slice(plane * size, (plane + 1) * size)
    return w1.at[:, here], w2.at[here, :]


def load_image(sc, own, other, dest):
    rows, part = own.shape
    dest[0:rows, pl.ds(pl.multiple_of(sc[0] * part, 128), part)] = own[...].astype(F32)
    dest[0:rows, pl.ds(pl.multiple_of((1 - sc[0]) * part, 128), part)] = other[...].astype(F32)
    if dest.shape[0] != rows:
        dest[rows:, :] = jnp.zeros((dest.shape[0] - rows, dest.shape[1]), F32)


def load_token_params(sc, tok, dest):
    for row in range(2):
        own, other = tok[2 * row : 2 * row + 2]
        part = own.shape[0]
        dest[row : row + 1, pl.ds(pl.multiple_of(sc[0] * part, 128), part)] = own[...][None]
        dest[row : row + 1, pl.ds(pl.multiple_of((1 - sc[0]) * part, 128), part)] = other[...][None]


def fill(dest, source):
    rows = source.shape[0]
    dest[0:rows, :] = source[...]
    if dest.shape[0] != rows:
        dest[rows:, :] = jnp.zeros((dest.shape[0] - rows, dest.shape[1]), dest.dtype)


def fill_column(dest, source):
    size = source.shape[0]
    if dest.shape[0] != size:
        dest[...] = jnp.zeros_like(dest)
    dest[0:size, :] = jnp.broadcast_to(source[...][None], (8, size)).T[:, 0:1]


def pick_kernel(n_deps, sc, *refs):
    count = refs[2].shape[0]
    theirs = pl.ds((1 - sc[0]) * count, count)
    wait_all(start_all([(far.at[theirs], ref) for far, ref in zip(refs[:2], refs[2:4])], refs[4]))


def pick(sc, *arrays):
    return call(
        pick_kernel, sc, [], [Far(a) for a in arrays],
        [((a.shape[0] // 2,) + a.shape[1:], a.dtype) for a in arrays], "pick", 2,
        [pltpu.SemaphoreType.DMA((2,))],
    )


def prepare_kernel(
    n_deps, sc, xs_far, xl_far, yl_far, el_far, pjl_far, es_far, pjs_far, bes_far, bps_far, bel_far, bpl_far,
    xs, xl, y, el, pjl, es_p, pjs_p, bes_c, bps_c, bel_c, bpl_c,
    es, pjs, bes, bps, bel, bpl, sems,
):
    count, half = xl.shape[0], yl_far.shape[1]
    own = pl.ds(sc[0] * count, count)
    pairs = [(es_far, es), (pjs_far, pjs), (bes_far, bes), (bps_far, bps), (bel_far, bel), (bpl_far, bpl)]
    pairs += [(xs_far, xs), (xl_far.at[own], xl), (el_far, el), (pjl_far, pjl)]
    base = y.shape[0] - 2 * half * count
    for i in range(count):
        at = pl.multiple_of(base + 2 * half * i + sc[0] * half, 16)
        pairs.append((yl_far.at[sc[0] * count + i], y.at[pl.ds(at, half)]))
    copies = start_all(pairs, sems)
    wait_all(copies[:6])
    fill(es_p, es)
    fill(pjs_p, pjs)
    fill_column(bes_c, bes)
    fill_column(bps_c, bps)
    fill_column(bel_c, bel)
    fill_column(bpl_c, bpl)
    wait_all(copies[6:])


def prepare(sc, xs, xl, ys, yl, token_s, token_l):
    small, images, part = xs.shape
    count, large, width = images // 2, xl.shape[1], 2 * part
    es, bes, pjs, bps = token_s
    el, bel, pjl, bpl = token_l
    hidden = es.shape[1]
    pad_s, pad_l = round_up(small, 16), round_up(large, 16)
    far = [xs, xl, yl, el, pjl, es, pjs, bes, bps, bel, bpl]
    return call(
        prepare_kernel, sc, [], [Far(a) for a in far],
        [
            (xs.shape, BF),
            ((count, large, part), BF),
            ((count * (pad_s + pad_l), width), BF),
            (el.shape, BF),
            (pjl.shape, BF),
            ((pad_s, hidden), BF),
            ((pad_s, hidden), BF),
            *[((rows, 1), F32) for rows in (hidden, pad_s, hidden, pad_l)],
        ],
        "prepare", 6, cost=3 * GFLOP, scratch=
        [pltpu.VMEM(es.shape, BF), pltpu.VMEM(pjs.shape, BF)]
        + [pltpu.VMEM(a.shape, F32) for a in (bes, bps, bel, bpl)]
        + [pltpu.SemaphoreType.DMA((10 + count,))],
    )


def front_kernel(
    n_deps, sc, xs, xs_in, xl, xl_in, gain_own, gain_in, shift_own, shift_in,
    el, pjl, es, pjs, bes, bps, bel, bpl, gain2, shift2, w1_far, w2_far,
    n2, w1, w2, x1_far, as_far, ds_far, al_far, dl_far,
    xs_f, xs_in_f, x_s, x_l, tk, x1, as_, ds_, al, dl, sems,
):
    count = xl.shape[0]
    copies = start_all(zip(quarter_of(ORDER[0], w1.shape[1], w1_far, w2_far), (w1, w2)), sems)
    xs_f[...] = xs[...].astype(F32)
    xs_in_f[...] = xs_in[...].astype(F32)
    load_token_params(sc, (gain_own, gain_in, shift_own, shift_in), tk)
    gain, shift = tk[0:1, :], tk[1:2, :]
    after_gain, after_shift = gain2[...][None], shift2[...][None]

    def group(x_ref, e, be, pj, bp, index, at, a_ref, d_ref, a_far, d_far):
        rows = x_ref.shape[0]
        hat, _ = norm(x_ref[...])
        normed = (hat * gain + shift).astype(BF)
        active, slope = gelu_pair(dot(e[...], normed, TN) + be[...])
        active = active.astype(BF)
        a_ref[index] = active
        d_ref[index] = slope
        copies.extend(
            start_all([(a_ref.at[index], a_far.at[index]), (d_ref.at[index], d_far.at[index])], sems, len(copies))
        )
        middle = (x_ref[...] + (dot(pj[...], active, NN) + bp[...])).astype(BF)
        here = slice(at, at + rows)
        x1[here, :] = middle
        copies.extend(start_all([(x1.at[here], x1_far.at[here])], sems, len(copies)))
        hat2, _ = norm(middle.astype(F32))
        n2[here, :] = (hat2 * after_gain + after_shift).astype(BF)

    pad_s, pad_l = x_s.shape[1], x_l.shape[1]
    for i in range(count):
        image = sc[0] * count + i
        load_image(sc, xl.at[i], xl_in.at[i], x_l.at[i])
        load_image(sc, xs_f.at[:, image], xs_in_f.at[:, image], x_s.at[i])
        group(x_l.at[i], el, bel, pjl, bpl, i, count * pad_s + i * pad_l, al, dl, al_far, dl_far)
        group(x_s.at[i], es, bes, pjs, bps, i, i * pad_s, as_, ds_, as_far, ds_far)
    wait_all(copies)


def front(sc, xs, xs_in, xl, xl_in, tok, weights, gain2, shift2, w1, w2):
    images, part = xs.shape[1:]
    count, width = images // 2, 2 * part
    pad_l, hidden = weights[0].shape
    pad_s = weights[2].shape[0]
    rows = count * (pad_s + pad_l)
    state = (count, hidden, width)
    quarter = w1.shape[1] // PLANES
    return call(
        front_kernel, sc, [], [xs, xs_in, xl, xl_in, *tok, *weights, gain2, shift2, Far(w1), Far(w2)],
        [((rows, width), BF), ((width, quarter), BF), ((quarter, width), BF), ((rows, width), BF, None)] + [(state, BF, None), (state, F32, None)] * 2,
        "front", 23, cost=8 * GFLOP, scratch=
        [
            *[pltpu.VMEM(xs.shape, F32)] * 2,
            pltpu.VMEM((count, pad_s, width), F32),
            pltpu.VMEM((count, pad_l, width), F32),
            pltpu.VMEM((2, width), F32),
            pltpu.VMEM((rows, width), BF),
            *[pltpu.VMEM(state, BF), pltpu.VMEM(state, F32)] * 2,
            pltpu.SemaphoreType.DMA((2 + 6 * count,)),
        ],
    )


def rows_kernel(n_deps, sc, *refs):
    ys, ys_in, yl_in, _, y, ys_f, ys_in_f, hold, sems = refs[n_deps:]
    first = sc[0] == 0
    half, images, width = ys.shape
    count = images // 2
    pad_s, half_l = hold.shape[0], yl_in.shape[1]
    pairs = []
    for i in range(count):
        at = pl.multiple_of(count * pad_s + 2 * half_l * i + (1 - sc[0]) * half_l, 16)
        pairs.append((yl_in.at[i], y.at[pl.ds(at, half_l)]))
    copies = start_all(pairs, sems)
    ys_f[...] = ys[...].astype(F32)
    ys_in_f[...] = ys_in[...].astype(F32)
    hold[2 * half :, :] = jnp.zeros((pad_s - 2 * half, width), F32)
    for i in range(count):
        image = sc[0] * count + i
        mine, theirs = ys_f[:, image, :], ys_in_f[:, image, :]
        hold[0:half, :] = jnp.where(first, mine, theirs)
        hold[half : 2 * half, :] = jnp.where(first, theirs, mine)
        y[i * pad_s : (i + 1) * pad_s, :] = hold[...].astype(BF)
    wait_all(copies)


def cotangent_rows(sc, deps, ys, ys_in, yl_in, y):
    hs, images, width = ys.shape
    count = images // 2
    pad_s = round_up(2 * hs, 16)
    return call(
        rows_kernel, sc, deps, [ys, ys_in, yl_in, y], [(y.shape, BF)], "rows", 8, cost=3 * GFLOP, scratch=
        [*[pltpu.VMEM(ys.shape, F32)] * 2, pltpu.VMEM((pad_s, width), F32), pltpu.SemaphoreType.DMA((count,))],
        aliases={3: 0},
    )[0]


def channel_kernel(following, is_first, n_deps, sc, *refs):
    is_last = following is None
    refs = list(refs[n_deps:])
    n2, y, w1, b1, w2 = [refs.pop(0) for _ in range(5)]
    if not is_first:
        del refs[:2]
    if is_last:
        x1_far, gain2 = refs.pop(0), refs.pop(0)
    else:
        w1_far, w2_far = refs.pop(0), refs.pop(0)
    send, keep, gb1, dn_low, dn_high, acts = [refs.pop(0) for _ in range(6)]
    dn = (dn_low, dn_high)
    if is_last:
        dx1, g2 = refs.pop(0), refs.pop(0)
    else:
        w1_next, w2_next = refs.pop(0), refs.pop(0)
    if is_first:
        gy = refs.pop(0)
        gy[...] = dot(jnp.ones((8, y.shape[0]), BF), y[...], NN)[0:1, :]
    grads, sems = refs.pop(0), refs.pop(0)
    rows, width = n2.shape
    hidden = acts.shape[1]
    tile = rows // 2
    if is_last:
        x1 = refs.pop(0)
        copies = start_all([(x1_far, x1)], sems)
    else:
        copies = start_all(zip(quarter_of(following, hidden, w1_far, w2_far), (w1_next, w2_next)), sems)
    bias_grad = jnp.zeros((1, hidden), F32)
    for step in range(2):
        here = pl.ds(step * tile, tile)
        active, slope = gelu_pair(dot(n2[here, :], w1[...], NN) + b1[...])
        grad = dot(y[here, :], w2[...], NT) * slope
        bias_grad = bias_grad + jnp.sum(grad, 0, keepdims=True)
        acts[here, :] = active.astype(BF)
        grads[here, :] = grad.astype(BF)
    gb1[...] = bias_grad
    for step in range(2):
        here = pl.ds(step * tile, tile)
        back = dot(grads[here, :], w1[...], NT)
        if is_first:
            dn[step][...] = back
        else:
            dn[step][...] += back
    if is_last:
        wait_all(copies)
        copies = []
        gain = gain2[...][None]
        gain_sum = jnp.zeros((1, width), F32)
        shift_sum = jnp.zeros((1, width), F32)
        for step in range(2):
            here = slice(step * tile, (step + 1) * tile)
            hat, scale = norm(x1[here, :].astype(F32))
            back = dn[step][...]
            gain_sum = gain_sum + jnp.sum(back * hat, 0, keepdims=True)
            shift_sum = shift_sum + jnp.sum(back, 0, keepdims=True)
            scaled = back * gain
            mean = jnp.sum(scaled, -1, keepdims=True) * (1.0 / width)
            along = jnp.sum(scaled * hat, -1, keepdims=True) * (1.0 / width)
            dx1[here, :] = (
                y[here, :].astype(F32) + scale * (scaled - mean - hat * along)
            ).astype(BF)
        g2[0:1, :] = gain_sum
        g2[1:2, :] = shift_sum
    weight_grads(sc, n2, y, acts, grads, send, keep)
    wait_all(copies)


def weight_grads(sc, n2, y, acts, grads, send, keep):
    width, hidden = n2.shape[1], acts.shape[1]
    first = sc[0] == 0
    quarter = width // 32
    cut = PLANES * quarter
    expand = dot(n2[...], grads[...], TN).reshape(PLANES, 4, 2, quarter, hidden)
    for c in range(4):
        low = expand[:, c, 0].reshape(cut, hidden)
        high = expand[:, c, 1].reshape(cut, hidden)
        keep[c, 0:cut, :] = jnp.where(first, low, high).astype(BF)
        send[c, 0:cut, :] = jnp.where(first, high, low).astype(BF)
    project = dot(acts[...], y[...], TN).reshape(4, 2, hidden // 8, width)
    for c in range(4):
        low, high = project[c, 0], project[c, 1]
        keep[c, cut:, :] = jnp.where(first, low, high).astype(BF)
        send[c, cut:, :] = jnp.where(first, high, low).astype(BF)


def channel(sc, deps, plane, following, rows_in, w1, b1, w2, carried, ending):
    is_first, is_last = not carried, following is None
    rows, width = rows_in[0].shape
    hidden = w1.shape[1]
    block = (4, width // 8 + hidden // 8, width)
    outs = [(block, BF)] * 2 + [((1, hidden), F32)] + [((rows // 2, width), F32)] * 2 + [((rows, hidden), BF)]
    scratch = [pltpu.VMEM((rows, hidden), BF), pltpu.SemaphoreType.DMA((2,))]
    if is_last:
        outs += [((rows, width), BF), ((2, width), F32)]
        scratch.append(pltpu.VMEM((rows, width), BF))
    else:
        outs += [(w1.shape, BF), (w2.shape, BF)]
    if is_first:
        outs.append(((1, width), F32))
    here = lax.slice_in_dim(b1, plane * hidden, (plane + 1) * hidden)
    return call(
        functools.partial(channel_kernel, following, is_first), sc, deps,
        [*rows_in, w1, here[None], w2, *carried, *ending], outs, "channel", 17 if is_last else 13, scratch,
        None if is_first else {5: 3, 6: 4},
        13 * GFLOP,
    )


def output_kernel(first, n_in, image, pad_s, n_deps, sc, *refs):
    acts, w2s, (x1_far, b2) = refs[n_deps : n_deps + 4], refs[n_deps + 4 : n_deps + 8], refs[n_deps + 8 : n_deps + 10]
    send, tick, *rest = refs[n_deps + n_in :]
    x1, hold, sems = rest[-3:]
    size = x1.shape[0]
    copies = start_all([(x1_far.at[first : first + size], x1)], sems)
    here = slice(first, first + size)
    parts = [dot(a[here, :], w[...], NN) for a, w in zip(acts, w2s)]
    total = (parts[0] + parts[1]) + (parts[2] + parts[3])
    wait_all(copies)
    hold[...] = x1[...].astype(F32) + total + b2[...][None]
    mine = sc[0] == 0
    tick[...] = jnp.zeros_like(tick)
    if image is None:
        keep = rest[0]
        count, half = keep.shape[:2]
        for i in range(count):
            low = hold[i * pad_s : i * pad_s + half, :]
            high = hold[i * pad_s + half : i * pad_s + 2 * half, :]
            keep[i] = jnp.where(mine, low, high).astype(BF)
            send[i, 0:half, :] = jnp.where(mine, high, low).astype(BF)
    else:
        full, keep = rest[0], rest[1]
        half = keep.shape[0]
        low, high = hold[0:half, :], hold[half : 2 * half, :]
        keep[...] = jnp.where(mine, low, high).astype(BF)
        copies = start_all([(keep, full.at[sc[0] * send.shape[0] + image])], sems)
        send[image, send.shape[1] - half :, :] = jnp.where(mine, high, low).astype(BF)
        wait_all(copies)


def output(sc, deps, acts, w2s, x1, b2, image, halves, send, full):
    count, half_s, half_l = halves
    width = w2s[0].shape[1]
    pad_s = round_up(2 * half_s, 16)
    first = 0 if image is None else count * pad_s + 2 * half_l * image
    size = count * pad_s if image is None else 2 * half_l
    inputs = [*acts, *w2s, Far(x1), b2]
    outs = [((count, round_up(half_s, 16) + half_l, width), BF), ((8, 128), F32)]
    aliases = {}
    if send is not None:
        aliases[len(inputs)] = 0
        inputs.append(send)
    scratch = []
    if image is None:
        outs.append(((count, half_s, width), BF))
    else:
        outs.append(((2 * count, half_l, width), BF, None))
        if full is not None:
            aliases[len(inputs)] = 2
            inputs.append(Far(full))
        scratch.append(pltpu.VMEM((half_l, width), BF))
    scratch += [pltpu.VMEM((size, width), BF), pltpu.VMEM((size, width), F32), pltpu.SemaphoreType.DMA((1,))]
    return call(
        functools.partial(output_kernel, first, len(inputs), image, pad_s), sc, deps, inputs, outs,
        "output", 14, scratch, aliases,
    )


def back_kernel(n_deps, sc, *refs):
    (
        dx1, xs_far, xs_in_far, xl_far, xl_in_far, gain_own, gain_in, shift_own, shift_in, as_far, ds_far, al_far, dl_far,
        es, pjs, el, pjl, g2, gy, b1a, b1b, b1c, b1d,
        gis_keep, gi_send, gil, w_keep, w_send,
        vec, x_s, x_l, tk, es_p, pjs_p, gps, ges, gpl, gel, gi_s, gi_l, gil_keep,
        xs_f, xs_in_f, xs, xs_in, xl, xl_in, as_, ds_, al, dl, sems,
    ) = refs[n_deps:]
    count = as_.shape[0]
    loads = []
    small_loads = start_all([(xs_far, xs), (xs_in_far, xs_in)], sems)
    for i in range(count):
        pairs = [(xl_far.at[sc[0] * count + i], xl.at[i]), (xl_in_far.at[i], xl_in.at[i])]
        pairs += [(far.at[i], ref.at[i]) for far, ref in ((ds_far, ds_), (as_far, as_), (dl_far, dl), (al_far, al))]
        loads.append(start_all(pairs, sems, 2 + 6 * i))
    load_token_params(sc, (gain_own, gain_in, shift_own, shift_in), tk)
    fill(es_p, es)
    fill(pjs_p, pjs)
    vec[...] = jnp.zeros_like(vec)
    gain, shift = tk[0:1, :], tk[1:2, :]

    def group(x_ref, index, at, a, d, e, pj, gp, ge, be_at, bp_row, gi, keep, send_at):
        rows, width = x_ref.shape
        hidden = a.shape[1]
        dx = dx1[at : at + rows, :]
        hat, scale = norm(x_ref[...])
        normed = (hat * gain + shift).astype(BF)
        before = (dot(pj[...], dx, TN) * d[index]).astype(BF)
        grad = dot(e[...], before, NN)
        project_grad = dot(dx, a[index], NT)
        expand_grad = dot(normed, before, NT)
        if index == 0:
            gp[0:rows, :] = project_grad
            ge[0:rows, :] = expand_grad
        else:
            gp[0:rows, :] += project_grad
            ge[0:rows, :] += expand_grad
        ones = jnp.ones((8, width), BF)
        vec[bp_row : bp_row + 1, 0:rows] += dot(ones, dx, NT)[0:1, :]
        vec[9:10, be_at : be_at + hidden] += dot(ones, before, NT)[0:1, :]
        vec[0:1, :] += jnp.sum(grad * hat, 0, keepdims=True)
        vec[1:2, :] += jnp.sum(grad, 0, keepdims=True)
        scaled = grad * gain
        mean = jnp.sum(scaled, -1, keepdims=True) * (1.0 / width)
        along = jnp.sum(scaled * hat, -1, keepdims=True) * (1.0 / width)
        gi[...] = dx.astype(F32) + scale * (scaled - mean - hat * along)
        part = width // 2
        size = keep.shape[1]
        keep[index] = gi[0:size, pl.ds(pl.multiple_of(sc[0] * part, 128), part)].astype(BF)
        theirs = gi[0:size, pl.ds(pl.multiple_of((1 - sc[0]) * part, 128), part)]
        gi_send[index, send_at : send_at + size, :] = theirs.astype(BF)

    hidden = as_.shape[1]
    pad_s, pad_l = x_s.shape[1], x_l.shape[1]
    wait_all(small_loads)
    xs_f[...] = xs[...].astype(F32)
    xs_in_f[...] = xs_in[...].astype(F32)
    for i in range(count):
        wait_all(loads[i])
        image = sc[0] * count + i
        load_image(sc, xs_f.at[:, image], xs_in_f.at[:, image], x_s.at[i])
        load_image(sc, xl.at[i], xl_in.at[i], x_l.at[i])
        group(x_s.at[i], i, i * pad_s, as_, ds_, es_p, pjs_p, gps, ges, 0, 10, gi_s, gis_keep, 0)
        group(
            x_l.at[i], i, count * pad_s + i * pad_l, al, dl, el, pjl, gpl, gel, hidden, 11,
            gi_l, gil_keep, pad_s,
        )
    copies = start_all([(gil_keep, gil.at[pl.ds(sc[0] * count, count)])], sems)
    vec[2:4, :] = g2[...]
    vec[4:5, :] = gy[...]
    for i, ref in enumerate((b1a, b1b, b1c, b1d)):
        vec[5 + i : 6 + i, :] = ref[...]
    size = w_keep.shape[2]
    half_s, half_l = gps.shape[0] // 2, gpl.shape[0] // 2
    for ref in (gps, ges):
        ref[pad_s:, :] = jnp.zeros((ref.shape[0] - pad_s, hidden), F32)
    for side, ref in ((sc[0], w_keep), (1 - sc[0], w_send)):
        for t, (small, large) in enumerate(((gps, gpl), (ges, gel))):
            at = pl.multiple_of(side * half_s, 8)
            ref[0, t] = small[pl.ds(at, size), :].astype(BF)
            for c in range(1, 4):
                have = min(size, half_l - (c - 1) * size)
                at = pl.multiple_of(side * half_l + (c - 1) * size, 8)
                ref[c, t, 0:have, :] = large[pl.ds(at, have), :].astype(BF)
                if have < size:
                    ref[c, t, have:, :] = jnp.zeros((size - have, hidden), BF)
        at = pl.multiple_of(side * hidden, 128)
        ref[3, 0, have : have + VEC, :] = vec[:, pl.ds(at, hidden)].astype(BF)
    wait_all(copies)


def piece_rows(pad_s, pad_l):
    return max(round_up(pad_s // 2, 16), round_up(-(-(pad_l // 2 + VEC) // 3), 16))


def back(sc, deps, dx1, xs, xs_in, xl, xl_in, tok, saved, weights, vectors):
    small, images, part = xs.shape
    count, large, width = images // 2, xl.shape[1], 2 * part
    pad_s, pad_l = round_up(small, 16), round_up(large, 16)
    hidden = saved[0].shape[1]
    size = piece_rows(pad_s, pad_l)
    return call(
        back_kernel, sc, deps,
        [dx1, Far(xs), Far(xs_in), Far(xl), Far(xl_in), *tok, *[Far(a) for a in saved], *weights, *vectors],
        [
            ((count, small, part), BF),
            ((count, pad_s + large, part), BF),
            ((images, large, part), BF, None),
            ((4, 2, size, hidden), BF),
            ((4, 2, size, hidden), BF),
        ],
        "back", 30, cost=12 * GFLOP, scratch=
        [
            pltpu.VMEM((VEC, width), F32),
            pltpu.VMEM((count, pad_s, width), F32),
            pltpu.VMEM((count, pad_l, width), F32),
            pltpu.VMEM((2, width), F32),
            pltpu.VMEM((pad_s, hidden), BF),
            pltpu.VMEM((pad_s, hidden), BF),
            pltpu.VMEM((2 * size, hidden), F32),
            pltpu.VMEM((2 * size, hidden), F32),
            pltpu.VMEM((pad_l, hidden), F32),
            pltpu.VMEM((pad_l, hidden), F32),
            pltpu.VMEM((pad_s, width), F32),
            pltpu.VMEM((pad_l, width), F32),
            pltpu.VMEM((count, large, part), BF),
            *[pltpu.VMEM(xs.shape, F32)] * 2,
            *[pltpu.VMEM(xs.shape, BF)] * 2,
            *[pltpu.VMEM((count, large, part), BF)] * 2,
            *[pltpu.VMEM((count, hidden, width), BF), pltpu.VMEM((count, hidden, width), F32)] * 2,
            pltpu.SemaphoreType.DMA((2 + 6 * count,)),
        ],
    )


def total4(parts):
    a, b, c, d = [p.astype(F32) for p in parts]
    return (a + b) + (c + d)


def pair_kernel(n_deps, sc, *refs):
    keep, recv = refs[n_deps : n_deps + 2]
    for k, ref in enumerate(refs[-4:]):
        ref[...] = (keep[sc[1] ^ k].astype(F32) + recv[sc[1] ^ k].astype(F32)).astype(BF)


def pair_sum(sc, deps, keep, recv, passenger=None):
    outs = [(keep.shape[1:], BF)] * 4
    if passenger is None:
        return call(pair_kernel, sc, deps, [keep, recv], outs, "pair_sum", 4)
    passed, *sums = call(
        pair_kernel, sc, deps, [keep, recv, passenger], [(passenger.shape, BF)] + outs, "pair_sum", 4,
        aliases={2: 0},
    )
    return sums, passed


def sides_kernel(n_deps, sc, *refs):
    parts, outs = refs[n_deps : n_deps + 4], refs[-4:]
    rows = parts[0].shape[1]
    half = parts[0].shape[2] // 2
    x, y = sc[1] % 2, sc[1] // 2
    for side in range(2):
        cols = slice(side * half, (side + 1) * half)
        for stays, ref in ((True, outs[2 * side]), (False, outs[2 * side + 1])):
            for k in range(2):
                if side == 0:
                    chip = 2 * (y ^ k) + (x if stays else 1 - x)
                else:
                    chip = 2 * (y if stays else 1 - y) + (x ^ k)
                for i in range(2):
                    keep, recv = parts[2 * i : 2 * i + 2]
                    total = keep[chip, :, cols].astype(F32) + recv[chip, :, cols].astype(F32)
                    ref[k, i * rows : (i + 1) * rows, :] = total.astype(BF)


def sides_sum(sc, deps, parts):
    chips, rows, width = parts[0].shape
    return call(sides_kernel, sc, deps, parts, [((2, 2 * rows, width // 2), BF)] * 4, "sides_sum", 6)


def second_kernel(n_deps, sc, *refs):
    refs = refs[n_deps:]
    for side in range(2):
        keep, recv = refs[2 * side : 2 * side + 2]
        for k in range(2):
            refs[4 + 2 * side + k][...] = (keep[k].astype(F32) + recv[k].astype(F32)).astype(BF)


def second_sum(sc, deps, parts):
    return call(second_kernel, sc, deps, parts, [(parts[0].shape[1:], BF)] * 4, "second_sum", 4)


def quad_kernel(n_parts, n_deps, sc, *refs):
    parts, (keep, send, hold, rest) = refs[n_deps : n_deps + n_parts], refs[-4:]
    rows = keep.shape[0] // 2
    quarter = rows // PLANES
    for i in range(2):
        if len(parts) == 4:
            here = slice(2 * rows * i, 2 * rows * (i + 1))
            sums = [parts[j][here, :].astype(F32) + parts[j + 1][here, :].astype(F32) for j in (0, 2)]
            total = jnp.concatenate(sums, 1)
        else:
            total = total4([r[...] for r in parts[4 * i : 4 * i + 4]])
        hold[i] = total[0:rows].reshape(hold.shape[1:])
        rest[i] = total[rows:]
    high, low = sc[2] // 2, sc[2] % 2
    for side, ref in ((high, keep), (1 - high, send)):
        for k in range(2):
            pair = [hold[i, 2 * side + (low ^ k)] for i in range(2)]
            ref[2 * k * quarter : 2 * (k + 1) * quarter, :] = jnp.concatenate(pair, 0).astype(BF)
        ref[rows:, :] = rest[side].astype(BF)


def quad_sum(sc, deps, parts, passengers=()):
    rows, width = parts[0].shape
    if len(parts) == 4:
        rows, width = rows // 2, 2 * width
    quarter = rows // 2 // PLANES
    passed = [(a.shape, a.dtype) for a in passengers]
    *passed, keep, send = call(
        functools.partial(quad_kernel, len(parts)), sc, deps, [*parts, *passengers],
        passed + [((rows, width), BF)] * 2, "quad_sum", 6,
        [pltpu.VMEM((2, PLANES, quarter, width), F32), pltpu.VMEM((2, rows // 2, width), F32)],
        {len(parts) + i: i for i in range(len(passed))},
    )
    return keep, send, passed


def planes_kernel(n_deps, sc, *refs):
    a, b = refs[n_deps : n_deps + 2]
    keep, send = refs[-2:]
    rows = a.shape[0]
    cut = rows // 4
    total = a[...].astype(F32) + b[...].astype(F32)
    keep[0:cut, :] = total[0:cut].astype(BF)
    send[0:cut, :] = total[cut : 2 * cut].astype(BF)
    rest = total[2 * cut :].astype(BF)
    keep[cut:, :] = rest
    send[cut:, :] = rest


def planes_sum(sc, deps, keep, recv, passengers=()):
    rows, width = keep.shape
    passed = [(a.shape, a.dtype) for a in passengers]
    *passed, keep, send = call(
        planes_kernel, sc, deps, [keep, recv, *passengers], passed + [((3 * rows // 4, width), BF)] * 2,
        "planes_sum", 4, aliases={2 + i: i for i in range(len(passed))},
    )
    return keep, send, passed


def last_kernel(groups, n_deps, sc, *refs):
    refs = refs[n_deps:]
    expand_out, project_out, expand, project, sems = refs[-5:]
    width = expand.shape[1] // PLANES
    quarter = expand.shape[0]
    for g, planes in enumerate(groups):
        total = refs[2 * g][...].astype(F32) + refs[2 * g + 1][...].astype(F32)
        for i, plane in enumerate(planes):
            expand[:, plane * width : (plane + 1) * width] = total[i * quarter : (i + 1) * quarter]

        @pl.when((sc[2] == planes[0]) | (sc[2] == planes[1]))
        def _():
            project[...] = total[2 * quarter :]

    wait_all(start_all([(expand, expand_out), (project, project_out)], sems))


def last_sum(sc, groups, pieces):
    flat = [a for group in groups for a in pieces[group]]
    rows, width = flat[0].shape
    shapes = [(rows // 6, PLANES * width), (2 * rows // 3, width)]
    return call(
        functools.partial(last_kernel, groups), sc, [], flat, [(s, F32, None) for s in shapes], "last_sum", 4,
        [pltpu.VMEM(s, F32) for s in shapes] + [pltpu.SemaphoreType.DMA((2,))],
    )


def piece_at(rows):
    size = round_up(-(-rows // 2), 16)
    return rows - size, size


def split_kernel(n_deps, sc, *refs):
    parts, outs, hold = refs[n_deps : n_deps + 4], refs[-5:-1], refs[-1]
    hold[...] = total4([r[...] for r in parts])
    second, size = piece_at(hold.shape[1])
    for k, ref in enumerate(outs):
        piece = sc[2] ^ k
        at = pl.multiple_of((piece % 2) * second, 16)
        ref[...] = hold[piece // 2, pl.ds(at, size), :].astype(BF)


def token_split(sc, deps, parts, passenger):
    size = piece_at(parts[0].shape[1])[1]
    return call(
        split_kernel, sc, deps, [*parts, passenger],
        [(passenger.shape, passenger.dtype)] + [((size, parts[0].shape[2]), BF)] * 4, "token_split", 4,
        [pltpu.VMEM(parts[0].shape, F32)], {4: 0},
    )


def token_sum_kernel(n_deps, sc, *refs):
    refs[-1][...] = total4([r[...] for r in refs[n_deps : n_deps + 4]]).astype(BF)


def token_sum(sc, deps, parts, passenger):
    outs = [(passenger.shape, passenger.dtype), (parts[0].shape, BF)]
    return call(token_sum_kernel, sc, deps, [*parts, passenger], outs, "token_sum", 4, aliases={4: 0})


def join_kernel(n_deps, sc, *refs):
    parts, w, hold = refs[n_deps : n_deps + 4], refs[-2], refs[-1]
    for k, ref in enumerate(parts):
        hold[sc[2] ^ k] = ref[...]
    second, size = piece_at(w.shape[1])
    for piece in range(PLANES):
        at = (piece % 2) * second
        w[piece // 2, at : at + size, :] = hold[piece]


def token_join(sc, deps, parts, rows):
    size, hidden = parts[0].shape
    return call(
        join_kernel, sc, deps, parts, [((2, rows, hidden), BF)], "token_join", 4,
        [pltpu.VMEM((PLANES, size, hidden), BF)],
    )[0]


def unpack_kernel(n_deps, sc, *refs):
    refs = refs[n_deps:]
    mine, theirs = refs[0:4], refs[4:8]
    ges, gps, gel, gpl = refs[8:12]
    vectors = refs[12:22]
    hold, vec = refs[22:]
    for k in range(4):
        hold[sc[0], sc[1] ^ k] = mine[k][...]
        hold[1 - sc[0], sc[1] ^ k] = theirs[k][...]
    size, hidden = mine[0].shape[1:]
    small, large = ges.shape[0], gel.shape[0]
    for side in range(2):
        low = side * size
        have = min(size, small - low)
        for t, ref in enumerate((gps, ges)):
            ref[low : low + have, :] = hold[side, 0, t].astype(F32)[0:have, :]
        for c in range(1, 4):
            low = side * (large // 2) + (c - 1) * size
            have = min(size, large // 2 - (c - 1) * size)
            for t, ref in enumerate((gpl, gel)):
                ref[low : low + have, :] = hold[side, c, t].astype(F32)[0:have, :]
        vec[:, side * hidden : (side + 1) * hidden] = hold[side, 3, 0].astype(F32)[have : have + VEC, :]
    width = vec.shape[1]
    picks = [(0, 0), (1, 0), (9, 0), (10, 0), (9, hidden), (11, 0), (2, 0), (3, 0), None, (4, 0)]
    for ref, pick in zip(vectors, picks):
        if pick is None:
            for i in range(ref.shape[0] // width):
                ref[i * width : (i + 1) * width] = vec[5 + i, :]
        else:
            row, at = pick
            ref[...] = vec[row, at : at + ref.shape[0]]


def unpack(sc, deps, mine, theirs, small, large, width, channel_hidden):
    hidden = mine[0].shape[2]
    outs = [(small, hidden)] * 2 + [(large, hidden)] * 2
    outs += [(n,) for n in (width, width, hidden, small, hidden, large, width, width, channel_hidden, width)]
    return pl.pallas_call(
        functools.partial(unpack_kernel, len(deps)),
        in_specs=[pl.BlockSpec(memory_space=pltpu.SMEM)]
        + [pl.BlockSpec(memory_space=pltpu.VMEM)] * (len(deps) + 8),
        out_shape=[jax.ShapeDtypeStruct(s, F32) for s in outs],
        scratch_shapes=[pltpu.VMEM((2, 4) + mine[0].shape, BF), pltpu.VMEM((VEC, width), F32)],
        compiler_params=pltpu.CompilerParams(vmem_limit_bytes=12 * MB),
        cost_estimate=pl.CostEstimate(flops=0, bytes_accessed=0, transcendentals=0),
        name="unpack",
    )(sc, *deps, *mine, *theirs)


def place_kernel(n_deps, sc, *refs):
    refs = refs[n_deps:]
    keeps, received = refs[0:2], refs[2:4]
    tick, far_small, far_large, near, sems = refs[6], refs[7:9], refs[9:11], refs[11:13], refs[13]
    count = keeps[0].shape[0]
    pairs = []
    for theirs, far in zip(received, far_large):
        at = theirs.shape[1] - far.shape[1]
        for i in range(count):
            pairs.append((theirs.at[i, at:, :], far.at[(1 - sc[0]) * count + i]))
    copies = start_all(pairs, sems)
    for mine, theirs, ref in zip(keeps, received, near):
        size = mine.shape[1]
        for j in range(2 * count):
            k = j % count
            other = theirs[k, 0:size, :].astype(F32)
            ref[:, j, :] = jnp.where(sc[0] == j // count, mine[k].astype(F32), other).astype(BF)
    copies += start_all(zip(near, far_small), sems, len(copies))
    tick[...] = jnp.zeros_like(tick)
    wait_all(copies)


def place(sc, deps, keeps, received, filled):
    shapes = [(a.shape[1], 2 * a.shape[0], a.shape[2]) for a in keeps]
    count = keeps[0].shape[0]
    return call(
        place_kernel, sc, deps, keeps + received + [Far(a) for a in filled],
        [((8, 128), F32)] + [(shape, BF, None) for shape in shapes] + [(a.shape, BF, None) for a in filled],
        "place", 6,
        [pltpu.VMEM(shape, BF) for shape in shapes] + [pltpu.SemaphoreType.DMA((2 * count + 2,))],
        {4: 3, 5: 4},
    )


def swap(values):
    return lax.ppermute(values, "mp", [(0, 1), (1, 0)])


def across(values, mask, pairs):
    return lax.ppermute(values, "dp", [(i, i ^ mask) for i in pairs])


def per_device(
    chips,
    small_images,
    large_images,
    token_gain,
    token_shift,
    small_expand,
    small_expand_bias,
    small_project,
    small_project_bias,
    large_expand,
    large_expand_bias,
    large_project,
    large_project_bias,
    channel_gain,
    channel_shift,
    channel_expand,
    channel_expand_bias,
    channel_project,
    channel_project_bias,
    small_cotangent,
    large_cotangent,
):
    core = lax.axis_index("mp")
    chip = lax.axis_index("dp")
    sc = jnp.stack([core, chip % 4, (chip // 4) % PLANES]).astype(jnp.int32)
    small_images, small_cotangent = small_images.transpose(1, 0, 2), small_cotangent.transpose(1, 0, 2)
    small, images, part = small_images.shape
    large = large_images.shape[1]
    count = images // 2
    width = channel_expand.shape[0]
    everyone = range(chips)
    tuned = chips == 4 * PLANES

    xl_send, yl_send = pick(sc, large_images, large_cotangent)
    xs_in, xl_in = swap(small_images), swap(xl_send)
    tok = [token_gain, swap(token_gain), token_shift, swap(token_shift)]
    ys_in, yl_in = swap(small_cotangent), swap(yl_send)
    token_s = [small_expand, small_expand_bias, small_project.T, small_project_bias]
    token_l = [large_expand, large_expand_bias, large_project.T, large_project_bias]
    xs, xl, y, *weights = prepare(
        sc, small_images, large_images, small_cotangent, large_cotangent, token_s, token_l
    )
    n2, w1, w2, x1, as_, ds_, al, dl = front(
        sc, xs, xs_in, xl, xl_in, tok, weights, channel_gain, channel_shift, channel_expand, channel_project
    )
    y = cotangent_rows(sc, [n2], small_cotangent, ys_in, yl_in, y)
    carried = []
    sends, keeps, b1_grads, halved, pieces = {}, {}, {}, {}, {}
    groups = (ORDER[:2], ORDER[2:])

    def halve(plane, deps, passenger=None):
        sums = pair_sum(sc, deps, keeps[plane], swap(sends[plane]), None if passenger is None else sends[passenger])
        if passenger is not None:
            sums, sends[passenger] = sums
        own, *others = sums
        halved[plane] = [own] + [across(o, k + 1, everyone) for k, o in enumerate(others)]

    def quarter(group, deps, passenger=None):
        parts = halved[group] if group in halved else halved[group[0]] + halved[group[1]]
        if passenger is None:
            keep, send, _ = quad_sum(sc, deps, parts)
        else:
            keep, send, (sends[passenger],) = quad_sum(sc, deps, parts, [sends[passenger]])
        pieces[group] = [keep, across(send, 8, everyone)]

        def finish(deps, passengers=()):
            keep, send, passed = planes_sum(sc, deps, *pieces[group], passengers)
            pieces[group] = [keep, send]
            return passed

        return finish

    n_last = PLANES - 1
    acts, w2s = [], []
    halves = (count, small // 2, large // 2)

    def rows_out(deps, image, send, full):
        return output(sc, deps, acts, w2s, x1, channel_project_bias, image, halves, send, full)

    for i, plane in enumerate(ORDER):
        is_last = i == n_last
        following = None if is_last else ORDER[i + 1]
        if is_last:
            ending = [Far(x1), channel_gain]
        else:
            ending = [Far(channel_expand), Far(channel_project)]
        deps = []
        if tuned and i >= 2:
            arrived = halved[ORDER[i - 3]][1:] if i >= 3 else []
            halve(ORDER[i - 2], [b1_grads[ORDER[i - 1]]] + arrived, ORDER[2] if is_last else None)
            deps = halved[ORDER[i - 2]][:1]
        w2s.append(w2)
        sends[plane], keeps[plane], b1_grads[plane], dn_low, dn_high, active, *carried = channel(
            sc, deps, plane, following, [n2, y], w1, channel_expand_bias, w2, carried, ending
        )
        acts.append(active)
        if i == 0:
            *carried, gy = carried
        if not is_last:
            w1, w2 = carried
            carried = [dn_low, dn_high]
    dx1, g2 = carried
    deps = []
    if tuned:
        finish = quarter(groups[0], [b1_grads[ORDER[3]]], ORDER[3])
        keep_a, send_a, keep_b, send_b = sides_sum(
            sc, [pieces[groups[0]][0]],
            [a for plane in groups[1] for a in (keeps[plane], swap(sends[plane]))],
        )
        recv_a, recv_b = across(send_a, 1, everyone), across(send_b, 2, everyone)
        deps = [keep_a]
    gis_keep, gi_send, gil, w_keep, w_send = back(
        sc, deps, dx1, small_images, xs_in, large_images, xl_in, tok,
        [as_, ds_, al, dl],
        [small_expand, small_project.T, large_expand, large_project.T],
        [g2, gy] + [b1_grads[plane] for plane in range(PLANES)],
    )

    if tuned:
        w_send, gi_send = finish([w_keep, recv_a, recv_b], [w_send, gi_send])
        gi_in = swap(gi_send)
        keep_a, send_a, keep_b, send_b = second_sum(
            sc, [pieces[groups[0]][0]], [keep_a, recv_a, keep_b, recv_b]
        )
        halved[groups[1]] = [keep_a, across(send_a, 2, everyone), keep_b, across(send_b, 1, everyone)]
        own, *others = pair_sum(sc, [keep_a, gi_in], w_keep, swap(w_send))
        parts = [own] + [across(o, k + 1, everyone) for k, o in enumerate(others)]
        out_send, tick, outl_full = rows_out([own], 0, None, None)
        finish = quarter(groups[1], [tick])
        send, own, *others = token_split(sc, [pieces[groups[1]][0]], parts, pieces[groups[0]][1])
        pieces[groups[0]][1] = across(send, 4, everyone)
        parts = [own] + [across(o, 4 * (k + 1), everyone) for k, o in enumerate(others)]
        out_send, tick, outs_keep = rows_out([own], None, out_send, None)
        out_send, tick, outl_full = rows_out([tick], 1, out_send, outl_full)
        out_send, w = token_sum(sc, [tick, pieces[groups[0]][1], pieces[groups[1]][1]], parts, out_send)
        out_in = swap(out_send)
        parts = [w] + [across(w, 4 * k, everyone) for k in (1, 2, 3)]
        finish([w])
        pieces[groups[1]][1] = across(pieces[groups[1]][1], 4, everyone)
        tick, small_output, small_input_grad, large_output, large_input_grad = place(
            sc, [pieces[groups[1]][0]], [outs_keep, gis_keep], [out_in, gi_in], [outl_full, gil]
        )
        w = token_join(sc, [tick], parts, w_keep.shape[2])
        mine = [w] + [across(w, k, everyone) for k in (1, 2, 3)]
        extra = []
        expand_part, project_part = last_sum(sc, groups, pieces)
    else:
        out_send, _, outl_full = rows_out([], 0, None, None)
        out_send, _, outl_full = rows_out([], 1, out_send, outl_full)
        out_send, _, outs_keep = rows_out([], None, out_send, None)
        _, small_output, small_input_grad, large_output, large_input_grad = place(
            sc, [], [outs_keep, gis_keep], [swap(out_send), swap(gi_send)], [outl_full, gil]
        )
        extra = []

        def both(keep, send):
            return jnp.where(core == 0, jnp.stack([keep, send]), jnp.stack([send, keep])).astype(F32)

        expand_full, project_full = [], []
        for plane in range(PLANES):
            parts = both(keeps[plane], sends[plane])
            cut = width // 8
            e = parts[:, :, :cut].reshape(2, 4, PLANES, width // 32, -1)
            expand_full.append(e.transpose(2, 1, 0, 3, 4).reshape(width, -1))
            project_full.append(parts[:, :, cut:].transpose(1, 0, 2, 3).reshape(-1, width))
        expand_part = lax.psum_scatter(
            jnp.concatenate(expand_full, 1), ("dp", "mp"), scatter_dimension=0, tiled=True
        )
        project_part = lax.psum_scatter(
            jnp.concatenate(project_full, 0), ("dp", "mp"), scatter_dimension=0, tiled=True
        )
        token = lax.psum(both(w_keep, w_send), ("dp", "mp"))
        token = lax.dynamic_index_in_dim(token, core, 0, False).astype(BF)
        mine = [lax.dynamic_index_in_dim(token, sc[1] ^ k, 0, False) for k in range(4)]
    unpacked = unpack(
        sc, extra, mine, [swap(w) for w in mine], small, large, width, channel_expand.shape[1]
    )
    (ges, gps_t, gel, gpl_t, gtg, gts, gbes, gbps, gbel, gbpl, gcg, gcs, gb1, gb2) = unpacked
    small_output, small_input_grad = small_output.transpose(1, 0, 2), small_input_grad.transpose(1, 0, 2)
    return (
        small_output, large_output, small_input_grad, large_input_grad,
        gtg, gts, ges, gbes, gps_t.T, gbps, gel, gbel, gpl_t.T, gbpl,
        gcg, gcs, expand_part, gb1, project_part, gb2,
    )


def solution(mesh):
    replicated = P()
    by_channel = P("dp", None, "mp")
    by_patch = P("dp", "mp", None)
    by_row = P(("dp", "mp"), None)
    return jax.shard_map(
        functools.partial(per_device, mesh.shape["dp"]),
        mesh=mesh,
        in_specs=(by_channel, by_channel, P("mp"), P("mp")) + (replicated,) * 14 + (by_patch, by_patch),
        out_specs=(by_patch, by_patch, by_channel, by_channel)
        + (replicated,) * 12
        + (by_row, replicated, by_row, replicated),
        check_vma=False,
    )
```

```python
import functools

import jax
import jax.numpy as jnp
from jax import lax
from jax.experimental import pallas as pl
from jax.experimental.pallas import tpu as pltpu
from jax.sharding import PartitionSpec as P

BF = jnp.bfloat16
F32 = jnp.float32
EPS = 1e-06
SQRT_HALF = 0.7071067811865476
INV_SQRT_2PI = 0.3989422804014327
HALF_LOG2E = 0.7213475204444817
NN = ((1,), (0,))
NT = ((1,), (1,))
TN = ((0,), (0,))
MB = 1 << 20
GFLOP = 10**9
PLANES = 4
ORDER = (1, 2, 0, 3)
VEC = 16


def dot(left, right, dims):
    return lax.dot_general(left, right, (dims, ((), ())), preferred_element_type=F32)


def gelu_pair(values):
    cdf = 0.5 * lax.erf(values * SQRT_HALF) + 0.5
    pdf = jnp.exp2((values * values) * (-HALF_LOG2E)) * INV_SQRT_2PI
    return values * cdf, cdf + values * pdf


def norm(values):
    width = values.shape[-1]
    mean = jnp.sum(values, -1, keepdims=True) * (1.0 / width)
    square = jnp.sum(values * values, -1, keepdims=True) * (1.0 / width)
    scale = lax.rsqrt(square - mean * mean + EPS)
    return (values - mean) * scale, scale


def round_up(value, to):
    return (value + to - 1) // to * to


def call(kernel, sc, deps, inputs, outs, name, limit, scratch=(), aliases=None, cost=0):
    anywhere, vmem = pl.BlockSpec(memory_space=pl.ANY), pl.BlockSpec(memory_space=pltpu.VMEM)
    first = 1 + len(deps)
    return pl.pallas_call(
        functools.partial(kernel, len(deps)),
        in_specs=[pl.BlockSpec(memory_space=pltpu.SMEM)]
        + [vmem] * len(deps)
        + [vmem if not isinstance(a, Far) else anywhere for a in inputs],
        out_specs=[anywhere if len(o) == 3 else vmem for o in outs],
        out_shape=[pltpu.HBM(*o[:2]) if len(o) == 3 else pltpu.VMEM(*o) for o in outs],
        scratch_shapes=scratch,
        input_output_aliases={first + a: b for a, b in (aliases or {}).items()},
        compiler_params=pltpu.CompilerParams(vmem_limit_bytes=limit * MB),
        cost_estimate=pl.CostEstimate(flops=cost, bytes_accessed=0, transcendentals=0),
        name=name,
    )(sc, *deps, *[a.array if isinstance(a, Far) else a for a in inputs])


class Far:
    def __init__(self, array):
        self.array = pltpu.with_memory_space_constraint(array, pltpu.HBM)


def start_all(pairs, sems, first=0):
    copies = [pltpu.make_async_copy(a, b, sems.at[first + i]) for i, (a, b) in enumerate(pairs)]
    for copy in copies:
        copy.start()
    return copies


def wait_all(copies):
    for copy in copies:
        copy.wait()


def quarter_of(plane, size, w1, w2):
    here = slice(plane * size, (plane + 1) * size)
    return w1.at[:, here], w2.at[here, :]


def load_image(sc, own, other, dest):
    rows, part = own.shape
    dest[0:rows, pl.ds(pl.multiple_of(sc[0] * part, 128), part)] = own[...].astype(F32)
    dest[0:rows, pl.ds(pl.multiple_of((1 - sc[0]) * part, 128), part)] = other[...].astype(F32)
    if dest.shape[0] != rows:
        dest[rows:, :] = jnp.zeros((dest.shape[0] - rows, dest.shape[1]), F32)


def load_token_params(sc, tok, dest):
    for row in range(2):
        own, other = tok[2 * row : 2 * row + 2]
        part = own.shape[0]
        dest[row : row + 1, pl.ds(pl.multiple_of(sc[0] * part, 128), part)] = own[...][None]
        dest[row : row + 1, pl.ds(pl.multiple_of((1 - sc[0]) * part, 128), part)] = other[...][None]


def fill(dest, source):
    rows = source.shape[0]
    dest[0:rows, :] = source[...]
    if dest.shape[0] != rows:
        dest[rows:, :] = jnp.zeros((dest.shape[0] - rows, dest.shape[1]), dest.dtype)


def fill_column(dest, source):
    size = source.shape[0]
    if dest.shape[0] != size:
        dest[...] = jnp.zeros_like(dest)
    dest[0:size, :] = jnp.broadcast_to(source[...][None], (8, size)).T[:, 0:1]


def pick_kernel(n_deps, sc, *refs):
    count = refs[2].shape[0]
    theirs = pl.ds((1 - sc[0]) * count, count)
    wait_all(start_all([(far.at[theirs], ref) for far, ref in zip(refs[:2], refs[2:4])], refs[4]))


def pick(sc, *arrays):
    return call(
        pick_kernel, sc, [], [Far(a) for a in arrays],
        [((a.shape[0] // 2,) + a.shape[1:], a.dtype) for a in arrays], "pick", 2,
        [pltpu.SemaphoreType.DMA((2,))],
    )


def prepare_kernel(
    n_deps, sc, xs_far, xl_far, yl_far, el_far, pjl_far, es_far, pjs_far, bes_far, bps_far, bel_far, bpl_far,
    xs, xl, y, el, pjl, es_p, pjs_p, bes_c, bps_c, bel_c, bpl_c,
    es, pjs, bes, bps, bel, bpl, sems,
):
    count, half = xl.shape[0], yl_far.shape[1]
    own = pl.ds(sc[0] * count, count)
    pairs = [(es_far, es), (pjs_far, pjs), (bes_far, bes), (bps_far, bps), (bel_far, bel), (bpl_far, bpl)]
    pairs += [(xs_far, xs), (xl_far.at[own], xl), (el_far, el), (pjl_far, pjl)]
    base = y.shape[0] - 2 * half * count
    for i in range(count):
        at = pl.multiple_of(base + 2 * half * i + sc[0] * half, 16)
        pairs.append((yl_far.at[sc[0] * count + i], y.at[pl.ds(at, half)]))
    copies = start_all(pairs, sems)
    wait_all(copies[:6])
    fill(es_p, es)
    fill(pjs_p, pjs)
    fill_column(bes_c, bes)
    fill_column(bps_c, bps)
    fill_column(bel_c, bel)
    fill_column(bpl_c, bpl)
    wait_all(copies[6:])


def prepare(sc, xs, xl, ys, yl, token_s, token_l):
    small, images, part = xs.shape
    count, large, width = images // 2, xl.shape[1], 2 * part
    es, bes, pjs, bps = token_s
    el, bel, pjl, bpl = token_l
    hidden = es.shape[1]
    pad_s, pad_l = round_up(small, 16), round_up(large, 16)
    far = [xs, xl, yl, el, pjl, es, pjs, bes, bps, bel, bpl]
    return call(
        prepare_kernel, sc, [], [Far(a) for a in far],
        [
            (xs.shape, BF),
            ((count, large, part), BF),
            ((count * (pad_s + pad_l), width), BF),
            (el.shape, BF),
            (pjl.shape, BF),
            ((pad_s, hidden), BF),
            ((pad_s, hidden), BF),
            *[((rows, 1), F32) for rows in (hidden, pad_s, hidden, pad_l)],
        ],
        "prepare", 6, cost=3 * GFLOP, scratch=
        [pltpu.VMEM(es.shape, BF), pltpu.VMEM(pjs.shape, BF)]
        + [pltpu.VMEM(a.shape, F32) for a in (bes, bps, bel, bpl)]
        + [pltpu.SemaphoreType.DMA((10 + count,))],
    )


def front_kernel(
    n_deps, sc, xs, xs_in, xl, xl_in, gain_own, gain_in, shift_own, shift_in,
    el, pjl, es, pjs, bes, bps, bel, bpl, gain2, shift2, w1_far, w2_far,
    n2, w1, w2, x1_far, as_far, ds_far, al_far, dl_far,
    xs_f, xs_in_f, x_s, x_l, tk, x1, as_, ds_, al, dl, sems,
):
    count = xl.shape[0]
    copies = start_all(zip(quarter_of(ORDER[0], w1.shape[1], w1_far, w2_far), (w1, w2)), sems)
    xs_f[...] = xs[...].astype(F32)
    xs_in_f[...] = xs_in[...].astype(F32)
    load_token_params(sc, (gain_own, gain_in, shift_own, shift_in), tk)
    gain, shift = tk[0:1, :], tk[1:2, :]
    after_gain, after_shift = gain2[...][None], shift2[...][None]

    def group(x_ref, e, be, pj, bp, index, at, a_ref, d_ref, a_far, d_far):
        rows = x_ref.shape[0]
        hat, _ = norm(x_ref[...])
        normed = (hat * gain + shift).astype(BF)
        active, slope = gelu_pair(dot(e[...], normed, TN) + be[...])
        active = active.astype(BF)
        a_ref[index] = active
        d_ref[index] = slope
        copies.extend(
            start_all([(a_ref.at[index], a_far.at[index]), (d_ref.at[index], d_far.at[index])], sems, len(copies))
        )
        middle = (x_ref[...] + (dot(pj[...], active, NN) + bp[...])).astype(BF)
        here = slice(at, at + rows)
        x1[here, :] = middle
        copies.extend(start_all([(x1.at[here], x1_far.at[here])], sems, len(copies)))
        hat2, _ = norm(middle.astype(F32))
        n2[here, :] = (hat2 * after_gain + after_shift).astype(BF)

    pad_s, pad_l = x_s.shape[1], x_l.shape[1]
    for i in range(count):
        image = sc[0] * count + i
        load_image(sc, xl.at[i], xl_in.at[i], x_l.at[i])
        load_image(sc, xs_f.at[:, image], xs_in_f.at[:, image], x_s.at[i])
        group(x_l.at[i], el, bel, pjl, bpl, i, count * pad_s + i * pad_l, al, dl, al_far, dl_far)
        group(x_s.at[i], es, bes, pjs, bps, i, i * pad_s, as_, ds_, as_far, ds_far)
    wait_all(copies)


def front(sc, xs, xs_in, xl, xl_in, tok, weights, gain2, shift2, w1, w2):
    images, part = xs.shape[1:]
    count, width = images // 2, 2 * part
    pad_l, hidden = weights[0].shape
    pad_s = weights[2].shape[0]
    rows = count * (pad_s + pad_l)
    state = (count, hidden, width)
    quarter = w1.shape[1] // PLANES
    return call(
        front_kernel, sc, [], [xs, xs_in, xl, xl_in, *tok, *weights, gain2, shift2, Far(w1), Far(w2)],
        [((rows, width), BF), ((width, quarter), BF), ((quarter, width), BF), ((rows, width), BF, None)] + [(state, BF, None), (state, F32, None)] * 2,
        "front", 23, cost=8 * GFLOP, scratch=
        [
            *[pltpu.VMEM(xs.shape, F32)] * 2,
            pltpu.VMEM((count, pad_s, width), F32),
            pltpu.VMEM((count, pad_l, width), F32),
            pltpu.VMEM((2, width), F32),
            pltpu.VMEM((rows, width), BF),
            *[pltpu.VMEM(state, BF), pltpu.VMEM(state, F32)] * 2,
            pltpu.SemaphoreType.DMA((2 + 6 * count,)),
        ],
    )


def rows_kernel(n_deps, sc, *refs):
    ys, ys_in, yl_in, _, y, ys_f, ys_in_f, hold, sems = refs[n_deps:]
    first = sc[0] == 0
    half, images, width = ys.shape
    count = images // 2
    pad_s, half_l = hold.shape[0], yl_in.shape[1]
    pairs = []
    for i in range(count):
        at = pl.multiple_of(count * pad_s + 2 * half_l * i + (1 - sc[0]) * half_l, 16)
        pairs.append((yl_in.at[i], y.at[pl.ds(at, half_l)]))
    copies = start_all(pairs, sems)
    ys_f[...] = ys[...].astype(F32)
    ys_in_f[...] = ys_in[...].astype(F32)
    hold[2 * half :, :] = jnp.zeros((pad_s - 2 * half, width), F32)
    for i in range(count):
        image = sc[0] * count + i
        mine, theirs = ys_f[:, image, :], ys_in_f[:, image, :]
        hold[0:half, :] = jnp.where(first, mine, theirs)
        hold[half : 2 * half, :] = jnp.where(first, theirs, mine)
        y[i * pad_s : (i + 1) * pad_s, :] = hold[...].astype(BF)
    wait_all(copies)


def cotangent_rows(sc, deps, ys, ys_in, yl_in, y):
    hs, images, width = ys.shape
    count = images // 2
    pad_s = round_up(2 * hs, 16)
    return call(
        rows_kernel, sc, deps, [ys, ys_in, yl_in, y], [(y.shape, BF)], "rows", 8, cost=3 * GFLOP, scratch=
        [*[pltpu.VMEM(ys.shape, F32)] * 2, pltpu.VMEM((pad_s, width), F32), pltpu.SemaphoreType.DMA((count,))],
        aliases={3: 0},
    )[0]


def channel_kernel(following, is_first, n_deps, sc, *refs):
    is_last = following is None
    refs = list(refs[n_deps:])
    n2, y, w1, b1, w2 = [refs.pop(0) for _ in range(5)]
    if not is_first:
        del refs[:2]
    if is_last:
        x1_far, gain2 = refs.pop(0), refs.pop(0)
    else:
        w1_far, w2_far = refs.pop(0), refs.pop(0)
    send, keep, gb1, dn_low, dn_high, acts = [refs.pop(0) for _ in range(6)]
    dn = (dn_low, dn_high)
    if is_last:
        dx1, g2 = refs.pop(0), refs.pop(0)
    else:
        w1_next, w2_next = refs.pop(0), refs.pop(0)
    if is_first:
        gy = refs.pop(0)
        gy[...] = dot(jnp.ones((8, y.shape[0]), BF), y[...], NN)[0:1, :]
    grads, sems = refs.pop(0), refs.pop(0)
    rows, width = n2.shape
    hidden = acts.shape[1]
    tile = rows // 2
    if is_last:
        x1 = refs.pop(0)
        copies = start_all([(x1_far, x1)], sems)
    else:
        copies = start_all(zip(quarter_of(following, hidden, w1_far, w2_far), (w1_next, w2_next)), sems)
    bias_grad = jnp.zeros((1, hidden), F32)
    for step in range(2):
        here = pl.ds(step * tile, tile)
        active, slope = gelu_pair(dot(n2[here, :], w1[...], NN) + b1[...])
        grad = dot(y[here, :], w2[...], NT) * slope
        bias_grad = bias_grad + jnp.sum(grad, 0, keepdims=True)
        acts[here, :] = active.astype(BF)
        grads[here, :] = grad.astype(BF)
    gb1[...] = bias_grad
    for step in range(2):
        here = pl.ds(step * tile, tile)
        back = dot(grads[here, :], w1[...], NT)
        if is_first:
            dn[step][...] = back
        else:
            dn[step][...] += back
    if is_last:
        wait_all(copies)
        copies = []
        gain = gain2[...][None]
        gain_sum = jnp.zeros((1, width), F32)
        shift_sum = jnp.zeros((1, width), F32)
        for step in range(2):
            here = slice(step * tile, (step + 1) * tile)
            hat, scale = norm(x1[here, :].astype(F32))
            back = dn[step][...]
            gain_sum = gain_sum + jnp.sum(back * hat, 0, keepdims=True)
            shift_sum = shift_sum + jnp.sum(back, 0, keepdims=True)
            scaled = back * gain
            mean = jnp.sum(scaled, -1, keepdims=True) * (1.0 / width)
            along = jnp.sum(scaled * hat, -1, keepdims=True) * (1.0 / width)
            dx1[here, :] = (
                y[here, :].astype(F32) + scale * (scaled - mean - hat * along)
            ).astype(BF)
        g2[0:1, :] = gain_sum
        g2[1:2, :] = shift_sum
    weight_grads(sc, n2, y, acts, grads, send, keep)
    wait_all(copies)


def weight_grads(sc, n2, y, acts, grads, send, keep):
    width, hidden = n2.shape[1], acts.shape[1]
    first = sc[0] == 0
    quarter = width // 32
    cut = PLANES * quarter
    expand = dot(n2[...], grads[...], TN).reshape(PLANES, 4, 2, quarter, hidden)
    for c in range(4):
        low = expand[:, c, 0].reshape(cut, hidden)
        high = expand[:, c, 1].reshape(cut, hidden)
        keep[c, 0:cut, :] = jnp.where(first, low, high).astype(BF)
        send[c, 0:cut, :] = jnp.where(first, high, low).astype(BF)
    project = dot(acts[...], y[...], TN).reshape(4, 2, hidden // 8, width)
    for c in range(4):
        low, high = project[c, 0], project[c, 1]
        keep[c, cut:, :] = jnp.where(first, low, high).astype(BF)
        send[c, cut:, :] = jnp.where(first, high, low).astype(BF)


def channel(sc, deps, plane, following, rows_in, w1, b1, w2, carried, ending):
    is_first, is_last = not carried, following is None
    rows, width = rows_in[0].shape
    hidden = w1.shape[1]
    block = (4, width // 8 + hidden // 8, width)
    outs = [(block, BF)] * 2 + [((1, hidden), F32)] + [((rows // 2, width), F32)] * 2 + [((rows, hidden), BF)]
    scratch = [pltpu.VMEM((rows, hidden), BF), pltpu.SemaphoreType.DMA((2,))]
    if is_last:
        outs += [((rows, width), BF), ((2, width), F32)]
        scratch.append(pltpu.VMEM((rows, width), BF))
    else:
        outs += [(w1.shape, BF), (w2.shape, BF)]
    if is_first:
        outs.append(((1, width), F32))
    here = lax.slice_in_dim(b1, plane * hidden, (plane + 1) * hidden)
    return call(
        functools.partial(channel_kernel, following, is_first), sc, deps,
        [*rows_in, w1, here[None], w2, *carried, *ending], outs, "channel", 17 if is_last else 13, scratch,
        None if is_first else {5: 3, 6: 4},
        13 * GFLOP,
    )


def output_kernel(first, n_in, image, pad_s, n_deps, sc, *refs):
    acts, w2s, (x1_far, b2) = refs[n_deps : n_deps + 4], refs[n_deps + 4 : n_deps + 8], refs[n_deps + 8 : n_deps + 10]
    send, tick, *rest = refs[n_deps + n_in :]
    x1, hold, sems = rest[-3:]
    size = x1.shape[0]
    copies = start_all([(x1_far.at[first : first + size], x1)], sems)
    here = slice(first, first + size)
    parts = [dot(a[here, :], w[...], NN) for a, w in zip(acts, w2s)]
    total = (parts[0] + parts[1]) + (parts[2] + parts[3])
    wait_all(copies)
    hold[...] = x1[...].astype(F32) + total + b2[...][None]
    mine = sc[0] == 0
    tick[...] = jnp.zeros_like(tick)
    if image is None:
        keep = rest[0]
        count, half = keep.shape[:2]
        for i in range(count):
            low = hold[i * pad_s : i * pad_s + half, :]
            high = hold[i * pad_s + half : i * pad_s + 2 * half, :]
            keep[i] = jnp.where(mine, low, high).astype(BF)
            send[i, 0:half, :] = jnp.where(mine, high, low).astype(BF)
    else:
        full, keep = rest[0], rest[1]
        half = keep.shape[0]
        low, high = hold[0:half, :], hold[half : 2 * half, :]
        keep[...] = jnp.where(mine, low, high).astype(BF)
        copies = start_all([(keep, full.at[sc[0] * send.shape[0] + image])], sems)
        send[image, send.shape[1] - half :, :] = jnp.where(mine, high, low).astype(BF)
        wait_all(copies)


def output(sc, deps, acts, w2s, x1, b2, image, halves, send, full):
    count, half_s, half_l = halves
    width = w2s[0].shape[1]
    pad_s = round_up(2 * half_s, 16)
    first = 0 if image is None else count * pad_s + 2 * half_l * image
    size = count * pad_s if image is None else 2 * half_l
    inputs = [*acts, *w2s, Far(x1), b2]
    outs = [((count, round_up(half_s, 16) + half_l, width), BF), ((8, 128), F32)]
    aliases = {}
    if send is not None:
        aliases[len(inputs)] = 0
        inputs.append(send)
    scratch = []
    if image is None:
        outs.append(((count, half_s, width), BF))
    else:
        outs.append(((2 * count, half_l, width), BF, None))
        if full is not None:
            aliases[len(inputs)] = 2
            inputs.append(Far(full))
        scratch.append(pltpu.VMEM((half_l, width), BF))
    scratch += [pltpu.VMEM((size, width), BF), pltpu.VMEM((size, width), F32), pltpu.SemaphoreType.DMA((1,))]
    return call(
        functools.partial(output_kernel, first, len(inputs), image, pad_s), sc, deps, inputs, outs,
        "output", 14, scratch, aliases,
    )


def back_kernel(n_deps, sc, *refs):
    (
        dx1, xs_far, xs_in_far, xl_far, xl_in_far, gain_own, gain_in, shift_own, shift_in, as_far, ds_far, al_far, dl_far,
        es, pjs, el, pjl, g2, gy, b1a, b1b, b1c, b1d,
        gis_keep, gi_send, gil, w_keep, w_send,
        vec, x_s, x_l, tk, es_p, pjs_p, gps, ges, gpl, gel, gi_s, gi_l, gil_keep,
        xs_f, xs_in_f, xs, xs_in, xl, xl_in, as_, ds_, al, dl, sems,
    ) = refs[n_deps:]
    count = as_.shape[0]
    loads = []
    small_loads = start_all([(xs_far, xs), (xs_in_far, xs_in)], sems)
    for i in range(count):
        pairs = [(xl_far.at[sc[0] * count + i], xl.at[i]), (xl_in_far.at[i], xl_in.at[i])]
        pairs += [(far.at[i], ref.at[i]) for far, ref in ((ds_far, ds_), (as_far, as_), (dl_far, dl), (al_far, al))]
        loads.append(start_all(pairs, sems, 2 + 6 * i))
    load_token_params(sc, (gain_own, gain_in, shift_own, shift_in), tk)
    fill(es_p, es)
    fill(pjs_p, pjs)
    vec[...] = jnp.zeros_like(vec)
    gain, shift = tk[0:1, :], tk[1:2, :]

    def group(x_ref, index, at, a, d, e, pj, gp, ge, be_at, bp_row, gi, keep, send_at):
        rows, width = x_ref.shape
        hidden = a.shape[1]
        dx = dx1[at : at + rows, :]
        hat, scale = norm(x_ref[...])
        normed = (hat * gain + shift).astype(BF)
        before = (dot(pj[...], dx, TN) * d[index]).astype(BF)
        grad = dot(e[...], before, NN)
        project_grad = dot(dx, a[index], NT)
        expand_grad = dot(normed, before, NT)
        if index == 0:
            gp[0:rows, :] = project_grad
            ge[0:rows, :] = expand_grad
        else:
            gp[0:rows, :] += project_grad
            ge[0:rows, :] += expand_grad
        ones = jnp.ones((8, width), BF)
        vec[bp_row : bp_row + 1, 0:rows] += dot(ones, dx, NT)[0:1, :]
        vec[9:10, be_at : be_at + hidden] += dot(ones, before, NT)[0:1, :]
        vec[0:1, :] += jnp.sum(grad * hat, 0, keepdims=True)
        vec[1:2, :] += jnp.sum(grad, 0, keepdims=True)
        scaled = grad * gain
        mean = jnp.sum(scaled, -1, keepdims=True) * (1.0 / width)
        along = jnp.sum(scaled * hat, -1, keepdims=True) * (1.0 / width)
        gi[...] = dx.astype(F32) + scale * (scaled - mean - hat * along)
        part = width // 2
        size = keep.shape[1]
        keep[index] = gi[0:size, pl.ds(pl.multiple_of(sc[0] * part, 128), part)].astype(BF)
        theirs = gi[0:size, pl.ds(pl.multiple_of((1 - sc[0]) * part, 128), part)]
        gi_send[index, send_at : send_at + size, :] = theirs.astype(BF)

    hidden = as_.shape[1]
    pad_s, pad_l = x_s.shape[1], x_l.shape[1]
    wait_all(small_loads)
    xs_f[...] = xs[...].astype(F32)
    xs_in_f[...] = xs_in[...].astype(F32)
    for i in range(count):
        wait_all(loads[i])
        image = sc[0] * count + i
        load_image(sc, xs_f.at[:, image], xs_in_f.at[:, image], x_s.at[i])
        load_image(sc, xl.at[i], xl_in.at[i], x_l.at[i])
        group(x_s.at[i], i, i * pad_s, as_, ds_, es_p, pjs_p, gps, ges, 0, 10, gi_s, gis_keep, 0)
        group(
            x_l.at[i], i, count * pad_s + i * pad_l, al, dl, el, pjl, gpl, gel, hidden, 11,
            gi_l, gil_keep, pad_s,
        )
    copies = start_all([(gil_keep, gil.at[pl.ds(sc[0] * count, count)])], sems)
    vec[2:4, :] = g2[...]
    vec[4:5, :] = gy[...]
    for i, ref in enumerate((b1a, b1b, b1c, b1d)):
        vec[5 + i : 6 + i, :] = ref[...]
    size = w_keep.shape[2]
    half_s, half_l = gps.shape[0] // 2, gpl.shape[0] // 2
    for ref in (gps, ges):
        ref[pad_s:, :] = jnp.zeros((ref.shape[0] - pad_s, hidden), F32)
    for side, ref in ((sc[0], w_keep), (1 - sc[0], w_send)):
        for t, (small, large) in enumerate(((gps, gpl), (ges, gel))):
            at = pl.multiple_of(side * half_s, 8)
            ref[0, t] = small[pl.ds(at, size), :].astype(BF)
            for c in range(1, 4):
                have = min(size, half_l - (c - 1) * size)
                at = pl.multiple_of(side * half_l + (c - 1) * size, 8)
                ref[c, t, 0:have, :] = large[pl.ds(at, have), :].astype(BF)
                if have < size:
                    ref[c, t, have:, :] = jnp.zeros((size - have, hidden), BF)
        at = pl.multiple_of(side * hidden, 128)
        ref[3, 0, have : have + VEC, :] = vec[:, pl.ds(at, hidden)].astype(BF)
    wait_all(copies)


def piece_rows(pad_s, pad_l):
    return max(round_up(pad_s // 2, 16), round_up(-(-(pad_l // 2 + VEC) // 3), 16))


def back(sc, deps, dx1, xs, xs_in, xl, xl_in, tok, saved, weights, vectors):
    small, images, part = xs.shape
    count, large, width = images // 2, xl.shape[1], 2 * part
    pad_s, pad_l = round_up(small, 16), round_up(large, 16)
    hidden = saved[0].shape[1]
    size = piece_rows(pad_s, pad_l)
    return call(
        back_kernel, sc, deps,
        [dx1, Far(xs), Far(xs_in), Far(xl), Far(xl_in), *tok, *[Far(a) for a in saved], *weights, *vectors],
        [
            ((count, small, part), BF),
            ((count, pad_s + large, part), BF),
            ((images, large, part), BF, None),
            ((4, 2, size, hidden), BF),
            ((4, 2, size, hidden), BF),
        ],
        "back", 30, cost=12 * GFLOP, scratch=
        [
            pltpu.VMEM((VEC, width), F32),
            pltpu.VMEM((count, pad_s, width), F32),
            pltpu.VMEM((count, pad_l, width), F32),
            pltpu.VMEM((2, width), F32),
            pltpu.VMEM((pad_s, hidden), BF),
            pltpu.VMEM((pad_s, hidden), BF),
            pltpu.VMEM((2 * size, hidden), F32),
            pltpu.VMEM((2 * size, hidden), F32),
            pltpu.VMEM((pad_l, hidden), F32),
            pltpu.VMEM((pad_l, hidden), F32),
            pltpu.VMEM((pad_s, width), F32),
            pltpu.VMEM((pad_l, width), F32),
            pltpu.VMEM((count, large, part), BF),
            *[pltpu.VMEM(xs.shape, F32)] * 2,
            *[pltpu.VMEM(xs.shape, BF)] * 2,
            *[pltpu.VMEM((count, large, part), BF)] * 2,
            *[pltpu.VMEM((count, hidden, width), BF), pltpu.VMEM((count, hidden, width), F32)] * 2,
            pltpu.SemaphoreType.DMA((2 + 6 * count,)),
        ],
    )


def total4(parts):
    a, b, c, d = [p.astype(F32) for p in parts]
    return (a + b) + (c + d)


def pair_kernel(n_deps, sc, *refs):
    keep, recv = refs[n_deps : n_deps + 2]
    for k, ref in enumerate(refs[-4:]):
        ref[...] = (keep[sc[1] ^ k].astype(F32) + recv[sc[1] ^ k].astype(F32)).astype(BF)


def pair_sum(sc, deps, keep, recv, passenger=None):
    outs = [(keep.shape[1:], BF)] * 4
    if passenger is None:
        return call(pair_kernel, sc, deps, [keep, recv], outs, "pair_sum", 4)
    passed, *sums = call(
        pair_kernel, sc, deps, [keep, recv, passenger], [(passenger.shape, BF)] + outs, "pair_sum", 4,
        aliases={2: 0},
    )
    return sums, passed


def sides_kernel(n_deps, sc, *refs):
    parts, outs = refs[n_deps : n_deps + 4], refs[-4:]
    rows = parts[0].shape[1]
    half = parts[0].shape[2] // 2
    x, y = sc[1] % 2, sc[1] // 2
    for side in range(2):
        cols = slice(side * half, (side + 1) * half)
        for stays, ref in ((True, outs[2 * side]), (False, outs[2 * side + 1])):
            for k in range(2):
                if side == 0:
                    chip = 2 * (y ^ k) + (x if stays else 1 - x)
                else:
                    chip = 2 * (y if stays else 1 - y) + (x ^ k)
                for i in range(2):
                    keep, recv = parts[2 * i : 2 * i + 2]
                    total = keep[chip, :, cols].astype(F32) + recv[chip, :, cols].astype(F32)
                    ref[k, i * rows : (i + 1) * rows, :] = total.astype(BF)


def sides_sum(sc, deps, parts):
    chips, rows, width = parts[0].shape
    return call(sides_kernel, sc, deps, parts, [((2, 2 * rows, width // 2), BF)] * 4, "sides_sum", 6)


def second_kernel(n_deps, sc, *refs):
    refs = refs[n_deps:]
    for side in range(2):
        keep, recv = refs[2 * side : 2 * side + 2]
        for k in range(2):
            refs[4 + 2 * side + k][...] = (keep[k].astype(F32) + recv[k].astype(F32)).astype(BF)


def second_sum(sc, deps, parts):
    return call(second_kernel, sc, deps, parts, [(parts[0].shape[1:], BF)] * 4, "second_sum", 4)


def quad_kernel(n_parts, n_deps, sc, *refs):
    parts, (keep, send, hold, rest) = refs[n_deps : n_deps + n_parts], refs[-4:]
    rows = keep.shape[0] // 2
    quarter = rows // PLANES
    for i in range(2):
        if len(parts) == 4:
            here = slice(2 * rows * i, 2 * rows * (i + 1))
            sums = [parts[j][here, :].astype(F32) + parts[j + 1][here, :].astype(F32) for j in (0, 2)]
            total = jnp.concatenate(sums, 1)
        else:
            total = total4([r[...] for r in parts[4 * i : 4 * i + 4]])
        hold[i] = total[0:rows].reshape(hold.shape[1:])
        rest[i] = total[rows:]
    high, low = sc[2] // 2, sc[2] % 2
    for side, ref in ((high, keep), (1 - high, send)):
        for k in range(2):
            pair = [hold[i, 2 * side + (low ^ k)] for i in range(2)]
            ref[2 * k * quarter : 2 * (k + 1) * quarter, :] = jnp.concatenate(pair, 0).astype(BF)
        ref[rows:, :] = rest[side].astype(BF)


def quad_sum(sc, deps, parts, passengers=()):
    rows, width = parts[0].shape
    if len(parts) == 4:
        rows, width = rows // 2, 2 * width
    quarter = rows // 2 // PLANES
    passed = [(a.shape, a.dtype) for a in passengers]
    *passed, keep, send = call(
        functools.partial(quad_kernel, len(parts)), sc, deps, [*parts, *passengers],
        passed + [((rows, width), BF)] * 2, "quad_sum", 6,
        [pltpu.VMEM((2, PLANES, quarter, width), F32), pltpu.VMEM((2, rows // 2, width), F32)],
        {len(parts) + i: i for i in range(len(passed))},
    )
    return keep, send, passed


def planes_kernel(n_deps, sc, *refs):
    a, b = refs[n_deps : n_deps + 2]
    keep, send = refs[-2:]
    rows = a.shape[0]
    cut = rows // 4
    total = a[...].astype(F32) + b[...].astype(F32)
    keep[0:cut, :] = total[0:cut].astype(BF)
    send[0:cut, :] = total[cut : 2 * cut].astype(BF)
    rest = total[2 * cut :].astype(BF)
    keep[cut:, :] = rest
    send[cut:, :] = rest


def planes_sum(sc, deps, keep, recv, passengers=()):
    rows, width = keep.shape
    passed = [(a.shape, a.dtype) for a in passengers]
    *passed, keep, send = call(
        planes_kernel, sc, deps, [keep, recv, *passengers], passed + [((3 * rows // 4, width), BF)] * 2,
        "planes_sum", 4, aliases={2 + i: i for i in range(len(passed))},
    )
    return keep, send, passed


def last_kernel(groups, n_deps, sc, *refs):
    refs = refs[n_deps:]
    expand_out, project_out, expand, project, sems = refs[-5:]
    width = expand.shape[1] // PLANES
    quarter = expand.shape[0]
    for g, planes in enumerate(groups):
        total = refs[2 * g][...].astype(F32) + refs[2 * g + 1][...].astype(F32)
        for i, plane in enumerate(planes):
            expand[:, plane * width : (plane + 1) * width] = total[i * quarter : (i + 1) * quarter]

        @pl.when((sc[2] == planes[0]) | (sc[2] == planes[1]))
        def _():
            project[...] = total[2 * quarter :]

    wait_all(start_all([(expand, expand_out), (project, project_out)], sems))


def last_sum(sc, groups, pieces):
    flat = [a for group in groups for a in pieces[group]]
    rows, width = flat[0].shape
    shapes = [(rows // 6, PLANES * width), (2 * rows // 3, width)]
    return call(
        functools.partial(last_kernel, groups), sc, [], flat, [(s, F32, None) for s in shapes], "last_sum", 4,
        [pltpu.VMEM(s, F32) for s in shapes] + [pltpu.SemaphoreType.DMA((2,))],
    )


def piece_at(rows):
    size = round_up(-(-rows // 2), 16)
    return rows - size, size


def split_kernel(n_deps, sc, *refs):
    parts, outs, hold = refs[n_deps : n_deps + 4], refs[-5:-1], refs[-1]
    hold[...] = total4([r[...] for r in parts])
    second, size = piece_at(hold.shape[1])
    for k, ref in enumerate(outs):
        piece = sc[2] ^ k
        at = pl.multiple_of((piece % 2) * second, 16)
        ref[...] = hold[piece // 2, pl.ds(at, size), :].astype(BF)


def token_split(sc, deps, parts, passenger):
    size = piece_at(parts[0].shape[1])[1]
    return call(
        split_kernel, sc, deps, [*parts, passenger],
        [(passenger.shape, passenger.dtype)] + [((size, parts[0].shape[2]), BF)] * 4, "token_split", 4,
        [pltpu.VMEM(parts[0].shape, F32)], {4: 0},
    )


def token_sum_kernel(n_deps, sc, *refs):
    refs[-1][...] = total4([r[...] for r in refs[n_deps : n_deps + 4]]).astype(BF)


def token_sum(sc, deps, parts, passenger):
    outs = [(passenger.shape, passenger.dtype), (parts[0].shape, BF)]
    return call(token_sum_kernel, sc, deps, [*parts, passenger], outs, "token_sum", 4, aliases={4: 0})


def join_kernel(n_deps, sc, *refs):
    parts, w, hold = refs[n_deps : n_deps + 4], refs[-2], refs[-1]
    for k, ref in enumerate(parts):
        hold[sc[2] ^ k] = ref[...]
    second, size = piece_at(w.shape[1])
    for piece in range(PLANES):
        at = (piece % 2) * second
        w[piece // 2, at : at + size, :] = hold[piece]


def token_join(sc, deps, parts, rows):
    size, hidden = parts[0].shape
    return call(
        join_kernel, sc, deps, parts, [((2, rows, hidden), BF)], "token_join", 4,
        [pltpu.VMEM((PLANES, size, hidden), BF)],
    )[0]


def unpack_kernel(n_deps, sc, *refs):
    refs = refs[n_deps:]
    mine, theirs = refs[0:4], refs[4:8]
    ges, gps, gel, gpl = refs[8:12]
    vectors = refs[12:22]
    hold, vec = refs[22:]
    for k in range(4):
        hold[sc[0], sc[1] ^ k] = mine[k][...]
        hold[1 - sc[0], sc[1] ^ k] = theirs[k][...]
    size, hidden = mine[0].shape[1:]
    small, large = ges.shape[0], gel.shape[0]
    for side in range(2):
        low = side * size
        have = min(size, small - low)
        for t, ref in enumerate((gps, ges)):
            ref[low : low + have, :] = hold[side, 0, t].astype(F32)[0:have, :]
        for c in range(1, 4):
            low = side * (large // 2) + (c - 1) * size
            have = min(size, large // 2 - (c - 1) * size)
            for t, ref in enumerate((gpl, gel)):
                ref[low : low + have, :] = hold[side, c, t].astype(F32)[0:have, :]
        vec[:, side * hidden : (side + 1) * hidden] = hold[side, 3, 0].astype(F32)[have : have + VEC, :]
    width = vec.shape[1]
    picks = [(0, 0), (1, 0), (9, 0), (10, 0), (9, hidden), (11, 0), (2, 0), (3, 0), None, (4, 0)]
    for ref, pick in zip(vectors, picks):
        if pick is None:
            for i in range(ref.shape[0] // width):
                ref[i * width : (i + 1) * width] = vec[5 + i, :]
        else:
            row, at = pick
            ref[...] = vec[row, at : at + ref.shape[0]]


def unpack(sc, deps, mine, theirs, small, large, width, channel_hidden):
    hidden = mine[0].shape[2]
    outs = [(small, hidden)] * 2 + [(large, hidden)] * 2
    outs += [(n,) for n in (width, width, hidden, small, hidden, large, width, width, channel_hidden, width)]
    return pl.pallas_call(
        functools.partial(unpack_kernel, len(deps)),
        in_specs=[pl.BlockSpec(memory_space=pltpu.SMEM)]
        + [pl.BlockSpec(memory_space=pltpu.VMEM)] * (len(deps) + 8),
        out_shape=[jax.ShapeDtypeStruct(s, F32) for s in outs],
        scratch_shapes=[pltpu.VMEM((2, 4) + mine[0].shape, BF), pltpu.VMEM((VEC, width), F32)],
        compiler_params=pltpu.CompilerParams(vmem_limit_bytes=12 * MB),
        cost_estimate=pl.CostEstimate(flops=0, bytes_accessed=0, transcendentals=0),
        name="unpack",
    )(sc, *deps, *mine, *theirs)


def place_kernel(n_deps, sc, *refs):
    refs = refs[n_deps:]
    keeps, received = refs[0:2], refs[2:4]
    tick, far_small, far_large, near, sems = refs[6], refs[7:9], refs[9:11], refs[11:13], refs[13]
    count = keeps[0].shape[0]
    pairs = []
    for theirs, far in zip(received, far_large):
        at = theirs.shape[1] - far.shape[1]
        for i in range(count):
            pairs.append((theirs.at[i, at:, :], far.at[(1 - sc[0]) * count + i]))
    copies = start_all(pairs, sems)
    for mine, theirs, ref in zip(keeps, received, near):
        size = mine.shape[1]
        for j in range(2 * count):
            k = j % count
            other = theirs[k, 0:size, :].astype(F32)
            ref[:, j, :] = jnp.where(sc[0] == j // count, mine[k].astype(F32), other).astype(BF)
    copies += start_all(zip(near, far_small), sems, len(copies))
    tick[...] = jnp.zeros_like(tick)
    wait_all(copies)


def place(sc, deps, keeps, received, filled):
    shapes = [(a.shape[1], 2 * a.shape[0], a.shape[2]) for a in keeps]
    count = keeps[0].shape[0]
    return call(
        place_kernel, sc, deps, keeps + received + [Far(a) for a in filled],
        [((8, 128), F32)] + [(shape, BF, None) for shape in shapes] + [(a.shape, BF, None) for a in filled],
        "place", 6,
        [pltpu.VMEM(shape, BF) for shape in shapes] + [pltpu.SemaphoreType.DMA((2 * count + 2,))],
        {4: 3, 5: 4},
    )


def swap(values):
    return lax.ppermute(values, "mp", [(0, 1), (1, 0)])


def across(values, mask, pairs):
    return lax.ppermute(values, "dp", [(i, i ^ mask) for i in pairs])


def per_device(
    chips,
    small_images,
    large_images,
    token_gain,
    token_shift,
    small_expand,
    small_expand_bias,
    small_project,
    small_project_bias,
    large_expand,
    large_expand_bias,
    large_project,
    large_project_bias,
    channel_gain,
    channel_shift,
    channel_expand,
    channel_expand_bias,
    channel_project,
    channel_project_bias,
    small_cotangent,
    large_cotangent,
):
    core = lax.axis_index("mp")
    chip = lax.axis_index("dp")
    sc = jnp.stack([core, chip % 4, (chip // 4) % PLANES]).astype(jnp.int32)
    small_images, small_cotangent = small_images.transpose(1, 0, 2), small_cotangent.transpose(1, 0, 2)
    small, images, part = small_images.shape
    large = large_images.shape[1]
    count = images // 2
    width = channel_expand.shape[0]
    everyone = range(chips)
    tuned = chips == 4 * PLANES

    xl_send, yl_send = pick(sc, large_images, large_cotangent)
    xs_in, xl_in = swap(small_images), swap(xl_send)
    tok = [token_gain, swap(token_gain), token_shift, swap(token_shift)]
    ys_in, yl_in = swap(small_cotangent), swap(yl_send)
    token_s = [small_expand, small_expand_bias, small_project.T, small_project_bias]
    token_l = [large_expand, large_expand_bias, large_project.T, large_project_bias]
    xs, xl, y, *weights = prepare(
        sc, small_images, large_images, small_cotangent, large_cotangent, token_s, token_l
    )
    n2, w1, w2, x1, as_, ds_, al, dl = front(
        sc, xs, xs_in, xl, xl_in, tok, weights, channel_gain, channel_shift, channel_expand, channel_project
    )
    y = cotangent_rows(sc, [n2], small_cotangent, ys_in, yl_in, y)
    carried = []
    sends, keeps, b1_grads, halved, pieces = {}, {}, {}, {}, {}
    groups = (ORDER[:2], ORDER[2:])

    def halve(plane, deps, passenger=None):
        sums = pair_sum(sc, deps, keeps[plane], swap(sends[plane]), None if passenger is None else sends[passenger])
        if passenger is not None:
            sums, sends[passenger] = sums
        own, *others = sums
        halved[plane] = [own] + [across(o, k + 1, everyone) for k, o in enumerate(others)]

    def quarter(group, deps, passenger=None):
        parts = halved[group] if group in halved else halved[group[0]] + halved[group[1]]
        if passenger is None:
            keep, send, _ = quad_sum(sc, deps, parts)
        else:
            keep, send, (sends[passenger],) = quad_sum(sc, deps, parts, [sends[passenger]])
        pieces[group] = [keep, across(send, 8, everyone)]

        def finish(deps, passengers=()):
            keep, send, passed = planes_sum(sc, deps, *pieces[group], passengers)
            pieces[group] = [keep, send]
            return passed

        return finish

    n_last = PLANES - 1
    acts, w2s = [], []
    halves = (count, small // 2, large // 2)

    def rows_out(deps, image, send, full):
        return output(sc, deps, acts, w2s, x1, channel_project_bias, image, halves, send, full)

    for i, plane in enumerate(ORDER):
        is_last = i == n_last
        following = None if is_last else ORDER[i + 1]
        if is_last:
            ending = [Far(x1), channel_gain]
        else:
            ending = [Far(channel_expand), Far(channel_project)]
        deps = []
        if tuned and i >= 2:
            arrived = halved[ORDER[i - 3]][1:] if i >= 3 else []
            halve(ORDER[i - 2], [b1_grads[ORDER[i - 1]]] + arrived, ORDER[2] if is_last else None)
            deps = halved[ORDER[i - 2]][:1]
        w2s.append(w2)
        sends[plane], keeps[plane], b1_grads[plane], dn_low, dn_high, active, *carried = channel(
            sc, deps, plane, following, [n2, y], w1, channel_expand_bias, w2, carried, ending
        )
        acts.append(active)
        if i == 0:
            *carried, gy = carried
        if not is_last:
            w1, w2 = carried
            carried = [dn_low, dn_high]
    dx1, g2 = carried
    deps = []
    if tuned:
        finish = quarter(groups[0], [b1_grads[ORDER[3]]], ORDER[3])
        keep_a, send_a, keep_b, send_b = sides_sum(
            sc, [pieces[groups[0]][0]],
            [a for plane in groups[1] for a in (keeps[plane], swap(sends[plane]))],
        )
        recv_a, recv_b = across(send_a, 1, everyone), across(send_b, 2, everyone)
        deps = [keep_a]
    gis_keep, gi_send, gil, w_keep, w_send = back(
        sc, deps, dx1, small_images, xs_in, large_images, xl_in, tok,
        [as_, ds_, al, dl],
        [small_expand, small_project.T, large_expand, large_project.T],
        [g2, gy] + [b1_grads[plane] for plane in range(PLANES)],
    )

    if tuned:
        w_send, gi_send = finish([w_keep, recv_a, recv_b], [w_send, gi_send])
        gi_in = swap(gi_send)
        keep_a, send_a, keep_b, send_b = second_sum(
            sc, [pieces[groups[0]][0]], [keep_a, recv_a, keep_b, recv_b]
        )
        halved[groups[1]] = [keep_a, across(send_a, 2, everyone), keep_b, across(send_b, 1, everyone)]
        own, *others = pair_sum(sc, [keep_a, gi_in], w_keep, swap(w_send))
        parts = [own] + [across(o, k + 1, everyone) for k, o in enumerate(others)]
        out_send, tick, outl_full = rows_out([own], 0, None, None)
        finish = quarter(groups[1], [tick])
        send, own, *others = token_split(sc, [pieces[groups[1]][0]], parts, pieces[groups[0]][1])
        pieces[groups[0]][1] = across(send, 4, everyone)
        parts = [own] + [across(o, 4 * (k + 1), everyone) for k, o in enumerate(others)]
        out_send, tick, outs_keep = rows_out([own], None, out_send, None)
        out_send, tick, outl_full = rows_out([tick], 1, out_send, outl_full)
        out_send, w = token_sum(sc, [tick, pieces[groups[0]][1], pieces[groups[1]][1]], parts, out_send)
        out_in = swap(out_send)
        parts = [w] + [across(w, 4 * k, everyone) for k in (1, 2, 3)]
        finish([w])
        pieces[groups[1]][1] = across(pieces[groups[1]][1], 4, everyone)
        tick, small_output, small_input_grad, large_output, large_input_grad = place(
            sc, [pieces[groups[1]][0]], [outs_keep, gis_keep], [out_in, gi_in], [outl_full, gil]
        )
        w = token_join(sc, [tick], parts, w_keep.shape[2])
        mine = [w] + [across(w, k, everyone) for k in (1, 2, 3)]
        extra = []
        expand_part, project_part = last_sum(sc, groups, pieces)
    else:
        out_send, _, outl_full = rows_out([], 0, None, None)
        out_send, _, outl_full = rows_out([], 1, out_send, outl_full)
        out_send, _, outs_keep = rows_out([], None, out_send, None)
        _, small_output, small_input_grad, large_output, large_input_grad = place(
            sc, [], [outs_keep, gis_keep], [swap(out_send), swap(gi_send)], [outl_full, gil]
        )
        extra = []

        def both(keep, send):
            return jnp.where(core == 0, jnp.stack([keep, send]), jnp.stack([send, keep])).astype(F32)

        expand_full, project_full = [], []
        for plane in range(PLANES):
            parts = both(keeps[plane], sends[plane])
            cut = width // 8
            e = parts[:, :, :cut].reshape(2, 4, PLANES, width // 32, -1)
            expand_full.append(e.transpose(2, 1, 0, 3, 4).reshape(width, -1))
            project_full.append(parts[:, :, cut:].transpose(1, 0, 2, 3).reshape(-1, width))
        expand_part = lax.psum_scatter(
            jnp.concatenate(expand_full, 1), ("dp", "mp"), scatter_dimension=0, tiled=True
        )
        project_part = lax.psum_scatter(
            jnp.concatenate(project_full, 0), ("dp", "mp"), scatter_dimension=0, tiled=True
        )
        token = lax.psum(both(w_keep, w_send), ("dp", "mp"))
        token = lax.dynamic_index_in_dim(token, core, 0, False).astype(BF)
        mine = [lax.dynamic_index_in_dim(token, sc[1] ^ k, 0, False) for k in range(4)]
    unpacked = unpack(
        sc, extra, mine, [swap(w) for w in mine], small, large, width, channel_expand.shape[1]
    )
    (ges, gps_t, gel, gpl_t, gtg, gts, gbes, gbps, gbel, gbpl, gcg, gcs, gb1, gb2) = unpacked
    small_output, small_input_grad = small_output.transpose(1, 0, 2), small_input_grad.transpose(1, 0, 2)
    return (
        small_output, large_output, small_input_grad, large_input_grad,
        gtg, gts, ges, gbes, gps_t.T, gbps, gel, gbel, gpl_t.T, gbpl,
        gcg, gcs, expand_part, gb1, project_part, gb2,
    )


def solution(mesh):
    replicated = P()
    by_channel = P("dp", None, "mp")
    by_patch = P("dp", "mp", None)
    by_row = P(("dp", "mp"), None)
    return jax.shard_map(
        functools.partial(per_device, mesh.shape["dp"]),
        mesh=mesh,
        in_specs=(by_channel, by_channel, P("mp"), P("mp")) + (replicated,) * 14 + (by_patch, by_patch),
        out_specs=(by_patch, by_patch, by_channel, by_channel)
        + (replicated,) * 12
        + (by_row, replicated, by_row, replicated),
        check_vma=False,
    )
```
